128 devices in a mesh: panel: 2 (over x_hi), colat: 4 (over z), lon: 16 (over y, x_lo, core).
Axes of the slice: x: 4 (x_hi: 2, x_lo: 2; x = x_hi * 2 + x_lo), y: 4, z: 4, core: 2. Of those that a mesh axis runs over, the one named last changes fastest.
Arguments:
- state: float32 [4, 2, 4, 1536, 512], P(None, 'panel', None, 'lon', 'colat'), may hold values from -6 to 6
- partners: int32 [2, 4, 16, 2], P('panel', 'colat', 'lon'), may hold values from 0 to 63, as said below
- send_counts: int32 [2, 4, 16, 2], P('panel', 'colat', 'lon'), may hold values from 0 to 128
- source_cells: int32 [2, 4, 16, 256], P('panel', 'colat', 'lon'), may hold values from 0 to 12158, as said below
- weights: float32 [4, 2, 4, 16, 256], P(None, 'panel', 'colat', 'lon'), may hold values from 0 to 1, as said below
- turn_angles: float32 [2, 4, 16, 256], P('panel', 'colat', 'lon'), may hold values from -3.140625 to 3.140625
- ghost_slots: int32 [2, 4, 16, 896], P('panel', 'colat', 'lon'), may hold values from -1 to 8191, as said below
Outputs:
- new_state: float32 [4, 2, 4, 1536, 512], P(None, 'panel', None, 'lon', 'colat')
The draws below stay inside these ranges and needn't reach their ends.
Inputs may be any that keep to these rules, and one draw needn't show every extreme that they name: `partners`: A block's slots with a positive count name distinct blocks; every live row is read by exactly one ghost position of the block that its slot names. `source_cells`: the interpolation square lies inside the block: lat offset at most 126, lon offset at most 94. Positive; the four weights of a row sum to one. `ghost_slots`: -1 exactly on the sides of a block that are not panel borders; on border sides each ghost position points to a live row of a slot that names this block; the positions of one side come in consecutive runs of rows.
All inputs are finite; a program needn't handle non-finite values.
Results may differ from the reference program's by a relative error of at most 0.00002.
Values sent between devices are 32-bit elements; how exact they have to be, the bound alone decides.
No kernel may reach another device: no remote copies, remote signals or barrier semaphores. Data moves between devices by JAX's collectives and lax.ppermute only.
A program may use at most 128 MiB of HBM per device.

```python
import math
import jax
import jax.numpy as jnp
import numpy as np
from jax import lax

CT = 128
LEV = 4
STEPS = 2
CP = 96
CAP = 128
PARTNERS = 2
SLOTS = 256
GHOSTS = 896
NTH = 512
NPH = 1536
N_COLAT = 4
N_LON = 16


def edge_tables():
    edge_list = []
    for lat_block in range(N_COLAT):
        for lon_block in range(N_LON):
            owner = lat_block * N_LON + lon_block
            if lat_block == 0:
                edge_list.append((owner, 0, 2 * CP, 3))
            if lat_block == N_COLAT - 1:
                edge_list.append((owner, 2 * CP, 2 * CP, 3))
            if lon_block == 0:
                edge_list.append((owner, 4 * CP, 2 * CT, 4))
            if lon_block == N_LON - 1:
                edge_list.append((owner, 4 * CP + 2 * CT, 2 * CT, 4))
    base_list = []
    run_owner = []
    run_side = []
    run_local = []
    for side_number in range(len(edge_list)):
        record = edge_list[side_number]
        base_list.append(len(run_owner))
        for local_run in range(record[3]):
            run_owner.append(record[0])
            run_side.append(side_number)
            run_local.append(local_run)
    next_table = [[(local_run + 1) % record[3] if local_run < record[3] else 0 for local_run in range(4)] for record in edge_list]
    return (edge_list, base_list, run_owner, run_side, run_local, next_table)


def panel_plan(key):
    edge_list, base_list, run_owner, run_side, run_local, next_table = edge_tables()
    peers = N_COLAT * N_LON
    half = CT // 2
    side_total = len(edge_list)
    run_total = len(run_owner)
    side_runs = jnp.asarray(np.array([record[3] for record in edge_list], dtype=np.int32))
    key_order, key_cuts, key_pick, key_spare = jax.random.split(key, 4)
    order = jax.random.permutation(key_order, peers).astype(jnp.int32)
    pick = jax.random.randint(key_pick, (side_total,), 0, 12, dtype=jnp.int32) % side_runs
    after = (pick + 1) % side_runs
    columns = jnp.arange(4, dtype=jnp.int32)[None, :]
    cuts = jax.random.randint(key_cuts, (side_total, 4), 0, half + 1, dtype=jnp.int32)
    cuts = jnp.where(columns == pick[:, None], half, jnp.where(columns == after[:, None], 0, cuts))
    following = jnp.take_along_axis(cuts, jnp.asarray(np.array(next_table, dtype=np.int32)), axis=1)
    lengths = jnp.where(columns < side_runs[:, None], half + cuts - following, 0)
    ends = jnp.cumsum(lengths, axis=1)
    starts = ends - lengths
    first_full = pick[0] % peers
    holder = order[first_full]
    order = jnp.where(order == peers - 1, holder, jnp.where(jnp.arange(peers, dtype=jnp.int32) == first_full, peers - 1, order))
    position = jnp.argsort(order).astype(jnp.int32)
    run_of = jnp.arange(PARTNERS, dtype=jnp.int32)[None, :] * peers + position[:, None]
    valid = run_of < run_total
    clipped = jnp.minimum(run_of, run_total - 1)
    owner_of = jnp.asarray(np.array(run_owner, dtype=np.int32))[clipped]
    side_of = jnp.asarray(np.array(run_side, dtype=np.int32))[clipped]
    local_of = jnp.asarray(np.array(run_local, dtype=np.int32))[clipped]
    spare = jax.random.randint(key_spare, (peers, PARTNERS), 0, peers, dtype=jnp.int32)
    partner = jnp.where(valid, owner_of, spare)
    count = jnp.where(valid, lengths[side_of, local_of], 0)
    ghost = jnp.full((peers, GHOSTS), -1, jnp.int32)
    for side_number in range(side_total):
        owner, offset, length, runs = edge_list[side_number]
        points = jnp.arange(length, dtype=jnp.int32)
        local_run = jnp.sum((ends[side_number, :runs][None, :] <= points[:, None]).astype(jnp.int32), axis=1)
        local_run = jnp.minimum(local_run, runs - 1)
        sender = order[(base_list[side_number] + local_run) % peers]
        value = sender * CAP + points - starts[side_number][local_run]
        ghost = ghost.at[owner, offset:offset + length].set(value)
    return (partner, count, ghost)


def overset_plan(key):
    yin_plan = panel_plan(jax.random.fold_in(key, 51))
    yang_plan = panel_plan(jax.random.fold_in(key, 52))
    partners = jnp.stack([yang_plan[0], yin_plan[0]]).reshape(2, N_COLAT, N_LON, PARTNERS)
    counts = jnp.stack([yang_plan[1], yin_plan[1]]).reshape(2, N_COLAT, N_LON, PARTNERS)
    ghosts = jnp.stack([yin_plan[2], yang_plan[2]]).reshape(2, N_COLAT, N_LON, GHOSTS)
    return (partners, counts, ghosts)


def draw_partners(key, part):
    return overset_plan(key)[0]


def draw_send_counts(key, part):
    return overset_plan(key)[1]


def draw_ghost_slots(key, part):
    return overset_plan(key)[2]


def draw_source_cells(key, part):
    key = jax.random.fold_in(key, 3)
    key_lat, key_lon, key_high, key_low = jax.random.split(key, 4)
    shape = (2, N_COLAT, N_LON, SLOTS)
    lat_cell = jax.random.randint(key_lat, shape, 0, CT - 1, dtype=jnp.int32)
    lon_cell = jax.random.randint(key_lon, shape, 0, CP - 1, dtype=jnp.int32)
    cells = lon_cell * CT + lat_cell
    high_place = jax.random.randint(key_high, (2, N_COLAT, N_LON, 1), 0, SLOTS, dtype=jnp.int32)
    low_place = (high_place + 1 + jax.random.randint(key_low, (2, N_COLAT, N_LON, 1), 0, SLOTS - 1, dtype=jnp.int32)) % SLOTS
    index = jnp.arange(SLOTS, dtype=jnp.int32)
    return jnp.where(index == high_place, (CP - 2) * CT + CT - 2, jnp.where(index == low_place, 0, cells))


def draw_weights(key, part):
    key = jax.random.fold_in(key, 4)
    raw = jax.random.uniform(key, (4, 2, N_COLAT, N_LON, SLOTS), jnp.float32, 0.1, 1.0)
    return raw / jnp.sum(raw, axis=0, keepdims=True)


def steps_of(key, shape, cuts, least, top_value):
    def one(dim, parts):
        draws = jax.random.uniform(jax.random.fold_in(jax.random.fold_in(key, 6), dim), (parts,), jnp.float32, least / len(cuts), top_value / len(cuts))
        return jnp.repeat(jnp.exp(draws), shape[dim] // parts).reshape((-1,) + (1,) * (len(shape) - dim - 1))

    level = one(*cuts[0])
    for cut in cuts[1:]:
        level = level * one(*cut)
    return level


def gaussian(key, extent, spread, bound, pieces=(), held_as=jnp.bfloat16):
    loudness = steps_of(key, extent, pieces, -0.22, 0.18) if pieces else 1.0
    result = jax.random.normal(key, extent, jnp.float32) * spread * loudness
    return jnp.minimum(jnp.maximum(result, -bound), bound).astype(held_as)


def setup_inputs(seed: int = 0) -> dict:
    keys = jax.random.split(jax.random.key(seed), 8)
    return {
        "state": gaussian(keys[0], (4, 2, LEV, NPH, NTH), 1.0, 6.0, ((1, 2), (3, 16), (4, 4)), jnp.float32),
        "partners": draw_partners(jax.random.fold_in(keys[7], 71), 0),
        "send_counts": draw_send_counts(jax.random.fold_in(keys[7], 71), 0),
        "source_cells": draw_source_cells(jax.random.fold_in(keys[7], 71), 0),
        "weights": draw_weights(jax.random.fold_in(keys[7], 71), 0),
        "turn_angles": jnp.clip(jax.random.uniform(keys[5], (2, N_COLAT, N_LON, SLOTS), jnp.float32, -3.140625, 3.140625), -3.140625, 3.140625),
        "ghost_slots": draw_ghost_slots(jax.random.fold_in(keys[7], 71), 0),
    }


R_LOW = 0.7
HALF_ROOT = 0.7071067811865476


def constants(lat_total, lon_total):
    d_theta = 0.5 * math.pi / lat_total
    d_phi = 1.5 * math.pi / lon_total
    spacing = R_LOW * min(d_theta, HALF_ROOT * d_phi)
    time_step = 0.25 * spacing
    kappa = 0.04 * spacing * spacing / time_step
    viscous = 0.06 * spacing * spacing / time_step
    return (d_theta, d_phi, time_step, kappa, viscous, 0.05 / time_step, 0.2 / time_step, 4.0 * spacing)


def spin_parts(theta, phi, is_yang, omega):
    cos_t = jnp.cos(theta)[None, :]
    sin_t = jnp.sin(theta)[None, :]
    cos_p = jnp.cos(phi)[:, None]
    sin_p = jnp.sin(phi)[:, None]
    keep = 1.0 - is_yang
    spin_r = omega * (keep * cos_t + is_yang * sin_t * sin_p)
    spin_t = omega * (is_yang * cos_t * sin_p - keep * sin_t)
    spin_p = omega * (is_yang * cos_p) + 0.0 * cos_t
    return spin_r, spin_t, spin_p


def rates(padded, lower, upper, radius, sin_t, cot_t, spins, consts):
    d_theta, d_phi, time_step, kappa, viscous, omega, buoyancy, radial = consts
    center = padded[..., 2:-2, 2:-2]
    lat_far_up = padded[..., 2:-2, 4:]
    lat_up = padded[..., 2:-2, 3:-1]
    lat_down = padded[..., 2:-2, 1:-3]
    lat_far_down = padded[..., 2:-2, :-4]
    lon_far_up = padded[..., 4:, 2:-2]
    lon_up = padded[..., 3:-1, 2:-2]
    lon_down = padded[..., 1:-3, 2:-2]
    lon_far_down = padded[..., :-4, 2:-2]
    lat_one = (8.0 * (lat_up - lat_down) - (lat_far_up - lat_far_down)) / (12.0 * d_theta)
    lat_two = (16.0 * (lat_up + lat_down) - (lat_far_up + lat_far_down) - 30.0 * center) / (12.0 * d_theta * d_theta)
    lon_one = (8.0 * (lon_up - lon_down) - (lon_far_up - lon_far_down)) / (12.0 * d_phi)
    lon_two = (16.0 * (lon_up + lon_down) - (lon_far_up + lon_far_down) - 30.0 * center) / (12.0 * d_phi * d_phi)
    rad_one = (upper - lower) / (2.0 * radial)
    rad_two = (upper + lower - 2.0 * center) / (radial * radial)
    inverse = 1.0 / radius
    vel_r = center[1]
    vel_t = center[2]
    vel_p = center[3]
    advect = vel_r * rad_one + (vel_t * inverse) * lat_one + (vel_p * inverse / sin_t) * lon_one
    laplace = rad_two + (2.0 * inverse) * rad_one + (lat_two + cot_t * lat_one) * (inverse * inverse) + lon_two * (inverse * inverse / (sin_t * sin_t))
    spin_r, spin_t, spin_p = spins
    heat = kappa * laplace[0] - advect[0]
    rate_r = viscous * laplace[1] - advect[1] + buoyancy * center[0] - 2.0 * (spin_t * vel_p - spin_p * vel_t)
    rate_t = viscous * laplace[2] - advect[2] - 2.0 * (spin_p * vel_r - spin_r * vel_p)
    rate_p = viscous * laplace[3] - advect[3] - 2.0 * (spin_r * vel_t - spin_t * vel_r)
    return jnp.stack([heat, rate_r, rate_t, rate_p])


def turn_and_mask(value, turn, live):
    levels = value.shape[0] // 4
    cosine = jnp.cos(turn)
    sine = jnp.sin(turn)
    lat_part = value[2 * levels:3 * levels]
    lon_part = value[3 * levels:]
    value = jnp.concatenate([value[:2 * levels], cosine * lat_part + sine * lon_part, cosine * lon_part - sine * lat_part], axis=0)
    return jnp.where(live, value, 0.0)


def sender_values(current, source_cells, weights, turn_angles, send_counts):
    lat_index = jnp.arange(N_COLAT, dtype=jnp.int32)[:, None, None]
    lon_index = jnp.arange(N_LON, dtype=jnp.int32)[None, :, None]
    lat_local = source_cells % CT
    lon_local = source_cells // CT
    live = (jnp.arange(SLOTS, dtype=jnp.int32) % CAP) < jnp.repeat(send_counts, CAP, axis=-1)
    collected = []
    for panel in range(2):
        flat = current[:, panel].reshape(4 * LEV, NPH * NTH)
        corner = (lon_index * CP + lon_local[panel]) * NTH + lat_index * CT + lat_local[panel]
        wts = weights[:, panel]
        value = wts[0] * flat[:, corner] + wts[1] * flat[:, corner + 1] + wts[2] * flat[:, corner + NTH] + wts[3] * flat[:, corner + NTH + 1]
        collected.append(turn_and_mask(value, turn_angles[panel], live[panel]))
    return collected


def ghost_values(sent, partners, ghost_slots):
    receiver = jnp.arange(N_COLAT, dtype=jnp.int32)[:, None, None] * N_LON + jnp.arange(N_LON, dtype=jnp.int32)[None, :, None]
    collected = []
    for panel in range(2):
        other = 1 - panel
        slot_table = ghost_slots[panel]
        safe = jnp.maximum(slot_table, 0)
        sender = safe // CAP
        offset = safe % CAP
        lat_block = sender // N_LON
        lon_block = sender % N_LON
        total = jnp.zeros((4 * LEV,) + slot_table.shape, jnp.float32)
        for slot_number in range(PARTNERS):
            match = partners[other][lat_block, lon_block, slot_number] == receiver
            picked = sent[other][:, lat_block, lon_block, slot_number * CAP + offset]
            total = total + jnp.where(match, picked, 0.0)
        collected.append(jnp.where(slot_table >= 0, total, 0.0))
    return collected


def fill_panel(center_panel, ghost):
    width = 4 * LEV
    padded = jnp.pad(center_panel, ((0, 0), (2, 2), (2, 2)))
    north = ghost[:, 0, :, 0:2 * CP].reshape(width, N_LON, 2, CP).transpose(0, 2, 1, 3).reshape(width, 2, NPH)
    south = ghost[:, N_COLAT - 1, :, 2 * CP:4 * CP].reshape(width, N_LON, 2, CP).transpose(0, 2, 1, 3).reshape(width, 2, NPH)
    west = ghost[:, :, 0, 4 * CP:4 * CP + 2 * CT].reshape(width, N_COLAT, 2, CT).transpose(0, 2, 1, 3).reshape(width, 2, NTH)
    east = ghost[:, :, N_LON - 1, 4 * CP + 2 * CT:].reshape(width, N_COLAT, 2, CT).transpose(0, 2, 1, 3).reshape(width, 2, NTH)
    padded = padded.at[:, 2:-2, 1].set(north[:, 0]).at[:, 2:-2, 0].set(north[:, 1])
    padded = padded.at[:, 2:-2, NTH + 2].set(south[:, 0]).at[:, 2:-2, NTH + 3].set(south[:, 1])
    padded = padded.at[:, 1, 2:-2].set(west[:, 0]).at[:, 0, 2:-2].set(west[:, 1])
    padded = padded.at[:, NPH + 2, 2:-2].set(east[:, 0]).at[:, NPH + 3, 2:-2].set(east[:, 1])
    return padded


def panel_rates(padded, panel, consts):
    theta = (jnp.arange(NTH, dtype=jnp.int32).astype(jnp.float32) + 0.5) * consts[0] + 0.25 * math.pi
    phi = (jnp.arange(NPH, dtype=jnp.int32).astype(jnp.float32) + 0.5) * consts[1] - 0.75 * math.pi
    sin_t = jnp.sin(theta)
    cot_t = jnp.cos(theta) / sin_t
    spins = spin_parts(theta, phi, float(panel), consts[5])
    shaped = padded.reshape(4, LEV, NPH + 4, NTH + 4)

    def level_rate(level):
        here = lax.dynamic_index_in_dim(shaped, level, 1, keepdims=False)
        below = lax.dynamic_index_in_dim(shaped, jnp.maximum(level - 1, 0), 1, keepdims=False)[:, 2:-2, 2:-2]
        above = lax.dynamic_index_in_dim(shaped, jnp.minimum(level + 1, LEV - 1), 1, keepdims=False)[:, 2:-2, 2:-2]
        radius = level.astype(jnp.float32) * consts[7] + R_LOW
        return rates(here, below, above, radius, sin_t, cot_t, spins, consts)

    stacked = lax.map(level_rate, jnp.arange(LEV, dtype=jnp.int32))
    return jnp.transpose(stacked, (1, 0, 2, 3))


def reference(state, partners, send_counts, source_cells, weights, turn_angles, ghost_slots):
    consts = constants(NTH, NPH)
    time_step = consts[2]

    def tendency(current):
        sent = sender_values(current, source_cells, weights, turn_angles, send_counts)
        ghosts = ghost_values(sent, partners, ghost_slots)
        collected = []
        for panel in range(2):
            padded = fill_panel(current[:, panel].reshape(4 * LEV, NPH, NTH), ghosts[panel])
            collected.append(panel_rates(padded, panel, consts))
        return jnp.stack(collected, axis=1)

    current = state
    for sweep_index in range(STEPS):
        first = current + time_step * tendency(current)
        current = 0.5 * (current + first + time_step * tendency(first))
    return current
```

```python
import functools
import math

import jax
import jax.numpy as jnp
import numpy as np
from jax import lax
from jax.experimental import pallas as pl
from jax.experimental.pallas import tpu as pltpu
from jax.sharding import Mesh, PartitionSpec as P

STEPS = 2
R_LOW = 0.7
HALF_ROOT = 0.7071067811865476
LANES = 128
ROWS = 16
NO_KEY = 1.0e9
SWAP = [(0, 1), (1, 0)]


def constants(lat_total, lon_total):
    d_theta = 0.5 * math.pi / lat_total
    d_phi = 1.5 * math.pi / lon_total
    spacing = R_LOW * min(d_theta, HALF_ROOT * d_phi)
    time_step = 0.25 * spacing
    kappa = 0.04 * spacing * spacing / time_step
    viscous = 0.06 * spacing * spacing / time_step
    return (
        d_theta,
        d_phi,
        time_step,
        kappa,
        viscous,
        0.05 / time_step,
        0.2 / time_step,
        4.0 * spacing,
    )


def lane_ids(rows):
    return lax.broadcasted_iota(jnp.int32, (rows, LANES), 1)


def sub_ids():
    return lax.broadcasted_iota(jnp.int32, (8, LANES), 0)


def tile(ref, u):
    return ref[pl.ds(pl.multiple_of(u * ROWS, ROWS), ROWS), :]


def gather_rows(field, src, table, sent):
    lane = lane_ids(2 * ROWS)

    def one(slot, m, accs):
        cell = src[slot * LANES + m]
        lon = lax.shift_right_logical(cell, 7)
        lat = lax.bitwise_and(cell, LANES - 1)
        both = field[pl.ds(pl.multiple_of(lon * ROWS, ROWS), 2 * ROWS), :]
        both = pltpu.roll(both, lax.bitwise_and(m - lat + LANES, LANES - 1), 1)
        near, far = accs
        near = jnp.where(lane == m, both, near)
        far = jnp.where(lane == lax.bitwise_and(m + 1, LANES - 1), both, far)
        return near, far

    def body(m, accs):
        return one(0, m, accs[0:2]) + one(1, m, accs[2:4])

    zero = jnp.zeros((2 * ROWS, LANES), jnp.float32)
    accs = lax.fori_loop(0, LANES, body, (zero, zero, zero, zero), unroll=8)
    sub = sub_ids()
    for slot in range(2):
        near, far = accs[2 * slot], accs[2 * slot + 1]
        far = pltpu.roll(far, LANES - 1, 1)
        base = slot * 8
        w0 = table[base : base + 1, :]
        w1 = table[base + 1 : base + 2, :]
        w2 = table[base + 2 : base + 3, :]
        w3 = table[base + 3 : base + 4, :]
        value = w0 * near[:ROWS] + w1 * far[:ROWS] + w2 * near[ROWS:] + w3 * far[ROWS:]
        low, high = value[:8], value[8:]
        cosine = table[base + 4 : base + 5, :]
        sine = table[base + 5 : base + 6, :]
        turned = cosine * high + jnp.where(sub < 4, sine, -sine) * pltpu.roll(high, 4, 0)
        sent[slot * ROWS : slot * ROWS + 8, :] = low
        sent[slot * ROWS + 8 : slot * ROWS + 16, :] = turned
    sent[32:40, :] = table[16:24, :]


def put_edges(field, flag, lon_cells, edge_a, edge_b):
    first = field[0 : 2 * ROWS, :]
    last = field[(lon_cells - 2) * ROWS : lon_cells * ROWS, :]
    odd = flag[0] > 0
    edge_a[...] = jnp.where(odd, first, last)
    edge_b[...] = jnp.where(odd, last, first)


def strip_of(value, col):
    return pltpu.roll(value, 4 * col + 2, 1)


def start_kernel(lon_cells, state, src, table, flag, field, sent, edge_a, edge_b, strips):
    lane = lane_ids(ROWS)
    quad = lax.shift_right_logical(lane, 2)
    for block in range(lon_cells // 32):

        def body(col, acc, block=block):
            u = block * 32 + col
            low = state[pl.ds(u, 8, stride=lon_cells), :]
            high = state[pl.ds(u + 8 * lon_cells, 8, stride=lon_cells), :]
            value = jnp.concatenate([low, high], axis=0)
            field[pl.ds(pl.multiple_of(u * ROWS, ROWS), ROWS), :] = value
            return jnp.where(quad == col, strip_of(value, col), acc)

        acc = lax.fori_loop(0, 32, body, jnp.zeros((ROWS, LANES), jnp.float32), unroll=4)
        strips[block * ROWS : (block + 1) * ROWS, :] = acc
    put_edges(field, flag, lon_cells, edge_a, edge_b)
    gather_rows(field, src, table, sent)


def key_kernel(slots, keys, listed):
    lane = lane_ids(8)
    slot = slots[...]
    peer = lax.shift_right_arithmetic(slot, 7)
    shift = lax.bitwise_and(slot - lane, LANES - 1)
    key = jnp.where(slot >= 0, (peer * LANES + shift).astype(jnp.float32), NO_KEY)
    keys[...] = key

    def cond(carry):
        count, more = carry[0], carry[1]
        return jnp.logical_and(count < LANES, more > 0)

    def body(carry):
        count, _, last, found, total = carry
        now = jnp.min(jnp.where(key > last, key, NO_KEY), axis=1, keepdims=True)
        now = jnp.broadcast_to(now, (8, LANES))
        hit = now < NO_KEY
        found = jnp.where(lane == count, jnp.where(hit, now, 0.0), found)
        total = total + jnp.where(hit, 1.0, 0.0)
        more = (jnp.min(now) < NO_KEY).astype(jnp.int32)
        return count + 1, more, now, found, total

    zero = jnp.zeros((8, LANES), jnp.float32)
    out = lax.while_loop(cond, body, (jnp.int32(0), jnp.int32(1), zero - 1.0, zero, zero))
    listed[0:8, :] = out[3].astype(jnp.int32)
    listed[8:16, :] = out[4].astype(jnp.int32)


def fill_ghosts(received, keys, listed, ghosts):
    for row in range(8):
        wanted = keys[row : row + 1, :]

        def body(i, acc, row=row, wanted=wanted):
            key = listed[row, i]
            peer = lax.shift_right_logical(key, 7)
            shift = lax.bitwise_and(key, LANES - 1)
            value = pltpu.roll(tile(received, peer), lax.bitwise_and(LANES - shift, LANES - 1), 1)
            return jnp.where(wanted == key.astype(jnp.float32), value, acc)

        acc = lax.fori_loop(0, listed[8 + row, 0], body, jnp.zeros((ROWS, LANES), jnp.float32))
        ghosts[row * ROWS : (row + 1) * ROWS, :] = acc


def merge_strips(strip_a, strip_b, flag, ghosts, merged, blocks):
    lane = lane_ids(8)
    part = lax.bitwise_and(lane, 3)
    odd = flag[1] > 0
    for block in range(blocks):
        spread = lax.shift_right_logical(lane, 2) + 32 * block
        for half in range(2):
            at = block * ROWS + half * 8
            a = strip_a[at : at + 8, :]
            b = strip_b[at : at + 8, :]
            value = jnp.where(part < 2, jnp.where(odd, a, b), jnp.where(odd, b, a))
            extra = jnp.zeros((8, LANES), jnp.float32)
            for row, where in ((0, 1), (1, 0), (2, 2), (3, 3)):
                source = ghosts[row * ROWS + half * 8 : row * ROWS + half * 8 + 8, :]
                wide = jnp.take_along_axis(source, spread, axis=1)
                extra = jnp.where(part == where, wide, extra)
            merged[at : at + 8, :] = value + extra


def coefficients(geo, lon_cells, consts, coef):
    d_theta, d_phi, step, kappa, viscous, omega, buoyancy, radial = consts
    sub = sub_ids()
    low = sub < 4
    level = lax.bitwise_and(sub, 3).astype(jnp.float32)
    inverse = 1.0 / (level * radial + R_LOW)
    base = 2 * lon_cells
    sin_t = geo[base : base + 8, :]
    cos_t = geo[base + 8 : base + 16, :]
    yang = geo[base + 16 : base + 24, :]
    keep = 1.0 - yang
    over_sin = 1.0 / sin_t
    square = inverse * inverse
    advect_t = -step / (12.0 * d_theta) * inverse
    advect_p = -step / (12.0 * d_phi) * inverse * over_sin
    values = [advect_t, advect_p]
    for half in range(2):
        spread = jnp.where(low, step * kappa, step * viscous) if half == 0 else jnp.full((8, LANES), step * viscous)
        second_t = spread * square / (12.0 * d_theta * d_theta)
        first_t = spread * square * (cos_t * over_sin) / (12.0 * d_theta)
        second_p = spread * square * (over_sin * over_sin) / (12.0 * d_phi * d_phi)
        second_r = spread / (radial * radial)
        first_r = spread * inverse / radial
        middle = -30.0 * second_t - 30.0 * second_p - 2.0 * second_r
        values += [second_t, first_t, second_p, second_r, first_r, middle]
    twice = 2.0 * step * omega
    zero = jnp.zeros((8, LANES), jnp.float32)
    sign = jnp.where(low, 1.0, -1.0)
    values += [
        jnp.where(low, 0.0, step * buoyancy),
        jnp.where(low, zero, twice * keep * sin_t),
        jnp.where(low, zero, -twice * cos_t),
        jnp.where(low, 0.0, twice) + zero,
        sign * twice * keep * cos_t,
        sign * twice * sin_t,
        jnp.where(low, zero, -twice * keep * sin_t),
        jnp.where(low, zero, twice * cos_t),
        jnp.where(low, -twice, 0.0) + zero,
    ]
    for i, value in enumerate(values):
        coef[8 * i : 8 * i + 8, :] = value


def stage_kernel(
    second, final, lon_cells, consts, *refs
):
    refs = list(refs)
    field = refs.pop(0)
    origin = refs.pop(0) if second else None
    lon_a, lon_b, strip_a, strip_b, received, keys, listed, flag, geo, src, table = refs[:11]
    refs = refs[11:]
    if final:
        result = refs.pop(0)
    else:
        result, sent, edge_a, edge_b, strips = refs[:5]
        refs = refs[5:]
    ghosts, merged, coef, sides = refs

    radial = consts[7]
    coefficients(geo, lon_cells, consts, coef)
    fill_ghosts(received, keys, listed, ghosts)
    merge_strips(strip_a, strip_b, flag, ghosts, merged, lon_cells // 32)
    odd = flag[0] > 0
    before = jnp.where(odd, lon_a[...], lon_b[...])
    after = jnp.where(odd, lon_b[...], lon_a[...])
    sides[0:ROWS, :] = before[0:ROWS] + ghosts[5 * ROWS : 6 * ROWS, :]
    sides[ROWS : 2 * ROWS, :] = before[ROWS:] + ghosts[4 * ROWS : 5 * ROWS, :]
    sides[2 * ROWS : 3 * ROWS, :] = after[0:ROWS] + ghosts[6 * ROWS : 7 * ROWS, :]
    sides[3 * ROWS : 4 * ROWS, :] = after[ROWS:] + ghosts[7 * ROWS : 8 * ROWS, :]

    lane16 = lane_ids(ROWS)
    quad = lax.shift_right_logical(lane16, 2)
    sub = sub_ids()
    low = sub < 4
    level = lax.bitwise_and(sub, 3)
    top = level == 3
    bottom = level == 0
    advect_r = -consts[2] / (2.0 * radial)

    def c(i):
        return coef[8 * i : 8 * i + 8, :]

    def update(u, block, col, down2, down1, here, up1, up2):
        border = pltpu.roll(merged[block * ROWS : (block + 1) * ROWS, :], lax.bitwise_and(LANES - 2 - 4 * col, LANES - 1), 1)
        south1 = pltpu.roll(jnp.where(lane16 == LANES - 1, border, here), 1, 1)
        south2 = pltpu.roll(jnp.where(lane16 >= LANES - 2, border, here), 2, 1)
        north1 = pltpu.roll(jnp.where(lane16 == 0, border, here), LANES - 1, 1)
        north2 = pltpu.roll(jnp.where(lane16 < 2, border, here), LANES - 2, 1)
        lat_odd = 8.0 * (north1 - south1) - (north2 - south2)
        lat_even = 16.0 * (north1 + south1) - (north2 + south2)
        lon_odd = 8.0 * (up1 - down1) - (up2 - down2)
        lon_even = 16.0 * (up1 + down1) - (up2 + down2)
        v0, v1 = here[:8], here[8:]
        r0, r1 = pltpu.roll(v0, 4, 0), pltpu.roll(v1, 4, 0)
        vel_r = jnp.where(low, r0, v0)
        vel_t = jnp.where(low, v1, r1)
        vel_p = jnp.where(low, r1, v1)
        along_t = vel_t * c(0)
        along_p = vel_p * c(1)
        along_r = vel_r * advect_r
        sin_p = geo[pl.ds(u, 1), :]
        cos_p = geo[pl.ds(lon_cells + u, 1), :]
        turn0 = c(14) * r0 + (c(15) + c(16) * sin_p) * vel_p + (c(17) * cos_p) * vel_t
        turn1 = (c(18) + c(19) * sin_p) * r1 + (c(20) + c(21) * sin_p + c(22) * cos_p) * vel_r
        out = []
        for half, value, turn in ((0, v0, turn0), (1, v1, turn1)):
            at = 2 + 6 * half
            part = slice(8 * half, 8 * half + 8)
            above = jnp.where(top, value, pltpu.roll(value, 7, 0))
            below = jnp.where(bottom, value, pltpu.roll(value, 1, 0))
            change = (
                (c(at + 1) + along_t) * lat_odd[part]
                + c(at) * lat_even[part]
                + along_p * lon_odd[part]
                + c(at + 2) * lon_even[part]
                + (c(at + 4) + along_r) * (above - below)
                + c(at + 3) * (above + below)
                + c(at + 5) * value
                + turn
            )
            out.append(value + change)
        new = jnp.concatenate(out, axis=0)
        if second:
            new = 0.5 * (tile(origin, u) + new)
        return new

    def store(u, new):
        if final:
            result[pl.ds(u, 8, stride=lon_cells), :] = new[:8]
            result[pl.ds(u + 8 * lon_cells, 8, stride=lon_cells), :] = new[8:]
        else:
            result[pl.ds(pl.multiple_of(u * ROWS, ROWS), ROWS), :] = new

    def at(u):
        if u < 0:
            return sides[(u + 2) * ROWS : (u + 3) * ROWS, :]
        if u >= lon_cells:
            return sides[(u - lon_cells + 2) * ROWS : (u - lon_cells + 3) * ROWS, :]
        return field[u * ROWS : (u + 1) * ROWS, :]

    def edge(u, acc):
        block, col = divmod(u, 32)
        new = update(u, block, col, at(u - 2), at(u - 1), at(u), at(u + 1), at(u + 2))
        store(u, new)
        return acc if final else jnp.where(quad == col, strip_of(new, col), acc)

    blocks = lon_cells // 32
    for block in range(blocks):
        acc = jnp.zeros((ROWS, LANES), jnp.float32)
        first_col, last_col = 0, 32
        if block == 0:
            acc = edge(1, edge(0, acc))
            first_col = 2
        if block == blocks - 1:
            acc = edge(lon_cells - 1, edge(lon_cells - 2, acc))
            last_col = 30

        def body(col, acc, block=block):
            u = block * 32 + col
            new = update(u, block, col, tile(field, u - 2), tile(field, u - 1), tile(field, u), tile(field, u + 1), tile(field, u + 2))
            store(u, new)
            return acc if final else jnp.where(quad == col, strip_of(new, col), acc)

        acc = lax.fori_loop(first_col, last_col, body, acc, unroll=2)
        if not final:
            strips[block * ROWS : (block + 1) * ROWS, :] = acc
    if not final:
        put_edges(result, flag, lon_cells, edge_a, edge_b)
        gather_rows(result, src, table, sent)


def pairs(count, first):
    route = []
    for low in range(first, count - 1, 2):
        route += [(low, low + 1), (low + 1, low)]
    return route


def on_device(state, partners, send_counts, source_cells, weights, turn_angles, ghost_slots):
    lat_blocks = lax.axis_size("colat")
    lon_axes = ("lon_hi", "core")
    lon_blocks = lax.axis_size(lon_axes)
    peers = lat_blocks * lon_blocks
    lon_cells, lat_cells = state.shape[3], state.shape[4]
    consts = constants(lat_cells * lat_blocks, lon_cells * lon_blocks)
    core = lax.axis_index("core")
    colat = lax.axis_index("colat")
    lon = lax.axis_index(lon_axes)
    yang = lax.axis_index("panel").astype(jnp.float32)
    flag = jnp.stack([lon % 2, colat % 2]).astype(jnp.int32)

    live = jnp.arange(LANES, dtype=jnp.int32)[None, :] < send_counts[0, 0, 0][:, None]
    turn = turn_angles[0, 0, 0].reshape(2, LANES)
    wts = jnp.where(live[None], weights[:, 0, 0, 0].reshape(4, 2, LANES), 0.0)
    named = jnp.broadcast_to(partners[0, 0, 0].astype(jnp.float32)[:, None], (2, LANES))
    blank = jnp.zeros((2, LANES), jnp.float32)
    table = jnp.stack([wts[0], wts[1], wts[2], wts[3], jnp.cos(turn), jnp.sin(turn), blank, blank], axis=1)
    table = jnp.concatenate([table.reshape(16, LANES), named, jnp.zeros((6, LANES), jnp.float32)])
    src = source_cells[0, 0, 0]

    theta = ((colat * lat_cells + jnp.arange(lat_cells, dtype=jnp.int32)).astype(jnp.float32) + 0.5) * consts[0] + 0.25 * math.pi
    phi = ((lon * lon_cells + jnp.arange(lon_cells, dtype=jnp.int32)).astype(jnp.float32) + 0.5) * consts[1] - 0.75 * math.pi
    geo = jnp.concatenate(
        [
            jnp.broadcast_to((yang * jnp.sin(phi))[:, None], (lon_cells, LANES)),
            jnp.broadcast_to((yang * jnp.cos(phi))[:, None], (lon_cells, LANES)),
            jnp.broadcast_to(jnp.sin(theta)[None], (8, LANES)),
            jnp.broadcast_to(jnp.cos(theta)[None], (8, LANES)),
            jnp.broadcast_to(yang, (8, LANES)),
        ]
    )
    slot = ghost_slots[0, 0, 0]
    poles = jnp.pad(slot[: 4 * lon_cells].reshape(4, lon_cells), ((0, 0), (0, LANES - lon_cells)), constant_values=-1)
    slots = jnp.concatenate([poles, slot[4 * lon_cells :].reshape(4, LANES)])

    vmem = pl.BlockSpec(memory_space=pltpu.VMEM)
    smem = pl.BlockSpec(memory_space=pltpu.SMEM)

    def f32(*shape):
        return jax.ShapeDtypeStruct(shape, jnp.float32)

    cells = lon_cells * ROWS
    strip_rows = lon_cells // 32 * ROWS
    moving = [f32(cells, LANES), f32(40, LANES), f32(32, LANES), f32(32, LANES), f32(strip_rows, LANES)]
    params = pltpu.CompilerParams(vmem_limit_bytes=16 * 1024 * 1024)

    keys, listed = pl.pallas_call(
        key_kernel,
        out_shape=[f32(8, LANES), jax.ShapeDtypeStruct((16, LANES), jnp.int32)],
        in_specs=[vmem],
        out_specs=[vmem, vmem],
        compiler_params=params,
    )(slots)

    field, sent, edge_a, edge_b, strips = pl.pallas_call(
        functools.partial(start_kernel, lon_cells),
        out_shape=moving,
        in_specs=[vmem, smem, vmem, smem],
        out_specs=[vmem] * 5,
        compiler_params=params,
    )(state.reshape(cells, LANES), src, table, flag)

    place = jnp.arange(peers, dtype=jnp.int32)[:, None, None]

    def exchange(sent, edge_a, edge_b, strips):
        over = lax.ppermute(sent, "panel", SWAP)
        mate = lax.ppermute(over, "core", SWAP)
        buffer = jnp.zeros((peers, ROWS, LANES), jnp.float32)
        for message, own in ((over, core), (mate, 1 - core)):
            for number in range(2):
                target = message[32 + number, 0].astype(jnp.int32)
                spot = jnp.where(target % 2 == core, target - core + own, -1)
                buffer = buffer + jnp.where(place == spot, message[number * ROWS : (number + 1) * ROWS][None], 0.0)
        buffer, edge_a, edge_b, strips = lax.optimization_barrier((buffer, edge_a, edge_b, strips))
        received = lax.all_to_all(
            buffer.reshape(peers // 2, 2 * ROWS, LANES), ("colat", "lon_hi"), split_axis=0, concat_axis=0, tiled=True
        )
        lon_a = lax.ppermute(edge_a, lon_axes, pairs(lon_blocks, 0))
        lon_b = lax.ppermute(edge_b, lon_axes, pairs(lon_blocks, 1))
        strip_a = lax.ppermute(strips, "colat", pairs(lat_blocks, 0))
        strip_b = lax.ppermute(strips, "colat", pairs(lat_blocks, 1))
        return lon_a, lon_b, strip_a, strip_b, received.reshape(peers * ROWS, LANES)

    origin = field
    for number in range(2 * STEPS):
        second = number % 2 == 1
        final = number == 2 * STEPS - 1
        lon_a, lon_b, strip_a, strip_b, received = exchange(sent, edge_a, edge_b, strips)
        operands = [field] + ([origin] if second else [])
        specs = [vmem] * len(operands) + [vmem] * 5 + [vmem, smem, smem, vmem, smem, vmem]
        operands += [lon_a, lon_b, strip_a, strip_b, received, keys, listed, flag, geo, src, table]
        out = pl.pallas_call(
            functools.partial(stage_kernel, second, final, lon_cells, consts),
            out_shape=moving[:1] if final else moving,
            in_specs=specs,
            out_specs=[vmem] * (1 if final else 5),
            scratch_shapes=[
                pltpu.VMEM((8 * ROWS, LANES), jnp.float32),
                pltpu.VMEM((strip_rows, LANES), jnp.float32),
                pltpu.VMEM((8 * 23, LANES), jnp.float32),
                pltpu.VMEM((4 * ROWS, LANES), jnp.float32),
            ],
            compiler_params=params,
        )(*operands)
        if final:
            return out[0].reshape(state.shape)
        field, sent, edge_a, edge_b, strips = out
        if second:
            origin = field


def solution(mesh):
    lon = mesh.shape["lon"]
    fine = Mesh(
        mesh.devices.reshape(mesh.shape["panel"], mesh.shape["colat"], lon // 2, 2), ("panel", "colat", "lon_hi", "core")
    )
    lon_axes = ("lon_hi", "core")
    table = P("panel", "colat", lon_axes, None)
    in_specs = (
        P(None, "panel", None, lon_axes, "colat"),
        table,
        table,
        table,
        P(None, "panel", "colat", lon_axes, None),
        table,
        table,
    )
    out_specs = P(None, "panel", None, lon_axes, "colat")
    return jax.shard_map(on_device, mesh=fine, in_specs=in_specs, out_specs=out_specs, check_vma=False)
```

```python
import functools
import math

import jax
import jax.numpy as jnp
import numpy as np
from jax import lax
from jax.experimental import pallas as pl
from jax.experimental.pallas import tpu as pltpu
from jax.sharding import Mesh, PartitionSpec as P

STEPS = 2
R_LOW = 0.7
HALF_ROOT = 0.7071067811865476
LANES = 128
ROWS = 16
NO_KEY = 1.0e9
GROUP = 8
SWAP = [(0, 1), (1, 0)]


def constants(lat_total, lon_total):
    d_theta = 0.5 * math.pi / lat_total
    d_phi = 1.5 * math.pi / lon_total
    spacing = R_LOW * min(d_theta, HALF_ROOT * d_phi)
    time_step = 0.25 * spacing
    kappa = 0.04 * spacing * spacing / time_step
    viscous = 0.06 * spacing * spacing / time_step
    return (
        d_theta,
        d_phi,
        time_step,
        kappa,
        viscous,
        0.05 / time_step,
        0.2 / time_step,
        4.0 * spacing,
    )


def lane_ids(rows):
    return lax.broadcasted_iota(jnp.int32, (rows, LANES), 1)


def sub_ids():
    return lax.broadcasted_iota(jnp.int32, (8, LANES), 0)


def rows_of(u):
    if isinstance(u, int):
        return slice(u * ROWS, (u + 1) * ROWS)
    return pl.ds(pl.multiple_of(u * ROWS, ROWS), ROWS)


def tile(ref, u):
    return ref[rows_of(u), :]


def gather_rows(field, src, table, sent):
    lane = lane_ids(2 * ROWS)

    def one(slot, m, accs):
        cell = src[slot * LANES + m]
        lon = lax.shift_right_logical(cell, 7)
        lat = lax.bitwise_and(cell, LANES - 1)
        both = field[pl.ds(pl.multiple_of(lon * ROWS, ROWS), 2 * ROWS), :]
        both = pltpu.roll(both, lax.bitwise_and(m - lat + LANES, LANES - 1), 1)
        near, far = accs
        near = jnp.where(lane == m, both, near)
        far = jnp.where(lane == lax.bitwise_and(m + 1, LANES - 1), both, far)
        return near, far

    def body(m, accs):
        return one(0, m, accs[0:2]) + one(1, m, accs[2:4])

    zero = jnp.zeros((2 * ROWS, LANES), jnp.float32)
    accs = lax.fori_loop(0, LANES, body, (zero, zero, zero, zero), unroll=8)
    sub = sub_ids()
    for slot in range(2):
        near, far = accs[2 * slot], accs[2 * slot + 1]
        far = pltpu.roll(far, LANES - 1, 1)
        base = slot * 8
        w0 = table[base : base + 1, :]
        w1 = table[base + 1 : base + 2, :]
        w2 = table[base + 2 : base + 3, :]
        w3 = table[base + 3 : base + 4, :]
        value = w0 * near[:ROWS] + w1 * far[:ROWS] + w2 * near[ROWS:] + w3 * far[ROWS:]
        low, high = value[:8], value[8:]
        cosine = table[base + 4 : base + 5, :]
        sine = table[base + 5 : base + 6, :]
        turned = cosine * high + jnp.where(sub < 4, sine, -sine) * pltpu.roll(high, 4, 0)
        sent[slot * ROWS : slot * ROWS + 8, :] = low
        sent[slot * ROWS + 8 : slot * ROWS + 16, :] = turned
    sent[32:40, :] = table[16:24, :]


def put_edges(field, flag, lon_cells, edge_a, edge_b):
    first = field[0 : 2 * ROWS, :]
    last = field[(lon_cells - 2) * ROWS : lon_cells * ROWS, :]
    odd = flag[0] > 0
    edge_a[...] = jnp.where(odd, first, last)
    edge_b[...] = jnp.where(odd, last, first)


def strip_of(value, col):
    return pltpu.roll(value, 4 * col + 2, 1)


def start_kernel(lon_cells, state, src, table, flag, field, sent, edge_a, edge_b, strips):
    lane = lane_ids(ROWS)
    quad = lax.shift_right_logical(lane, 2)
    for block in range(lon_cells // 32):

        def body(col, acc, block=block):
            u = block * 32 + col
            low = state[pl.ds(u, 8, stride=lon_cells), :]
            high = state[pl.ds(u + 8 * lon_cells, 8, stride=lon_cells), :]
            value = jnp.concatenate([low, high], axis=0)
            field[pl.ds(pl.multiple_of(u * ROWS, ROWS), ROWS), :] = value
            return jnp.where(quad == col, strip_of(value, col), acc)

        acc = lax.fori_loop(0, 32, body, jnp.zeros((ROWS, LANES), jnp.float32), unroll=4)
        strips[block * ROWS : (block + 1) * ROWS, :] = acc
    put_edges(field, flag, lon_cells, edge_a, edge_b)
    gather_rows(field, src, table, sent)


def key_kernel(slots, keys, listed):
    lane = lane_ids(8)
    slot = slots[...]
    peer = lax.shift_right_arithmetic(slot, 7)
    shift = lax.bitwise_and(slot - lane, LANES - 1)
    key = jnp.where(slot >= 0, (peer * LANES + shift).astype(jnp.float32), NO_KEY)
    keys[...] = key

    def cond(carry):
        count, more = carry[0], carry[1]
        return jnp.logical_and(count < LANES, more > 0)

    def body(carry):
        count, _, last, found, total = carry
        now = jnp.min(jnp.where(key > last, key, NO_KEY), axis=1, keepdims=True)
        now = jnp.broadcast_to(now, (8, LANES))
        hit = now < NO_KEY
        found = jnp.where(lane == count, jnp.where(hit, now, 0.0), found)
        total = total + jnp.where(hit, 1.0, 0.0)
        more = (jnp.min(now) < NO_KEY).astype(jnp.int32)
        return count + 1, more, now, found, total

    zero = jnp.zeros((8, LANES), jnp.float32)
    out = lax.while_loop(cond, body, (jnp.int32(0), jnp.int32(1), zero - 1.0, zero, zero))
    listed[0:8, :] = out[3].astype(jnp.int32)
    listed[8:16, :] = out[4].astype(jnp.int32)


def fill_ghosts(received, keys, listed, ghosts):
    for row in range(8):
        wanted = keys[row : row + 1, :]

        def body(i, acc, row=row, wanted=wanted):
            key = listed[row, i]
            peer = lax.shift_right_logical(key, 7)
            shift = lax.bitwise_and(key, LANES - 1)
            value = pltpu.roll(tile(received, peer), lax.bitwise_and(LANES - shift, LANES - 1), 1)
            return jnp.where(wanted == key.astype(jnp.float32), value, acc)

        acc = lax.fori_loop(0, listed[8 + row, 0], body, jnp.zeros((ROWS, LANES), jnp.float32))
        ghosts[row * ROWS : (row + 1) * ROWS, :] = acc


def merge_strips(strip_a, strip_b, flag, ghosts, merged, blocks):
    lane = lane_ids(8)
    part = lax.bitwise_and(lane, 3)
    odd = flag[1] > 0
    for block in range(blocks):
        spread = lax.shift_right_logical(lane, 2) + 32 * block
        for half in range(2):
            at = block * ROWS + half * 8
            a = strip_a[at : at + 8, :]
            b = strip_b[at : at + 8, :]
            value = jnp.where(part < 2, jnp.where(odd, a, b), jnp.where(odd, b, a))
            extra = jnp.zeros((8, LANES), jnp.float32)
            for row, where in ((0, 1), (1, 0), (2, 2), (3, 3)):
                source = ghosts[row * ROWS + half * 8 : row * ROWS + half * 8 + 8, :]
                wide = jnp.take_along_axis(source, spread, axis=1)
                extra = jnp.where(part == where, wide, extra)
            merged[at : at + 8, :] = value + extra


def coefficients(geo, lon_cells, consts, coef):
    d_theta, d_phi, step, kappa, viscous, omega, buoyancy, radial = consts
    sub = sub_ids()
    low = sub < 4
    level = lax.bitwise_and(sub, 3).astype(jnp.float32)
    inverse = 1.0 / (level * radial + R_LOW)
    base = 2 * lon_cells
    sin_t = geo[base : base + 8, :]
    cos_t = geo[base + 8 : base + 16, :]
    yang = geo[base + 16 : base + 24, :]
    keep = 1.0 - yang
    over_sin = 1.0 / sin_t
    square = inverse * inverse
    advect_t = -step / (12.0 * d_theta) * inverse
    advect_p = -step / (12.0 * d_phi) * inverse * over_sin
    values = [advect_t, advect_p]
    for half in range(2):
        spread = jnp.where(low, step * kappa, step * viscous) if half == 0 else jnp.full((8, LANES), step * viscous)
        second_t = spread * square / (12.0 * d_theta * d_theta)
        first_t = spread * square * (cos_t * over_sin) / (12.0 * d_theta)
        second_p = spread * square * (over_sin * over_sin) / (12.0 * d_phi * d_phi)
        second_r = spread / (radial * radial)
        first_r = spread * inverse / radial
        middle = -30.0 * second_t - 30.0 * second_p - 2.0 * second_r
        values += [second_t, first_t, second_p, second_r, first_r, middle]
    twice = 2.0 * step * omega
    zero = jnp.zeros((8, LANES), jnp.float32)
    sign = jnp.where(low, 1.0, -1.0)
    values += [
        jnp.where(low, 0.0, step * buoyancy),
        jnp.where(low, zero, twice * keep * sin_t),
        jnp.where(low, zero, -twice * cos_t),
        jnp.where(low, 0.0, twice) + zero,
        sign * twice * keep * cos_t,
        sign * twice * sin_t,
        jnp.where(low, zero, -twice * keep * sin_t),
        jnp.where(low, zero, twice * cos_t),
        jnp.where(low, -twice, 0.0) + zero,
    ]
    for i, value in enumerate(values):
        coef[8 * i : 8 * i + 8, :] = value


def stage_kernel(
    second, final, lon_cells, consts, *refs
):
    refs = list(refs)
    field = refs.pop(0)
    origin = refs.pop(0) if second else None
    lon_a, lon_b, strip_a, strip_b, received, keys, listed, flag, geo, src, table = refs[:11]
    refs = refs[11:]
    if final:
        result = refs.pop(0)
    else:
        result, sent, edge_a, edge_b, strips = refs[:5]
        refs = refs[5:]
    ghosts, merged, coef, sides = refs

    radial = consts[7]
    coefficients(geo, lon_cells, consts, coef)
    fill_ghosts(received, keys, listed, ghosts)
    merge_strips(strip_a, strip_b, flag, ghosts, merged, lon_cells // 32)
    odd = flag[0] > 0
    before = jnp.where(odd, lon_a[...], lon_b[...])
    after = jnp.where(odd, lon_b[...], lon_a[...])
    sides[0:ROWS, :] = before[0:ROWS] + ghosts[5 * ROWS : 6 * ROWS, :]
    sides[ROWS : 2 * ROWS, :] = before[ROWS:] + ghosts[4 * ROWS : 5 * ROWS, :]
    sides[2 * ROWS : 3 * ROWS, :] = after[0:ROWS] + ghosts[6 * ROWS : 7 * ROWS, :]
    sides[3 * ROWS : 4 * ROWS, :] = after[ROWS:] + ghosts[7 * ROWS : 8 * ROWS, :]

    lane16 = lane_ids(ROWS)
    quad = lax.shift_right_logical(lane16, 2)
    sub = sub_ids()
    low = sub < 4
    level = lax.bitwise_and(sub, 3)
    top = level == 3
    bottom = level == 0
    advect_r = -consts[2] / (2.0 * radial)

    def c(i):
        return coef[8 * i : 8 * i + 8, :]

    def update(u, block, col, down2, down1, here, up1, up2):
        border = pltpu.roll(tile(merged, block), lax.bitwise_and(LANES - 2 - 4 * col, LANES - 1), 1)
        south1 = pltpu.roll(jnp.where(lane16 == LANES - 1, border, here), 1, 1)
        south2 = pltpu.roll(jnp.where(lane16 >= LANES - 2, border, here), 2, 1)
        north1 = pltpu.roll(jnp.where(lane16 == 0, border, here), LANES - 1, 1)
        north2 = pltpu.roll(jnp.where(lane16 < 2, border, here), LANES - 2, 1)
        lat_odd = 8.0 * (north1 - south1) - (north2 - south2)
        lat_even = 16.0 * (north1 + south1) - (north2 + south2)
        lon_odd = 8.0 * (up1 - down1) - (up2 - down2)
        lon_even = 16.0 * (up1 + down1) - (up2 + down2)
        v0, v1 = here[:8], here[8:]
        r0, r1 = pltpu.roll(v0, 4, 0), pltpu.roll(v1, 4, 0)
        vel_r = jnp.where(low, r0, v0)
        vel_t = jnp.where(low, v1, r1)
        vel_p = jnp.where(low, r1, v1)
        along_t = vel_t * c(0)
        along_p = vel_p * c(1)
        along_r = vel_r * advect_r
        sin_p = geo[pl.ds(u, 1), :]
        cos_p = geo[pl.ds(lon_cells + u, 1), :]
        turn0 = c(14) * r0 + (c(15) + c(16) * sin_p) * vel_p + (c(17) * cos_p) * vel_t
        turn1 = (c(18) + c(19) * sin_p) * r1 + (c(20) + c(21) * sin_p + c(22) * cos_p) * vel_r
        out = []
        for half, value, turn in ((0, v0, turn0), (1, v1, turn1)):
            at = 2 + 6 * half
            part = slice(8 * half, 8 * half + 8)
            above = jnp.where(top, value, pltpu.roll(value, 7, 0))
            below = jnp.where(bottom, value, pltpu.roll(value, 1, 0))
            change = (
                (c(at + 1) + along_t) * lat_odd[part]
                + c(at) * lat_even[part]
                + along_p * lon_odd[part]
                + c(at + 2) * lon_even[part]
                + (c(at + 4) + along_r) * (above - below)
                + c(at + 3) * (above + below)
                + c(at + 5) * value
                + turn
            )
            out.append(value + change)
        new = jnp.concatenate(out, axis=0)
        if second:
            new = 0.5 * (tile(origin, u) + new)
        return new

    def store(u, new):
        if final:
            result[pl.ds(u, 8, stride=lon_cells), :] = new[:8]
            result[pl.ds(u + 8 * lon_cells, 8, stride=lon_cells), :] = new[8:]
        else:
            result[rows_of(u), :] = new

    def at(u):
        if u < 0:
            return sides[(u + 2) * ROWS : (u + 3) * ROWS, :]
        if u >= lon_cells:
            return sides[(u - lon_cells + 2) * ROWS : (u - lon_cells + 3) * ROWS, :]
        return field[u * ROWS : (u + 1) * ROWS, :]

    def group(index, block, col, tiles):
        acc = jnp.zeros((ROWS, LANES), jnp.float32)
        for k in range(GROUP):
            new = update(index + k, block, col + k, *tiles[k : k + 5])
            store(index + k, new)
            if not final:
                acc = jnp.where(quad == col + k, strip_of(new, col + k), acc)
        if not final:
            rows = rows_of(block)
            mine = jnp.logical_and(quad >= col, quad < col + GROUP)
            strips[rows, :] = jnp.where(mine, acc, strips[rows, :])

    if not final:
        strips[...] = jnp.zeros(strips.shape, jnp.float32)
    for index in (0, lon_cells - GROUP):
        group(index, index // 32, index % 32, [at(u) for u in range(index - 2, index + GROUP + 2)])

    def body(number, carry):
        index = number * GROUP
        tiles = [tile(field, index + k) for k in range(-2, GROUP + 2)]
        group(index, lax.shift_right_logical(index, 5), lax.bitwise_and(index, 31), tiles)
        return carry

    lax.fori_loop(1, lon_cells // GROUP - 1, body, 0)
    if not final:
        put_edges(result, flag, lon_cells, edge_a, edge_b)
        gather_rows(result, src, table, sent)


def pack_kernel(message_a, message_b, flag, _, buffer, staged, sems):
    core = flag[0]
    copies = []
    for number, (message, own) in enumerate(((message_a, core), (message_b, 1 - core))):
        target0 = jnp.max(message[32:33, :]).astype(jnp.int32)
        target1 = jnp.max(message[33:34, :]).astype(jnp.int32)
        same = target0 == target1
        slot0, slot1 = message[0:ROWS, :], message[ROWS : 2 * ROWS, :]
        staged[2 * number * ROWS : (2 * number + 1) * ROWS, :] = jnp.where(same, slot0 + slot1, slot0)
        staged[(2 * number + 1) * ROWS : (2 * number + 2) * ROWS, :] = slot1
        for slot, target in ((0, target0), (1, target1)):
            wanted = lax.bitwise_and(target, 1) == core
            if slot == 1:
                wanted = jnp.logical_and(wanted, jnp.logical_not(same))
            place = pl.multiple_of((target - core + own) * ROWS, ROWS)
            at = 2 * number + slot
            copy = pltpu.make_async_copy(
                staged.at[pl.ds(at * ROWS, ROWS), :], buffer.at[pl.ds(place, ROWS), :], sems.at[at]
            )
            copies.append((wanted, copy))
    for wanted, copy in copies:
        pl.when(wanted)(copy.start)
    for wanted, copy in copies:
        pl.when(wanted)(copy.wait)


def pairs(count, first):
    route = []
    for low in range(first, count - 1, 2):
        route += [(low, low + 1), (low + 1, low)]
    return route


def on_device(state, partners, send_counts, source_cells, weights, turn_angles, ghost_slots):
    lat_blocks = lax.axis_size("colat")
    lon_axes = ("lon_hi", "core")
    lon_blocks = lax.axis_size(lon_axes)
    peers = lat_blocks * lon_blocks
    lon_cells, lat_cells = state.shape[3], state.shape[4]
    consts = constants(lat_cells * lat_blocks, lon_cells * lon_blocks)
    core = lax.axis_index("core")
    colat = lax.axis_index("colat")
    lon = lax.axis_index(lon_axes)
    yang = lax.axis_index("panel").astype(jnp.float32)
    flag = jnp.stack([lon % 2, colat % 2]).astype(jnp.int32)

    live = jnp.arange(LANES, dtype=jnp.int32)[None, :] < send_counts[0, 0, 0][:, None]
    turn = turn_angles[0, 0, 0].reshape(2, LANES)
    wts = jnp.where(live[None], weights[:, 0, 0, 0].reshape(4, 2, LANES), 0.0)
    named = jnp.broadcast_to(partners[0, 0, 0].astype(jnp.float32)[:, None], (2, LANES))
    blank = jnp.zeros((2, LANES), jnp.float32)
    table = jnp.stack([wts[0], wts[1], wts[2], wts[3], jnp.cos(turn), jnp.sin(turn), blank, blank], axis=1)
    table = jnp.concatenate([table.reshape(16, LANES), named, jnp.zeros((6, LANES), jnp.float32)])
    src = source_cells[0, 0, 0]

    theta = ((colat * lat_cells + jnp.arange(lat_cells, dtype=jnp.int32)).astype(jnp.float32) + 0.5) * consts[0] + 0.25 * math.pi
    phi = ((lon * lon_cells + jnp.arange(lon_cells, dtype=jnp.int32)).astype(jnp.float32) + 0.5) * consts[1] - 0.75 * math.pi
    geo = jnp.concatenate(
        [
            jnp.broadcast_to((yang * jnp.sin(phi))[:, None], (lon_cells, LANES)),
            jnp.broadcast_to((yang * jnp.cos(phi))[:, None], (lon_cells, LANES)),
            jnp.broadcast_to(jnp.sin(theta)[None], (8, LANES)),
            jnp.broadcast_to(jnp.cos(theta)[None], (8, LANES)),
            jnp.broadcast_to(yang, (8, LANES)),
        ]
    )
    slot = ghost_slots[0, 0, 0]
    poles = jnp.pad(slot[: 4 * lon_cells].reshape(4, lon_cells), ((0, 0), (0, LANES - lon_cells)), constant_values=-1)
    slots = jnp.concatenate([poles, slot[4 * lon_cells :].reshape(4, LANES)])

    vmem = pl.BlockSpec(memory_space=pltpu.VMEM)
    smem = pl.BlockSpec(memory_space=pltpu.SMEM)

    def f32(*shape):
        return jax.ShapeDtypeStruct(shape, jnp.float32)

    cells = lon_cells * ROWS
    strip_rows = lon_cells // 32 * ROWS
    moving = [f32(cells, LANES), f32(40, LANES), f32(32, LANES), f32(32, LANES), f32(strip_rows, LANES)]
    params = pltpu.CompilerParams(vmem_limit_bytes=16 * 1024 * 1024)

    keys, listed = pl.pallas_call(
        key_kernel,
        out_shape=[f32(8, LANES), jax.ShapeDtypeStruct((16, LANES), jnp.int32)],
        in_specs=[vmem],
        out_specs=[vmem, vmem],
        compiler_params=params,
    )(slots)

    field, sent, edge_a, edge_b, strips = pl.pallas_call(
        functools.partial(start_kernel, lon_cells),
        out_shape=moving,
        in_specs=[vmem, smem, vmem, smem],
        out_specs=[vmem] * 5,
        compiler_params=params,
    )(state.reshape(cells, LANES), src, table, flag)

    hbm = pl.BlockSpec(memory_space=pl.ANY)

    def exchange(buffer, sent, edge_a, edge_b, strips):
        over = lax.ppermute(sent, "panel", SWAP)
        mate = lax.ppermute(over, "core", SWAP)
        buffer = pl.pallas_call(
            pack_kernel,
            out_shape=f32(peers * ROWS, LANES),
            in_specs=[vmem, vmem, smem, hbm],
            out_specs=hbm,
            scratch_shapes=[pltpu.VMEM((4 * ROWS, LANES), jnp.float32), pltpu.SemaphoreType.DMA((4,))],
            input_output_aliases={3: 0},
            compiler_params=params,
        )(over, mate, flag, buffer)
        buffer, edge_a, edge_b, strips = lax.optimization_barrier((buffer, edge_a, edge_b, strips))
        received = lax.all_to_all(
            buffer.reshape(peers // 2, 2 * ROWS, LANES), ("colat", "lon_hi"), split_axis=0, concat_axis=0, tiled=True
        )
        lon_a = lax.ppermute(edge_a, lon_axes, pairs(lon_blocks, 0))
        lon_b = lax.ppermute(edge_b, lon_axes, pairs(lon_blocks, 1))
        strip_a = lax.ppermute(strips, "colat", pairs(lat_blocks, 0))
        strip_b = lax.ppermute(strips, "colat", pairs(lat_blocks, 1))
        return buffer, lon_a, lon_b, strip_a, strip_b, received.reshape(peers * ROWS, LANES)

    origin = field
    buffer = jnp.zeros((peers * ROWS, LANES), jnp.float32)
    for number in range(2 * STEPS):
        second = number % 2 == 1
        final = number == 2 * STEPS - 1
        buffer, lon_a, lon_b, strip_a, strip_b, received = exchange(buffer, sent, edge_a, edge_b, strips)
        operands = [field] + ([origin] if second else [])
        specs = [vmem] * len(operands) + [vmem] * 5 + [vmem, smem, smem, vmem, smem, vmem]
        operands += [lon_a, lon_b, strip_a, strip_b, received, keys, listed, flag, geo, src, table]
        out = pl.pallas_call(
            functools.partial(stage_kernel, second, final, lon_cells, consts),
            out_shape=moving[:1] if final else moving,
            in_specs=specs,
            out_specs=[vmem] * (1 if final else 5),
            scratch_shapes=[
                pltpu.VMEM((8 * ROWS, LANES), jnp.float32),
                pltpu.VMEM((strip_rows, LANES), jnp.float32),
                pltpu.VMEM((8 * 23, LANES), jnp.float32),
                pltpu.VMEM((4 * ROWS, LANES), jnp.float32),
            ],
            compiler_params=params,
        )(*operands)
        if final:
            return out[0].reshape(state.shape)
        field, sent, edge_a, edge_b, strips = out
        if second:
            origin = field


def solution(mesh):
    lon = mesh.shape["lon"]
    fine = Mesh(
        mesh.devices.reshape(mesh.shape["panel"], mesh.shape["colat"], lon // 2, 2), ("panel", "colat", "lon_hi", "core")
    )
    lon_axes = ("lon_hi", "core")
    table = P("panel", "colat", lon_axes, None)
    in_specs = (
        P(None, "panel", None, lon_axes, "colat"),
        table,
        table,
        table,
        P(None, "panel", "colat", lon_axes, None),
        table,
        table,
    )
    out_specs = P(None, "panel", None, lon_axes, "colat")
    return jax.shard_map(on_device, mesh=fine, in_specs=in_specs, out_specs=out_specs, check_vma=False)
```

```python
import functools
import math

import jax
import jax.numpy as jnp
import numpy as np
from jax import lax
from jax.experimental import pallas as pl
from jax.experimental.pallas import tpu as pltpu
from jax.sharding import Mesh, PartitionSpec as P

STEPS = 2
R_LOW = 0.7
HALF_ROOT = 0.7071067811865476
LANES = 128
ROWS = 16
NO_KEY = 1.0e9
GROUP = 8
SWAP = [(0, 1), (1, 0)]


def constants(lat_total, lon_total):
    d_theta = 0.5 * math.pi / lat_total
    d_phi = 1.5 * math.pi / lon_total
    spacing = R_LOW * min(d_theta, HALF_ROOT * d_phi)
    time_step = 0.25 * spacing
    kappa = 0.04 * spacing * spacing / time_step
    viscous = 0.06 * spacing * spacing / time_step
    return (
        d_theta,
        d_phi,
        time_step,
        kappa,
        viscous,
        0.05 / time_step,
        0.2 / time_step,
        4.0 * spacing,
    )


def lane_ids(rows):
    return lax.broadcasted_iota(jnp.int32, (rows, LANES), 1)


def sub_ids():
    return lax.broadcasted_iota(jnp.int32, (8, LANES), 0)


def rows_of(u):
    if isinstance(u, int):
        return slice(u * ROWS, (u + 1) * ROWS)
    return pl.ds(pl.multiple_of(u * ROWS, ROWS), ROWS)


def tile(ref, u):
    return ref[rows_of(u), :]


def pick(field, src, at, m, slot, accs):
    lane = lane_ids(2 * ROWS)
    cell = src[at]
    lon = lax.shift_right_logical(cell, 7)
    lat = lax.bitwise_and(cell, LANES - 1)
    both = field[pl.ds(pl.multiple_of(lon * ROWS, ROWS), 2 * ROWS), :]
    both = pltpu.roll(both, lax.bitwise_and(m - lat + LANES, LANES - 1), 1)
    here = lane == m
    beside = lane == lax.bitwise_and(m + 1, LANES - 1)
    accs = list(accs)
    for number in range(2):
        if isinstance(slot, int) and slot != number:
            continue
        ours, next_to = here, beside
        if not isinstance(slot, int):
            shown = jnp.where(slot == number, m, 2 * LANES)
            ours = lane == shown
            next_to = jnp.logical_and(beside, slot == number)
        accs[2 * number] = jnp.where(ours, both, accs[2 * number])
        accs[2 * number + 1] = jnp.where(next_to, both, accs[2 * number + 1])
    return tuple(accs)


def gather_all(field, src, lon_cells=0, listed=None):
    def note(at, count):
        if listed is None:
            return count
        cell = src[at]
        lon = lax.shift_right_logical(cell, 7)
        lat = lax.bitwise_and(cell, LANES - 1)
        low = jnp.logical_or(lat < 2, lon < 2)
        high = jnp.logical_or(lat >= LANES - 3, lon >= lon_cells - 3)
        listed[count] = at
        return count + jnp.logical_or(low, high).astype(jnp.int32)

    def body(m, carry):
        count, accs = carry
        accs = pick(field, src, m, m, 0, accs)
        count = note(m, count)
        accs = pick(field, src, LANES + m, m, 1, accs)
        count = note(LANES + m, count)
        return count, accs

    zero = jnp.zeros((2 * ROWS, LANES), jnp.float32)
    count, accs = lax.fori_loop(0, LANES, body, (jnp.int32(0), (zero, zero, zero, zero)), unroll=8)
    if listed is not None:
        for k in range(4):
            listed[count + k] = 0
        listed[listed.shape[0] - 1] = count
    return accs


def finish_rows(accs, table, sent):
    sub = sub_ids()
    for slot in range(2):
        near, far = accs[2 * slot], accs[2 * slot + 1]
        far = pltpu.roll(far, LANES - 1, 1)
        base = slot * 8
        w0 = table[base : base + 1, :]
        w1 = table[base + 1 : base + 2, :]
        w2 = table[base + 2 : base + 3, :]
        w3 = table[base + 3 : base + 4, :]
        value = w0 * near[:ROWS] + w1 * far[:ROWS] + w2 * near[ROWS:] + w3 * far[ROWS:]
        low, high = value[:8], value[8:]
        cosine = table[base + 4 : base + 5, :]
        sine = table[base + 5 : base + 6, :]
        turned = cosine * high + jnp.where(sub < 4, sine, -sine) * pltpu.roll(high, 4, 0)
        sent[slot * ROWS : slot * ROWS + 8, :] = low
        sent[slot * ROWS + 8 : slot * ROWS + 16, :] = turned
    sent[32:40, :] = table[16:24, :]


def put_edges(field, flag, lon_cells, edge_a, edge_b):
    first = field[0 : 2 * ROWS, :]
    last = field[(lon_cells - 2) * ROWS : lon_cells * ROWS, :]
    odd = flag[0] > 0
    edge_a[...] = jnp.where(odd, first, last)
    edge_b[...] = jnp.where(odd, last, first)


def strip_of(value, col):
    return pltpu.roll(value, 4 * col + 2, 1)


def start_kernel(
    lon_cells, state, src, counts, names, weights, turn, flag,
    field, edge_a, edge_b, strips, buffer, sent, table, listed, parts, zeros, sems
):
    blocks = lon_cells // 32
    loads = []
    for block in range(blocks):
        copy = pltpu.make_async_copy(state.at[:, pl.ds(32 * block, 32), :], parts.at[block], sems.at[block])
        copy.start()
        loads.append(copy)
    zeros[...] = jnp.zeros(zeros.shape, jnp.float32)
    count = zeros.shape[0]
    clears = []
    for number in range(buffer.shape[0] // count):
        copy = pltpu.make_async_copy(zeros, buffer.at[pl.ds(number * count, count), :], sems.at[blocks + number])
        copy.start()
        clears.append(copy)
    lane = lane_ids(ROWS)
    quad = lax.shift_right_logical(lane, 2)
    for block in range(blocks):
        loads[block].wait()
        rows = parts.at[block].reshape(32 * ROWS, LANES)

        def body(col, acc, block=block, rows=rows):
            low = rows[pl.ds(col, 8, stride=32), :]
            high = rows[pl.ds(col + 8 * 32, 8, stride=32), :]
            value = jnp.concatenate([low, high], axis=0)
            field[rows_of(block * 32 + col), :] = value
            return jnp.where(quad == col, strip_of(value, col), acc)

        acc = lax.fori_loop(0, 32, body, jnp.zeros((ROWS, LANES), jnp.float32), unroll=8)
        strips[block * ROWS : (block + 1) * ROWS, :] = acc
    put_edges(field, flag, lon_cells, edge_a, edge_b)
    row = lane_ids(1)
    table[...] = jnp.zeros(table.shape, jnp.float32)
    angle = turn[...]
    cosine, sine = jnp.cos(angle), jnp.sin(angle)
    for slot in range(2):
        for corner in range(4):
            value = weights[2 * corner + slot : 2 * corner + slot + 1, :]
            table[8 * slot + corner : 8 * slot + corner + 1, :] = jnp.where(row < counts[slot], value, 0.0)
        table[8 * slot + 4 : 8 * slot + 5, :] = cosine[slot : slot + 1]
        table[8 * slot + 5 : 8 * slot + 6, :] = sine[slot : slot + 1]
        table[16 + slot : 17 + slot, :] = jnp.full((1, LANES), names[slot], jnp.int32).astype(jnp.float32)
    finish_rows(gather_all(field, src, lon_cells, listed), table, sent)
    for copy in clears:
        copy.wait()


def key_kernel(slots, keys, listed):
    lane = lane_ids(8)
    slot = slots[...]
    peer = lax.shift_right_arithmetic(slot, 7)
    shift = lax.bitwise_and(slot - lane, LANES - 1)
    key = jnp.where(slot >= 0, (peer * LANES + shift).astype(jnp.float32), NO_KEY)
    keys[...] = key

    def cond(carry):
        count, more = carry[0], carry[1]
        return jnp.logical_and(count < LANES, more > 0)

    def body(carry):
        count, _, last, found, total = carry
        now = jnp.min(jnp.where(key > last, key, NO_KEY), axis=1, keepdims=True)
        now = jnp.broadcast_to(now, (8, LANES))
        hit = now < NO_KEY
        more = (jnp.min(now) < NO_KEY).astype(jnp.int32)
        found = jnp.where(lane == count, jnp.where(hit, now, -1.0), found)
        total = total + more.astype(jnp.float32)
        return count + 1, more, now, found, total

    zero = jnp.zeros((8, LANES), jnp.float32)
    out = lax.while_loop(cond, body, (jnp.int32(0), jnp.int32(1), zero - 1.0, zero - 1.0, zero))
    listed[0:8, :] = out[3].astype(jnp.int32)
    listed[8:16, :] = out[4].astype(jnp.int32)


def fill_ghosts(received, keys, listed, ghosts):
    def body(i, accs):
        out = []
        for row in range(4):
            key = listed[row, i]
            known = jnp.maximum(key, 0)
            peer = lax.shift_right_logical(known, 7)
            shift = lax.bitwise_and(known, LANES - 1)
            value = pltpu.roll(tile(received, peer), lax.bitwise_and(LANES - shift, LANES - 1), 1)
            out.append(jnp.where(keys[row : row + 1, :] == key.astype(jnp.float32), value, accs[row]))
        return tuple(out)

    zero = jnp.zeros((ROWS, LANES), jnp.float32)
    accs = lax.fori_loop(0, listed[8, 0], body, (zero, zero, zero, zero))
    for row in range(4):
        ghosts[row * ROWS : (row + 1) * ROWS, :] = accs[row]


def merge_strips(strip_a, strip_b, flag, ghosts, merged, blocks):
    lane = lane_ids(8)
    part = lax.bitwise_and(lane, 3)
    odd = flag[1] > 0
    north = flag[2] > 0
    first = part == jnp.where(north, 1, 2)
    second = part == jnp.where(north, 0, 3)
    for block in range(blocks):
        spread = lax.shift_right_logical(lane, 2) + 32 * block
        for half in range(2):
            at = block * ROWS + half * 8
            a = strip_a[at : at + 8, :]
            b = strip_b[at : at + 8, :]
            value = jnp.where(part < 2, jnp.where(odd, a, b), jnp.where(odd, b, a))
            wide0 = jnp.take_along_axis(ghosts[half * 8 : half * 8 + 8, :], spread, axis=1)
            wide1 = jnp.take_along_axis(ghosts[ROWS + half * 8 : ROWS + half * 8 + 8, :], spread, axis=1)
            merged[at : at + 8, :] = value + jnp.where(first, wide0, jnp.where(second, wide1, 0.0))


def coefficients(sin_t, cos_t, yang, consts):
    d_theta, d_phi, step, kappa, viscous, omega, buoyancy, radial = consts
    sub = sub_ids()
    low = sub < 4
    level = lax.bitwise_and(sub, 3).astype(jnp.float32)
    inverse = 1.0 / (level * radial + R_LOW)
    keep = 1.0 - yang
    over_sin = 1.0 / sin_t
    square = inverse * inverse
    advect_t = -step / (12.0 * d_theta) * inverse
    advect_p = -step / (12.0 * d_phi) * inverse * over_sin
    values = [advect_t, advect_p]
    for half in range(2):
        spread = jnp.where(low, step * kappa, step * viscous) if half == 0 else jnp.full((8, LANES), step * viscous)
        second_t = spread * square / (12.0 * d_theta * d_theta)
        first_t = spread * square * (cos_t * over_sin) / (12.0 * d_theta)
        second_p = spread * square * (over_sin * over_sin) / (12.0 * d_phi * d_phi)
        second_r = spread / (radial * radial)
        first_r = spread * inverse / radial
        middle = -30.0 * second_t - 30.0 * second_p - 2.0 * second_r
        values += [second_t, first_t, second_p, second_r, first_r, middle]
    twice = 2.0 * step * omega
    zero = jnp.zeros((8, LANES), jnp.float32)
    sign = jnp.where(low, 1.0, -1.0)
    values += [
        jnp.where(low, 0.0, step * buoyancy),
        jnp.where(low, zero, twice * keep * sin_t),
        jnp.where(low, zero, -twice * cos_t),
        jnp.where(low, 0.0, twice) + zero,
        sign * twice * keep * cos_t,
        sign * twice * sin_t,
        jnp.where(low, zero, -twice * keep * sin_t),
        jnp.where(low, zero, twice * cos_t),
        jnp.where(low, -twice, 0.0) + zero,
    ]
    return values


def inner_kernel(second, lon_cells, consts, *refs):
    refs = list(refs)
    field = refs.pop(0)
    origin = refs.pop(0) if second else None
    geo, result, strips, coef = refs
    base = 2 * lon_cells
    sin_t, cos_t, yang = (geo[base + 8 * i : base + 8 * i + 8, :] for i in range(3))
    for i, value in enumerate(coefficients(sin_t, cos_t, yang, consts)):
        coef[8 * i : 8 * i + 8, :] = value
    radial = consts[7]
    lane16 = lane_ids(ROWS)
    quad = lax.shift_right_logical(lane16, 2)
    sub = sub_ids()
    low = sub < 4
    level = lax.bitwise_and(sub, 3)
    top = level == 3
    bottom = level == 0
    advect_r = -consts[2] / (2.0 * radial)

    def c(i):
        return coef[8 * i : 8 * i + 8, :]

    def update(u, down2, down1, here, up1, up2):
        south1 = jnp.where(lane16 >= 1, pltpu.roll(here, 1, 1), 0.0)
        south2 = jnp.where(lane16 >= 2, pltpu.roll(here, 2, 1), 0.0)
        north1 = jnp.where(lane16 < LANES - 1, pltpu.roll(here, LANES - 1, 1), 0.0)
        north2 = jnp.where(lane16 < LANES - 2, pltpu.roll(here, LANES - 2, 1), 0.0)
        lat_odd = 8.0 * (north1 - south1) - (north2 - south2)
        lat_even = 16.0 * (north1 + south1) - (north2 + south2)
        lon_odd = 8.0 * (up1 - down1) - (up2 - down2)
        lon_even = 16.0 * (up1 + down1) - (up2 + down2)
        v0, v1 = here[:8], here[8:]
        r0, r1 = pltpu.roll(v0, 4, 0), pltpu.roll(v1, 4, 0)
        vel_r = jnp.where(low, r0, v0)
        vel_t = jnp.where(low, v1, r1)
        vel_p = jnp.where(low, r1, v1)
        along_t = vel_t * c(0)
        along_p = vel_p * c(1)
        along_r = vel_r * advect_r
        sin_p = geo[pl.ds(u, 1), :]
        cos_p = geo[pl.ds(lon_cells + u, 1), :]
        turn0 = c(14) * r0 + (c(15) + c(16) * sin_p) * vel_p + (c(17) * cos_p) * vel_t
        turn1 = (c(18) + c(19) * sin_p) * r1 + (c(20) + c(21) * sin_p + c(22) * cos_p) * vel_r
        out = []
        for half, value, turn in ((0, v0, turn0), (1, v1, turn1)):
            at = 2 + 6 * half
            part = slice(8 * half, 8 * half + 8)
            above = jnp.where(top, value, pltpu.roll(value, 7, 0))
            below = jnp.where(bottom, value, pltpu.roll(value, 1, 0))
            change = (
                (c(at + 1) + along_t) * lat_odd[part]
                + c(at) * lat_even[part]
                + along_p * lon_odd[part]
                + c(at + 2) * lon_even[part]
                + (c(at + 4) + along_r) * (above - below)
                + c(at + 3) * (above + below)
                + c(at + 5) * value
                + turn
            )
            out.append(value + change)
        new = jnp.concatenate(out, axis=0)
        if second:
            new = 0.5 * (tile(origin, u) + new)
        return new

    def at(u):
        if u < 0 or u >= lon_cells:
            return jnp.zeros((ROWS, LANES), jnp.float32)
        return tile(field, u)

    def group(index, block, col, tiles):
        acc = jnp.zeros((ROWS, LANES), jnp.float32)
        for k in range(GROUP):
            new = update(index + k, *tiles[k : k + 5])
            result[rows_of(index + k), :] = new
            acc = jnp.where(quad == col + k, strip_of(new, col + k), acc)
        rows = rows_of(block)
        mine = jnp.logical_and(quad >= col, quad < col + GROUP)
        strips[rows, :] = jnp.where(mine, acc, strips[rows, :])

    strips[...] = jnp.zeros(strips.shape, jnp.float32)
    for index in (0, lon_cells - GROUP):
        group(index, index // 32, index % 32, [at(u) for u in range(index - 2, index + GROUP + 2)])

    def body(number, carry):
        index = number * GROUP
        tiles = [tile(field, index + k) for k in range(-2, GROUP + 2)]
        group(index, lax.shift_right_logical(index, 5), lax.bitwise_and(index, 31), tiles)
        return carry

    lax.fori_loop(1, lon_cells // GROUP - 1, body, 0)


def rows_kernel(field, src, corners):
    for i, value in enumerate(gather_all(field, src)):
        corners[2 * i * ROWS : 2 * (i + 1) * ROWS, :] = value


def outer_kernel(second, final, lon_cells, consts, *refs):
    refs = list(refs)
    part, part_strips, own_a, own_b, own_strips, lon_a, lon_b, strip_a, strip_b, received, keys, listed, flag, geo = refs[:14]
    refs = refs[14:]
    if final:
        result = refs.pop(0)
    else:
        corners, again, src, table, result, sent, edge_a, edge_b, strips = refs[:9]
        refs = refs[9:]
    ghosts, merged, fixes, sides = refs
    blocks = lon_cells // 32
    fill_ghosts(received, keys, listed, ghosts)
    merge_strips(strip_a, strip_b, flag, ghosts, merged, blocks)

    base = 2 * lon_cells
    sin_t, cos_t, yang, strip_sin, strip_cos = (geo[base + 8 * i : base + 8 * i + 8, :] for i in range(5))
    low = sub_ids() < 4
    lane = lane_ids(8)
    scale = 0.5 if second else 1.0

    values = coefficients(strip_sin, strip_cos, yang, consts)
    quarter = lax.bitwise_and(lane, 3)
    for block in range(blocks):
        at = block * ROWS
        v1 = own_strips[at + 8 : at + 16, :]
        along = jnp.where(low, v1, pltpu.roll(v1, 4, 0)) * values[0]
        for half in range(2):
            rows = slice(at + 8 * half, at + 8 * half + 8)
            outside = merged[rows, :]
            left1, left2 = pltpu.roll(outside, LANES - 1, 1), pltpu.roll(outside, LANES - 2, 1)
            right1, right2 = pltpu.roll(outside, 1, 1), pltpu.roll(outside, 2, 1)
            near = jnp.where(quarter == 1, left1, jnp.where(quarter == 2, right1, 0.0))
            far = jnp.where(quarter < 2, left2, right2)
            first = jnp.where(quarter < 2, 8.0 * near - far, far - 8.0 * near)
            twice = 16.0 * near - far
            fixes[rows, :] = scale * ((values[3 + 6 * half] + along) * first + values[2 + 6 * half] * twice)

    values = coefficients(sin_t, cos_t, yang, consts)
    odd = flag[0] > 0
    west = flag[3] > 0
    for i, row in enumerate((3, 2, 2, 3)):
        came = jnp.where(odd, lon_a[...], lon_b[...]) if i < 2 else jnp.where(odd, lon_b[...], lon_a[...])
        ghost = jnp.where(west if i < 2 else jnp.logical_not(west), ghosts[rows_of(row), :], 0.0)
        sides[rows_of(i), :] = came[rows_of(i % 2)] + ghost
    before2, before1, after1, after2 = (sides[rows_of(i), :] for i in range(4))
    for i, (near, far, sign) in enumerate(
        ((before1, before2, -1.0), (None, before1, -1.0), (None, after1, 1.0), (after1, after2, 1.0))
    ):
        own = jnp.where(odd, own_a[...], own_b[...]) if i < 2 else jnp.where(odd, own_b[...], own_a[...])
        v1 = own[rows_of(i % 2)][8:]
        along = jnp.where(low, pltpu.roll(v1, 4, 0), v1) * values[1]
        first = -far if near is None else 8.0 * near - far
        twice = -far if near is None else 16.0 * near - far
        for half in range(2):
            rows = slice(8 * half, 8 * half + 8)
            change = sign * along * first[rows] + values[4 + 6 * half] * twice[rows]
            sides[i * ROWS + 8 * half : i * ROWS + 8 * half + 8, :] = scale * change

    lane16 = lane_ids(ROWS)
    rim = jnp.logical_or(lane16 < 2, lane16 >= LANES - 2)

    def corrected(u, block, col):
        moved = pltpu.roll(tile(fixes, block), lax.bitwise_and(LANES - 2 - 4 * col, LANES - 1), 1)
        return tile(part, u) + jnp.where(rim, moved, 0.0)

    def store(u, new):
        if final:
            result[pl.ds(u, 8, stride=lon_cells), :] = new[:8]
            result[pl.ds(u + 8 * lon_cells, 8, stride=lon_cells), :] = new[8:]
        else:
            result[rows_of(u), :] = new

    def body(number, carry):
        index = number * GROUP
        block = lax.shift_right_logical(index, 5)
        col = lax.bitwise_and(index, 31)
        for new, k in [(corrected(index + k, block, col + k), k) for k in range(GROUP)]:
            store(index + k, new)
        return carry

    lax.fori_loop(0, lon_cells // GROUP, body, 0)
    if not final:
        strips[...] = part_strips[...] + fixes[...]
    quad = lax.shift_right_logical(lane16, 2)
    for i, u in enumerate((0, 1, lon_cells - 2, lon_cells - 1)):
        block, col = divmod(u, 32)
        change = sides[rows_of(i), :]
        store(u, corrected(u, block, col) + change)
        if not final:
            strips[rows_of(block), :] += jnp.where(quad == col, strip_of(change, col), 0.0)
    if final:
        return
    put_edges(result, flag, lon_cells, edge_a, edge_b)

    def repeat(step, accs):
        for k in range(4):
            at = again[4 * step + k]
            accs = pick(result, src, at, lax.bitwise_and(at, LANES - 1), lax.shift_right_logical(at, 7), accs)
        return accs

    accs = tuple(corners[2 * i * ROWS : 2 * (i + 1) * ROWS, :] for i in range(4))
    steps = lax.shift_right_logical(again[again.shape[0] - 1] + 3, 2)
    finish_rows(lax.fori_loop(0, steps, repeat, accs), table, sent)


def pack_kernel(message_a, message_b, flag, _, buffer, staged, sems):
    core = flag[0]
    copies = []
    for number, (message, own) in enumerate(((message_a, core), (message_b, 1 - core))):
        target0 = jnp.max(message[32:33, :]).astype(jnp.int32)
        target1 = jnp.max(message[33:34, :]).astype(jnp.int32)
        same = target0 == target1
        slot0, slot1 = message[0:ROWS, :], message[ROWS : 2 * ROWS, :]
        staged[2 * number * ROWS : (2 * number + 1) * ROWS, :] = jnp.where(same, slot0 + slot1, slot0)
        staged[(2 * number + 1) * ROWS : (2 * number + 2) * ROWS, :] = slot1
        for slot, target in ((0, target0), (1, target1)):
            wanted = lax.bitwise_and(target, 1) == core
            if slot == 1:
                wanted = jnp.logical_and(wanted, jnp.logical_not(same))
            place = pl.multiple_of((target - core + own) * ROWS, ROWS)
            at = 2 * number + slot
            copy = pltpu.make_async_copy(
                staged.at[pl.ds(at * ROWS, ROWS), :], buffer.at[pl.ds(place, ROWS), :], sems.at[at]
            )
            copies.append((wanted, copy))
    for wanted, copy in copies:
        pl.when(wanted)(copy.start)
    for wanted, copy in copies:
        pl.when(wanted)(copy.wait)


def pairs(count, first):
    route = []
    for low in range(first, count - 1, 2):
        route += [(low, low + 1), (low + 1, low)]
    return route


def on_device(state, partners, send_counts, source_cells, weights, turn_angles, ghost_slots):
    lat_blocks = lax.axis_size("colat")
    lon_axes = ("lon_hi", "core")
    lon_blocks = lax.axis_size(lon_axes)
    peers = lat_blocks * lon_blocks
    lon_cells, lat_cells = state.shape[3], state.shape[4]
    consts = constants(lat_cells * lat_blocks, lon_cells * lon_blocks)
    core = lax.axis_index("core")
    colat = lax.axis_index("colat")
    lon = lax.axis_index(lon_axes)
    yang = lax.axis_index("panel").astype(jnp.float32)
    flag = jnp.stack([lon % 2, colat % 2, colat == 0, lon == 0]).astype(jnp.int32)

    src = source_cells[0, 0, 0]
    theta = ((colat * lat_cells + jnp.arange(lat_cells, dtype=jnp.int32)).astype(jnp.float32) + 0.5) * consts[0] + 0.25 * math.pi
    rim_lat = (jnp.arange(LANES, dtype=jnp.int32) + 2) % 4 + jnp.where(jnp.arange(LANES, dtype=jnp.int32) % 4 < 2, lat_cells - 4, 0)
    rim_theta = ((colat * lat_cells + rim_lat).astype(jnp.float32) + 0.5) * consts[0] + 0.25 * math.pi
    phi = ((lon * lon_cells + jnp.arange(lon_cells, dtype=jnp.int32)).astype(jnp.float32) + 0.5) * consts[1] - 0.75 * math.pi
    geo = jnp.concatenate(
        [
            jnp.broadcast_to((yang * jnp.sin(phi))[:, None], (lon_cells, LANES)),
            jnp.broadcast_to((yang * jnp.cos(phi))[:, None], (lon_cells, LANES)),
            jnp.broadcast_to(jnp.sin(theta)[None], (8, LANES)),
            jnp.broadcast_to(jnp.cos(theta)[None], (8, LANES)),
            jnp.broadcast_to(yang, (8, LANES)),
            jnp.broadcast_to(jnp.sin(rim_theta)[None], (8, LANES)),
            jnp.broadcast_to(jnp.cos(rim_theta)[None], (8, LANES)),
        ]
    )
    slot = ghost_slots[0, 0, 0]
    pole = slot[: 4 * lon_cells].reshape(2, 2, lon_cells)
    pole = jnp.pad(jnp.maximum(pole[0], pole[1]), ((0, 0), (0, LANES - lon_cells)), constant_values=-1)
    side = slot[4 * lon_cells :].reshape(2, 2, LANES)
    slots = jnp.concatenate([pole, jnp.maximum(side[0], side[1]), jnp.full((4, LANES), -1, jnp.int32)])

    vmem = pl.BlockSpec(memory_space=pltpu.VMEM)
    smem = pl.BlockSpec(memory_space=pltpu.SMEM)

    def f32(*shape):
        return jax.ShapeDtypeStruct(shape, jnp.float32)

    cells = lon_cells * ROWS
    strip_rows = lon_cells // 32 * ROWS
    moving = [f32(cells, LANES), f32(40, LANES), f32(32, LANES), f32(32, LANES), f32(strip_rows, LANES)]
    params = pltpu.CompilerParams(vmem_limit_bytes=16 * 1024 * 1024)

    keys, listed = pl.pallas_call(
        key_kernel,
        out_shape=[f32(8, LANES), jax.ShapeDtypeStruct((16, LANES), jnp.int32)],
        in_specs=[vmem],
        out_specs=[vmem, vmem],
        compiler_params=params,
    )(slots)

    hbm = pl.BlockSpec(memory_space=pltpu.HBM)
    field, edge_a, edge_b, strips, buffer, sent, table, again = pl.pallas_call(
        functools.partial(start_kernel, lon_cells),
        out_shape=[moving[0], moving[2], moving[3], moving[4], f32(peers * ROWS, LANES), moving[1], f32(24, LANES)]
        + [jax.ShapeDtypeStruct((2 * LANES + 8,), jnp.int32)],
        in_specs=[hbm, smem, smem, smem, vmem, vmem, smem],
        out_specs=[vmem] * 4 + [hbm] + [vmem] * 2 + [smem],
        scratch_shapes=[
            pltpu.VMEM((lon_cells // 32, ROWS, 32, LANES), jnp.float32),
            pltpu.VMEM((LANES, LANES), jnp.float32),
            pltpu.SemaphoreType.DMA((lon_cells // 32 + peers * ROWS // LANES,)),
        ],
        compiler_params=params,
    )(
        state.reshape(ROWS, lon_cells, LANES),
        src,
        send_counts[0, 0, 0],
        partners[0, 0, 0],
        weights.reshape(8, LANES),
        turn_angles.reshape(2, LANES),
        flag,
    )

    origin = field
    for number in range(2 * STEPS):
        second = number % 2 == 1
        final = number == 2 * STEPS - 1
        over = lax.ppermute(sent, "panel", SWAP)
        operands = [field] + ([origin] if second else []) + [geo]
        part, part_strips = pl.pallas_call(
            functools.partial(inner_kernel, second, lon_cells, consts),
            out_shape=[moving[0], moving[4]],
            in_specs=[vmem] * len(operands),
            out_specs=[vmem, vmem],
            scratch_shapes=[pltpu.VMEM((8 * 23, LANES), jnp.float32)],
            compiler_params=params,
            cost_estimate=pl.CostEstimate(flops=20_000_000, bytes_accessed=1 << 23, transcendentals=0),
        )(*operands)
        over, part, part_strips = lax.optimization_barrier((over, part, part_strips))
        mate = lax.ppermute(over, "core", SWAP)
        buffer = pl.pallas_call(
            pack_kernel,
            out_shape=f32(peers * ROWS, LANES),
            in_specs=[vmem, vmem, smem, hbm],
            out_specs=hbm,
            scratch_shapes=[pltpu.VMEM((4 * ROWS, LANES), jnp.float32), pltpu.SemaphoreType.DMA((4,))],
            input_output_aliases={3: 0},
            compiler_params=params,
        )(over, mate, flag, buffer)
        buffer, own_a, own_b, own_strips, part = lax.optimization_barrier((buffer, edge_a, edge_b, strips, part))
        received = lax.all_to_all(
            buffer.reshape(peers // 2, 2 * ROWS, LANES), ("colat", "lon_hi"), split_axis=0, concat_axis=0, tiled=True
        ).reshape(peers * ROWS, LANES)
        if not final:
            corners = pl.pallas_call(
                rows_kernel,
                out_shape=f32(8 * ROWS, LANES),
                in_specs=[vmem, smem],
                out_specs=vmem,
                compiler_params=params,
                cost_estimate=pl.CostEstimate(flops=8_000_000, bytes_accessed=1 << 22, transcendentals=0),
            )(part, src)
        lon_a = lax.ppermute(own_a, lon_axes, pairs(lon_blocks, 0))
        lon_b = lax.ppermute(own_b, lon_axes, pairs(lon_blocks, 1))
        strip_a = lax.ppermute(own_strips, "colat", pairs(lat_blocks, 0))
        strip_b = lax.ppermute(own_strips, "colat", pairs(lat_blocks, 1))
        operands = [part, part_strips, own_a, own_b, own_strips, lon_a, lon_b, strip_a, strip_b, received, keys, listed, flag, geo]
        specs = [vmem] * 11 + [smem, smem, vmem]
        if not final:
            operands += [corners, again, src, table]
            specs += [vmem, smem, smem, vmem]
        out = pl.pallas_call(
            functools.partial(outer_kernel, second, final, lon_cells, consts),
            out_shape=moving[:1] if final else moving,
            in_specs=specs,
            out_specs=[vmem] * (1 if final else 5),
            scratch_shapes=[
                pltpu.VMEM((4 * ROWS, LANES), jnp.float32),
                pltpu.VMEM((strip_rows, LANES), jnp.float32),
                pltpu.VMEM((strip_rows, LANES), jnp.float32),
                pltpu.VMEM((4 * ROWS, LANES), jnp.float32),
            ],
            compiler_params=params,
        )(*operands)
        if final:
            return out[0].reshape(state.shape)
        field, sent, edge_a, edge_b, strips = out
        if second:
            origin = field


def solution(mesh):
    lon = mesh.shape["lon"]
    fine = Mesh(
        mesh.devices.reshape(mesh.shape["panel"], mesh.shape["colat"], lon // 2, 2), ("panel", "colat", "lon_hi", "core")
    )
    lon_axes = ("lon_hi", "core")
    table = P("panel", "colat", lon_axes, None)
    in_specs = (
        P(None, "panel", None, lon_axes, "colat"),
        table,
        table,
        table,
        P(None, "panel", "colat", lon_axes, None),
        table,
        table,
    )
    out_specs = P(None, "panel", None, lon_axes, "colat")
    return jax.shard_map(on_device, mesh=fine, in_specs=in_specs, out_specs=out_specs, check_vma=False)
```

```python
import functools
import math

import jax
import jax.numpy as jnp
import numpy as np
from jax import lax
from jax.experimental import pallas as pl
from jax.experimental.pallas import tpu as pltpu
from jax.sharding import Mesh, PartitionSpec as P

STEPS = 2
R_LOW = 0.7
HALF_ROOT = 0.7071067811865476
LANES = 128
ROWS = 16
NO_KEY = 1.0e9
AGAIN = 8
GROUP = 8
CROSS = [(0, 3), (3, 0), (1, 2), (2, 1)]


def constants(lat_total, lon_total):
    d_theta = 0.5 * math.pi / lat_total
    d_phi = 1.5 * math.pi / lon_total
    spacing = R_LOW * min(d_theta, HALF_ROOT * d_phi)
    time_step = 0.25 * spacing
    kappa = 0.04 * spacing * spacing / time_step
    viscous = 0.06 * spacing * spacing / time_step
    return (
        d_theta,
        d_phi,
        time_step,
        kappa,
        viscous,
        0.05 / time_step,
        0.2 / time_step,
        4.0 * spacing,
    )


def lane_ids(rows):
    return lax.broadcasted_iota(jnp.int32, (rows, LANES), 1)


def sub_ids():
    return lax.broadcasted_iota(jnp.int32, (8, LANES), 0)


def rows_of(u):
    if isinstance(u, int):
        return slice(u * ROWS, (u + 1) * ROWS)
    return pl.ds(pl.multiple_of(u * ROWS, ROWS), ROWS)


def tile(ref, u):
    return ref[rows_of(u), :]


def pick(field, src, at, m, slot, accs):
    lane = lane_ids(8)
    cell = src[at]
    lon = lax.shift_right_logical(cell, 7)
    lat = lax.bitwise_and(cell, LANES - 1)
    both = field[pl.ds(pl.multiple_of(lon * ROWS, ROWS), 2 * ROWS), :]
    near = pltpu.roll(both, lax.bitwise_and(m - lat + LANES, LANES - 1), 1)
    accs = list(accs)
    if isinstance(slot, int):
        columns = [(2 * slot, near, lane == m), (2 * slot + 1, near, lane == lax.bitwise_and(m + 1, LANES - 1))]
    else:
        far = pltpu.roll(both, lax.bitwise_and(m - lat + LANES - 1, LANES - 1), 1)
        columns = []
        for number in range(2):
            mask = lane == jnp.where(slot == number, m, 2 * LANES)
            columns += [(2 * number, near, mask), (2 * number + 1, far, mask)]
    for number, column, mask in columns:
        old = accs[number]
        rows = [jnp.where(mask, column[8 * i : 8 * i + 8], old[8 * i : 8 * i + 8]) for i in range(4)]
        accs[number] = jnp.concatenate(rows, axis=0)
    return tuple(accs)


def gather_all(field, src, lon_cells=0, listed=None):
    def note(at, count):
        if listed is None:
            return count
        cell = src[at]
        lon = lax.shift_right_logical(cell, 7)
        lat = lax.bitwise_and(cell, LANES - 1)
        low = jnp.logical_or(lat < 2, lon < 2)
        high = jnp.logical_or(lat >= LANES - 3, lon >= lon_cells - 3)
        listed[count] = at
        return count + jnp.logical_or(low, high).astype(jnp.int32)

    def body(m, carry):
        count, accs = carry
        accs = pick(field, src, m, m, 0, accs)
        count = note(m, count)
        accs = pick(field, src, LANES + m, m, 1, accs)
        count = note(LANES + m, count)
        return count, accs

    zero = jnp.zeros((2 * ROWS, LANES), jnp.float32)
    count, accs = lax.fori_loop(0, LANES, body, (jnp.int32(0), (zero, zero, zero, zero)), unroll=32)
    if listed is not None:
        for k in range(AGAIN):
            listed[count + k] = 0
        listed[listed.shape[0] - 1] = count
    near0, far0, near1, far1 = accs
    return near0, pltpu.roll(far0, LANES - 1, 1), near1, pltpu.roll(far1, LANES - 1, 1)


def finish_rows(accs, table, sent):
    sub = sub_ids()
    for slot in range(2):
        near, far = accs[2 * slot], accs[2 * slot + 1]
        base = slot * 8
        w0 = table[base : base + 1, :]
        w1 = table[base + 1 : base + 2, :]
        w2 = table[base + 2 : base + 3, :]
        w3 = table[base + 3 : base + 4, :]
        value = w0 * near[:ROWS] + w1 * far[:ROWS] + w2 * near[ROWS:] + w3 * far[ROWS:]
        low, high = value[:8], value[8:]
        cosine = table[base + 4 : base + 5, :]
        sine = table[base + 5 : base + 6, :]
        turned = cosine * high + jnp.where(sub < 4, sine, -sine) * pltpu.roll(high, 4, 0)
        sent[slot * ROWS : slot * ROWS + 8, :] = low
        sent[slot * ROWS + 8 : slot * ROWS + 16, :] = turned
    sent[32:40, :] = table[16:24, :]


def put_edges(field, flag, lon_cells, edge_a, edge_b):
    first = field[0 : 2 * ROWS, :]
    last = field[(lon_cells - 2) * ROWS : lon_cells * ROWS, :]
    odd = flag[0] > 0
    edge_a[...] = jnp.where(odd, first, last)
    edge_b[...] = jnp.where(odd, last, first)


def strip_of(value, col):
    return pltpu.roll(value, 4 * col + 2, 1)


def start_kernel(
    lon_cells, state, src, counts, names, weights, turn, flag,
    field, edge_a, edge_b, strips, buffer, sent, table, listed, parts, zeros, sems
):
    blocks = lon_cells // 32
    loads = []
    for block in range(blocks):
        copy = pltpu.make_async_copy(state.at[:, pl.ds(32 * block, 32), :], parts.at[block], sems.at[block])
        copy.start()
        loads.append(copy)
    zeros[...] = jnp.zeros(zeros.shape, jnp.float32)
    count = zeros.shape[0]
    clears = []
    for number in range(buffer.shape[0] // count):
        copy = pltpu.make_async_copy(zeros, buffer.at[pl.ds(number * count, count), :], sems.at[blocks + number])
        copy.start()
        clears.append(copy)
    lane = lane_ids(ROWS)
    quad = lax.shift_right_logical(lane, 2)
    for block in range(blocks):
        loads[block].wait()
        rows = parts.at[block].reshape(32 * ROWS, LANES)

        def body(col, acc, block=block, rows=rows):
            low = rows[pl.ds(col, 8, stride=32), :]
            high = rows[pl.ds(col + 8 * 32, 8, stride=32), :]
            value = jnp.concatenate([low, high], axis=0)
            field[rows_of(block * 32 + col), :] = value
            return jnp.where(quad == col, strip_of(value, col), acc)

        acc = lax.fori_loop(0, 32, body, jnp.zeros((ROWS, LANES), jnp.float32), unroll=8)
        strips[block * ROWS : (block + 1) * ROWS, :] = acc
    put_edges(field, flag, lon_cells, edge_a, edge_b)
    row = lane_ids(1)
    table[...] = jnp.zeros(table.shape, jnp.float32)
    angle = turn[...]
    cosine, sine = jnp.cos(angle), jnp.sin(angle)
    for slot in range(2):
        for corner in range(4):
            value = weights[2 * corner + slot : 2 * corner + slot + 1, :]
            table[8 * slot + corner : 8 * slot + corner + 1, :] = jnp.where(row < counts[slot], value, 0.0)
        table[8 * slot + 4 : 8 * slot + 5, :] = cosine[slot : slot + 1]
        table[8 * slot + 5 : 8 * slot + 6, :] = sine[slot : slot + 1]
        table[16 + slot : 17 + slot, :] = jnp.full((1, LANES), names[slot], jnp.int32).astype(jnp.float32)
    finish_rows(gather_all(field, src, lon_cells, listed), table, sent)
    for copy in clears:
        copy.wait()


def key_kernel(slots, keys, listed):
    lane = lane_ids(8)
    slot = slots[...]
    peer = lax.bitwise_xor(lax.shift_right_arithmetic(slot, 7), 1)
    shift = lax.bitwise_and(slot - lane, LANES - 1)
    key = jnp.where(slot >= 0, (peer * LANES + shift).astype(jnp.float32), NO_KEY)
    keys[...] = key

    def cond(carry):
        count, more = carry[0], carry[1]
        return jnp.logical_and(count < LANES, more > 0)

    def body(carry):
        count, _, last, found, total = carry
        now = jnp.min(jnp.where(key > last, key, NO_KEY), axis=1, keepdims=True)
        now = jnp.broadcast_to(now, (8, LANES))
        hit = now < NO_KEY
        more = (jnp.min(now) < NO_KEY).astype(jnp.int32)
        found = jnp.where(lane == count, jnp.where(hit, now, -1.0), found)
        total = total + more.astype(jnp.float32)
        return count + 1, more, now, found, total

    zero = jnp.zeros((8, LANES), jnp.float32)
    out = lax.while_loop(cond, body, (jnp.int32(0), jnp.int32(1), zero - 1.0, zero - 1.0, zero))
    listed[0:8, :] = out[3].astype(jnp.int32)
    listed[8:16, :] = out[4].astype(jnp.int32)


def fill_ghosts(received, keys, listed, ghosts):
    def body(i, accs):
        out = []
        for row in range(4):
            key = listed[row, i]
            known = jnp.maximum(key, 0)
            peer = lax.shift_right_logical(known, 7)
            shift = lax.bitwise_and(known, LANES - 1)
            value = pltpu.roll(tile(received, peer), lax.bitwise_and(LANES - shift, LANES - 1), 1)
            out.append(jnp.where(keys[row : row + 1, :] == key.astype(jnp.float32), value, accs[row]))
        return tuple(out)

    zero = jnp.zeros((ROWS, LANES), jnp.float32)
    accs = lax.fori_loop(0, listed[8, 0], body, (zero, zero, zero, zero))
    for row in range(4):
        ghosts[row * ROWS : (row + 1) * ROWS, :] = accs[row]


def merge_strips(strip_a, strip_b, flag, ghosts, merged, blocks):
    lane = lane_ids(8)
    part = lax.bitwise_and(lane, 3)
    odd = flag[1] > 0
    north = flag[2] > 0
    first = part == jnp.where(north, 1, 2)
    second = part == jnp.where(north, 0, 3)
    for block in range(blocks):
        spread = lax.shift_right_logical(lane, 2) + 32 * block
        for half in range(2):
            at = block * ROWS + half * 8
            a = strip_a[at : at + 8, :]
            b = strip_b[at : at + 8, :]
            value = jnp.where(part < 2, jnp.where(odd, a, b), jnp.where(odd, b, a))
            wide0 = jnp.take_along_axis(ghosts[half * 8 : half * 8 + 8, :], spread, axis=1)
            wide1 = jnp.take_along_axis(ghosts[ROWS + half * 8 : ROWS + half * 8 + 8, :], spread, axis=1)
            merged[at : at + 8, :] = value + jnp.where(first, wide0, jnp.where(second, wide1, 0.0))


def coefficients(sin_t, cos_t, yang, consts):
    d_theta, d_phi, step, kappa, viscous, omega, buoyancy, radial = consts
    sub = sub_ids()
    low = sub < 4
    level = lax.bitwise_and(sub, 3).astype(jnp.float32)
    inverse = 1.0 / (level * radial + R_LOW)
    keep = 1.0 - yang
    over_sin = 1.0 / sin_t
    square = inverse * inverse
    advect_t = -step / (12.0 * d_theta) * inverse
    advect_p = -step / (12.0 * d_phi) * inverse * over_sin
    values = [advect_t, advect_p]
    for half in range(2):
        spread = jnp.where(low, step * kappa, step * viscous) if half == 0 else jnp.full((8, LANES), step * viscous)
        second_t = spread * square / (12.0 * d_theta * d_theta)
        first_t = spread * square * (cos_t * over_sin) / (12.0 * d_theta)
        second_p = spread * square * (over_sin * over_sin) / (12.0 * d_phi * d_phi)
        second_r = spread / (radial * radial)
        first_r = spread * inverse / radial
        middle = -30.0 * second_t - 30.0 * second_p - 2.0 * second_r
        values += [second_t, first_t, second_p, second_r, first_r, middle]
    twice = 2.0 * step * omega
    zero = jnp.zeros((8, LANES), jnp.float32)
    sign = jnp.where(low, 1.0, -1.0)
    values += [
        jnp.where(low, 0.0, step * buoyancy),
        jnp.where(low, zero, twice * keep * sin_t),
        jnp.where(low, zero, -twice * cos_t),
        jnp.where(low, 0.0, twice) + zero,
        sign * twice * keep * cos_t,
        sign * twice * sin_t,
        jnp.where(low, zero, -twice * keep * sin_t),
        jnp.where(low, zero, twice * cos_t),
        jnp.where(low, -twice, 0.0) + zero,
    ]
    return values


def inner_kernel(second, lon_cells, consts, *refs):
    refs = list(refs)
    field = refs.pop(0)
    origin = refs.pop(0) if second else None
    geo, result, strips, coef = refs
    base = 2 * lon_cells
    sin_t, cos_t, yang = (geo[base + 8 * i : base + 8 * i + 8, :] for i in range(3))
    for i, value in enumerate(coefficients(sin_t, cos_t, yang, consts)):
        coef[8 * i : 8 * i + 8, :] = value
    radial = consts[7]
    lane16 = lane_ids(ROWS)
    quad = lax.shift_right_logical(lane16, 2)
    sub = sub_ids()
    low = sub < 4
    level = lax.bitwise_and(sub, 3)
    top = level == 3
    bottom = level == 0
    advect_r = -consts[2] / (2.0 * radial)

    def c(i):
        return coef[8 * i : 8 * i + 8, :]

    def update(u, down2, down1, here, up1, up2):
        south1 = jnp.where(lane16 >= 1, pltpu.roll(here, 1, 1), 0.0)
        south2 = jnp.where(lane16 >= 2, pltpu.roll(here, 2, 1), 0.0)
        north1 = jnp.where(lane16 < LANES - 1, pltpu.roll(here, LANES - 1, 1), 0.0)
        north2 = jnp.where(lane16 < LANES - 2, pltpu.roll(here, LANES - 2, 1), 0.0)
        lat_odd = 8.0 * (north1 - south1) - (north2 - south2)
        lat_even = 16.0 * (north1 + south1) - (north2 + south2)
        lon_odd = 8.0 * (up1 - down1) - (up2 - down2)
        lon_even = 16.0 * (up1 + down1) - (up2 + down2)
        v0, v1 = here[:8], here[8:]
        r0, r1 = pltpu.roll(v0, 4, 0), pltpu.roll(v1, 4, 0)
        vel_r = jnp.where(low, r0, v0)
        vel_t = jnp.where(low, v1, r1)
        vel_p = jnp.where(low, r1, v1)
        along_t = vel_t * c(0)
        along_p = vel_p * c(1)
        along_r = vel_r * advect_r
        sin_p = geo[pl.ds(u, 1), :]
        cos_p = geo[pl.ds(lon_cells + u, 1), :]
        turn0 = c(14) * r0 + (c(15) + c(16) * sin_p) * vel_p + (c(17) * cos_p) * vel_t
        turn1 = (c(18) + c(19) * sin_p) * r1 + (c(20) + c(21) * sin_p + c(22) * cos_p) * vel_r
        out = []
        for half, value, turn in ((0, v0, turn0), (1, v1, turn1)):
            at = 2 + 6 * half
            part = slice(8 * half, 8 * half + 8)
            above = jnp.where(top, value, pltpu.roll(value, 7, 0))
            below = jnp.where(bottom, value, pltpu.roll(value, 1, 0))
            change = (
                (c(at + 1) + along_t) * lat_odd[part]
                + c(at) * lat_even[part]
                + along_p * lon_odd[part]
                + c(at + 2) * lon_even[part]
                + (c(at + 4) + along_r) * (above - below)
                + c(at + 3) * (above + below)
                + c(at + 5) * value
                + turn
            )
            out.append(value + change)
        new = jnp.concatenate(out, axis=0)
        if second:
            new = 0.5 * (tile(origin, u) + new)
        return new

    def at(u):
        if u < 0 or u >= lon_cells:
            return jnp.zeros((ROWS, LANES), jnp.float32)
        return tile(field, u)

    def group(index, block, col, tiles):
        acc = jnp.zeros((ROWS, LANES), jnp.float32)
        for k in range(GROUP):
            new = update(index + k, *tiles[k : k + 5])
            result[rows_of(index + k), :] = new
            acc = jnp.where(quad == col + k, strip_of(new, col + k), acc)
        rows = rows_of(block)
        mine = jnp.logical_and(quad >= col, quad < col + GROUP)
        strips[rows, :] = jnp.where(mine, acc, strips[rows, :])

    strips[...] = jnp.zeros(strips.shape, jnp.float32)
    for index in (0, lon_cells - GROUP):
        group(index, index // 32, index % 32, [at(u) for u in range(index - 2, index + GROUP + 2)])

    def body(number, carry):
        index = number * GROUP
        tiles = [tile(field, index + k) for k in range(-2, GROUP + 2)]
        group(index, lax.shift_right_logical(index, 5), lax.bitwise_and(index, 31), tiles)
        return carry

    lax.fori_loop(1, lon_cells // GROUP - 1, body, 0)


def rows_kernel(field, src, corners):
    for i, value in enumerate(gather_all(field, src)):
        corners[2 * i * ROWS : 2 * (i + 1) * ROWS, :] = value


def outer_kernel(second, final, lon_cells, consts, *refs):
    refs = list(refs)
    part, part_strips, own_a, own_b, own_strips, lon_a, lon_b, strip_a, strip_b, received, keys, listed, flag, geo = refs[:14]
    refs = refs[14:]
    if final:
        result = refs.pop(0)
    else:
        corners, again, src, table, result, sent, edge_a, edge_b, strips = refs[:9]
        refs = refs[9:]
    ghosts, merged, fixes, sides = refs
    blocks = lon_cells // 32
    fill_ghosts(received, keys, listed, ghosts)
    merge_strips(strip_a, strip_b, flag, ghosts, merged, blocks)

    base = 2 * lon_cells
    sin_t, cos_t, yang, strip_sin, strip_cos = (geo[base + 8 * i : base + 8 * i + 8, :] for i in range(5))
    low = sub_ids() < 4
    lane = lane_ids(8)
    scale = 0.5 if second else 1.0

    values = coefficients(strip_sin, strip_cos, yang, consts)
    quarter = lax.bitwise_and(lane, 3)
    for block in range(blocks):
        at = block * ROWS
        v1 = own_strips[at + 8 : at + 16, :]
        along = jnp.where(low, v1, pltpu.roll(v1, 4, 0)) * values[0]
        for half in range(2):
            rows = slice(at + 8 * half, at + 8 * half + 8)
            outside = merged[rows, :]
            left1, left2 = pltpu.roll(outside, LANES - 1, 1), pltpu.roll(outside, LANES - 2, 1)
            right1, right2 = pltpu.roll(outside, 1, 1), pltpu.roll(outside, 2, 1)
            near = jnp.where(quarter == 1, left1, jnp.where(quarter == 2, right1, 0.0))
            far = jnp.where(quarter < 2, left2, right2)
            first = jnp.where(quarter < 2, 8.0 * near - far, far - 8.0 * near)
            twice = 16.0 * near - far
            fixes[rows, :] = scale * ((values[3 + 6 * half] + along) * first + values[2 + 6 * half] * twice)

    values = coefficients(sin_t, cos_t, yang, consts)
    odd = flag[0] > 0
    west = flag[3] > 0
    for i, row in enumerate((3, 2, 2, 3)):
        came = jnp.where(odd, lon_a[...], lon_b[...]) if i < 2 else jnp.where(odd, lon_b[...], lon_a[...])
        ghost = jnp.where(west if i < 2 else jnp.logical_not(west), ghosts[rows_of(row), :], 0.0)
        sides[rows_of(i), :] = came[rows_of(i % 2)] + ghost
    before2, before1, after1, after2 = (sides[rows_of(i), :] for i in range(4))
    for i, (near, far, sign) in enumerate(
        ((before1, before2, -1.0), (None, before1, -1.0), (None, after1, 1.0), (after1, after2, 1.0))
    ):
        own = jnp.where(odd, own_a[...], own_b[...]) if i < 2 else jnp.where(odd, own_b[...], own_a[...])
        v1 = own[rows_of(i % 2)][8:]
        along = jnp.where(low, pltpu.roll(v1, 4, 0), v1) * values[1]
        first = -far if near is None else 8.0 * near - far
        twice = -far if near is None else 16.0 * near - far
        for half in range(2):
            rows = slice(8 * half, 8 * half + 8)
            change = sign * along * first[rows] + values[4 + 6 * half] * twice[rows]
            sides[i * ROWS + 8 * half : i * ROWS + 8 * half + 8, :] = scale * change

    lane16 = lane_ids(ROWS)
    rim = jnp.logical_or(lane16 < 2, lane16 >= LANES - 2)

    def corrected(u, block, col):
        moved = pltpu.roll(tile(fixes, block), lax.bitwise_and(LANES - 2 - 4 * col, LANES - 1), 1)
        return tile(part, u) + jnp.where(rim, moved, 0.0)

    def store(u, new):
        if final:
            result[pl.ds(u, 8, stride=lon_cells), :] = new[:8]
            result[pl.ds(u + 8 * lon_cells, 8, stride=lon_cells), :] = new[8:]
        else:
            result[rows_of(u), :] = new

    def body(block, carry):
        for col in range(32):
            u = block * 32 + col
            store(u, corrected(u, block, col))
        return carry

    lax.fori_loop(0, blocks, body, 0)
    if not final:
        strips[...] = part_strips[...] + fixes[...]
    quad = lax.shift_right_logical(lane16, 2)
    for i, u in enumerate((0, 1, lon_cells - 2, lon_cells - 1)):
        block, col = divmod(u, 32)
        change = sides[rows_of(i), :]
        store(u, corrected(u, block, col) + change)
        if not final:
            strips[rows_of(block), :] += jnp.where(quad == col, strip_of(change, col), 0.0)
    if final:
        return
    put_edges(result, flag, lon_cells, edge_a, edge_b)

    def repeat(step, accs):
        for k in range(AGAIN):
            at = again[AGAIN * step + k]
            accs = pick(result, src, at, lax.bitwise_and(at, LANES - 1), lax.shift_right_logical(at, 7), accs)
        return accs

    accs = tuple(corners[2 * i * ROWS : 2 * (i + 1) * ROWS, :] for i in range(4))
    steps = (again[again.shape[0] - 1] + AGAIN - 1) // AGAIN
    finish_rows(lax.fori_loop(0, steps, repeat, accs), table, sent)


def pack_kernel(message, _, buffer, staged, sems):
    target0 = jnp.max(message[32:33, :]).astype(jnp.int32)
    target1 = jnp.max(message[33:34, :]).astype(jnp.int32)
    same = target0 == target1
    slot0, slot1 = message[0:ROWS, :], message[ROWS : 2 * ROWS, :]
    staged[0:ROWS, :] = jnp.where(same, slot0 + slot1, slot0)
    staged[ROWS : 2 * ROWS, :] = slot1
    copies = [
        pltpu.make_async_copy(
            staged.at[pl.ds(at * ROWS, ROWS), :],
            buffer.at[pl.ds(pl.multiple_of(target * ROWS, ROWS), ROWS), :],
            sems.at[at],
        )
        for at, target in enumerate((target0, target1))
    ]
    copies[0].start()
    pl.when(jnp.logical_not(same))(copies[1].start)
    copies[0].wait()
    pl.when(jnp.logical_not(same))(copies[1].wait)


def pairs(count, first):
    route = []
    for low in range(first, count - 1, 2):
        route += [(low, low + 1), (low + 1, low)]
    return route


def on_device(state, partners, send_counts, source_cells, weights, turn_angles, ghost_slots):
    lat_blocks = lax.axis_size("colat")
    lon_axes = ("lon_hi", "core")
    lon_blocks = lax.axis_size(lon_axes)
    peers = lat_blocks * lon_blocks
    lon_cells, lat_cells = state.shape[3], state.shape[4]
    consts = constants(lat_cells * lat_blocks, lon_cells * lon_blocks)
    core = lax.axis_index("core")
    colat = lax.axis_index("colat")
    lon = lax.axis_index(lon_axes)
    yang = lax.axis_index("panel").astype(jnp.float32)
    flag = jnp.stack([lon % 2, colat % 2, colat == 0, lon == 0]).astype(jnp.int32)

    src = source_cells[0, 0, 0]
    theta = ((colat * lat_cells + jnp.arange(lat_cells, dtype=jnp.int32)).astype(jnp.float32) + 0.5) * consts[0] + 0.25 * math.pi
    rim_lat = (jnp.arange(LANES, dtype=jnp.int32) + 2) % 4 + jnp.where(jnp.arange(LANES, dtype=jnp.int32) % 4 < 2, lat_cells - 4, 0)
    rim_theta = ((colat * lat_cells + rim_lat).astype(jnp.float32) + 0.5) * consts[0] + 0.25 * math.pi
    phi = ((lon * lon_cells + jnp.arange(lon_cells, dtype=jnp.int32)).astype(jnp.float32) + 0.5) * consts[1] - 0.75 * math.pi
    geo = jnp.concatenate(
        [
            jnp.broadcast_to((yang * jnp.sin(phi))[:, None], (lon_cells, LANES)),
            jnp.broadcast_to((yang * jnp.cos(phi))[:, None], (lon_cells, LANES)),
            jnp.broadcast_to(jnp.sin(theta)[None], (8, LANES)),
            jnp.broadcast_to(jnp.cos(theta)[None], (8, LANES)),
            jnp.broadcast_to(yang, (8, LANES)),
            jnp.broadcast_to(jnp.sin(rim_theta)[None], (8, LANES)),
            jnp.broadcast_to(jnp.cos(rim_theta)[None], (8, LANES)),
        ]
    )
    slot = ghost_slots[0, 0, 0]
    pole = slot[: 4 * lon_cells].reshape(2, 2, lon_cells)
    pole = jnp.pad(jnp.maximum(pole[0], pole[1]), ((0, 0), (0, LANES - lon_cells)), constant_values=-1)
    side = slot[4 * lon_cells :].reshape(2, 2, LANES)
    slots = jnp.concatenate([pole, jnp.maximum(side[0], side[1]), jnp.full((4, LANES), -1, jnp.int32)])

    vmem = pl.BlockSpec(memory_space=pltpu.VMEM)
    smem = pl.BlockSpec(memory_space=pltpu.SMEM)

    def f32(*shape):
        return jax.ShapeDtypeStruct(shape, jnp.float32)

    cells = lon_cells * ROWS
    strip_rows = lon_cells // 32 * ROWS
    moving = [f32(cells, LANES), f32(40, LANES), f32(32, LANES), f32(32, LANES), f32(strip_rows, LANES)]
    params = pltpu.CompilerParams(vmem_limit_bytes=16 * 1024 * 1024)

    keys, listed = pl.pallas_call(
        key_kernel,
        out_shape=[f32(8, LANES), jax.ShapeDtypeStruct((16, LANES), jnp.int32)],
        in_specs=[vmem],
        out_specs=[vmem, vmem],
        compiler_params=params,
    )(slots)

    hbm = pl.BlockSpec(memory_space=pltpu.HBM)
    field, edge_a, edge_b, strips, buffer, sent, table, again = pl.pallas_call(
        functools.partial(start_kernel, lon_cells),
        out_shape=[moving[0], moving[2], moving[3], moving[4], f32(peers * ROWS, LANES), moving[1], f32(24, LANES)]
        + [jax.ShapeDtypeStruct((2 * LANES + 16,), jnp.int32)],
        in_specs=[hbm, smem, smem, smem, vmem, vmem, smem],
        out_specs=[vmem] * 4 + [hbm] + [vmem] * 2 + [smem],
        scratch_shapes=[
            pltpu.VMEM((lon_cells // 32, ROWS, 32, LANES), jnp.float32),
            pltpu.VMEM((LANES, LANES), jnp.float32),
            pltpu.SemaphoreType.DMA((lon_cells // 32 + peers * ROWS // LANES,)),
        ],
        compiler_params=params,
    )(
        state.reshape(ROWS, lon_cells, LANES),
        src,
        send_counts[0, 0, 0],
        partners[0, 0, 0],
        weights.reshape(8, LANES),
        turn_angles.reshape(2, LANES),
        flag,
    )

    origin = field
    for number in range(2 * STEPS):
        second = number % 2 == 1
        final = number == 2 * STEPS - 1
        over = lax.ppermute(sent, ("panel", "core"), CROSS)
        operands = [field] + ([origin] if second else []) + [geo]
        part, part_strips = pl.pallas_call(
            functools.partial(inner_kernel, second, lon_cells, consts),
            out_shape=[moving[0], moving[4]],
            in_specs=[vmem] * len(operands),
            out_specs=[vmem, vmem],
            scratch_shapes=[pltpu.VMEM((8 * 23, LANES), jnp.float32)],
            compiler_params=params,
            cost_estimate=pl.CostEstimate(flops=20_000_000, bytes_accessed=1 << 23, transcendentals=0),
        )(*operands)
        lon_a = lax.ppermute(edge_a, lon_axes, pairs(lon_blocks, 0))
        over, part, part_strips, lon_a = lax.optimization_barrier((over, part, part_strips, lon_a))
        buffer = pl.pallas_call(
            pack_kernel,
            out_shape=f32(peers * ROWS, LANES),
            in_specs=[vmem, hbm],
            out_specs=hbm,
            scratch_shapes=[pltpu.VMEM((2 * ROWS, LANES), jnp.float32), pltpu.SemaphoreType.DMA((2,))],
            input_output_aliases={1: 0},
            compiler_params=params,
        )(over, buffer)
        buffer, own_a, own_b, own_strips, part = lax.optimization_barrier((buffer, edge_a, edge_b, strips, part))
        received = lax.all_to_all(
            buffer.reshape(peers, ROWS, LANES), ("colat", "lon_hi", "core"), split_axis=0, concat_axis=0, tiled=True
        ).reshape(peers * ROWS, LANES)
        if not final:
            corners = pl.pallas_call(
                rows_kernel,
                out_shape=f32(8 * ROWS, LANES),
                in_specs=[vmem, smem],
                out_specs=vmem,
                compiler_params=params,
                cost_estimate=pl.CostEstimate(flops=8_000_000, bytes_accessed=1 << 22, transcendentals=0),
            )(part, src)
        lon_b = lax.ppermute(own_b, lon_axes, pairs(lon_blocks, 1))
        strip_a = lax.ppermute(own_strips, "colat", pairs(lat_blocks, 0))
        strip_b = lax.ppermute(own_strips, "colat", pairs(lat_blocks, 1))
        operands = [part, part_strips, own_a, own_b, own_strips, lon_a, lon_b, strip_a, strip_b, received, keys, listed, flag, geo]
        specs = [vmem] * 11 + [smem, smem, vmem]
        if not final:
            operands += [corners, again, src, table]
            specs += [vmem, smem, smem, vmem]
        out = pl.pallas_call(
            functools.partial(outer_kernel, second, final, lon_cells, consts),
            out_shape=moving[:1] if final else moving,
            in_specs=specs,
            out_specs=[vmem] * (1 if final else 5),
            scratch_shapes=[
                pltpu.VMEM((4 * ROWS, LANES), jnp.float32),
                pltpu.VMEM((strip_rows, LANES), jnp.float32),
                pltpu.VMEM((strip_rows, LANES), jnp.float32),
                pltpu.VMEM((4 * ROWS, LANES), jnp.float32),
            ],
            compiler_params=params,
        )(*operands)
        if final:
            return out[0].reshape(state.shape)
        field, sent, edge_a, edge_b, strips = out
        if second:
            origin = field


def solution(mesh):
    lon = mesh.shape["lon"]
    fine = Mesh(
        mesh.devices.reshape(mesh.shape["panel"], mesh.shape["colat"], lon // 2, 2), ("panel", "colat", "lon_hi", "core")
    )
    lon_axes = ("lon_hi", "core")
    table = P("panel", "colat", lon_axes, None)
    in_specs = (
        P(None, "panel", None, lon_axes, "colat"),
        table,
        table,
        table,
        P(None, "panel", "colat", lon_axes, None),
        table,
        table,
    )
    out_specs = P(None, "panel", None, lon_axes, "colat")
    return jax.shard_map(on_device, mesh=fine, in_specs=in_specs, out_specs=out_specs, check_vma=False)
```

```python
import functools
import math

import jax
import jax.numpy as jnp
import numpy as np
from jax import lax
from jax.experimental import pallas as pl
from jax.experimental.pallas import tpu as pltpu
from jax.sharding import Mesh, PartitionSpec as P

STEPS = 2
R_LOW = 0.7
HALF_ROOT = 0.7071067811865476
LANES = 128
ROWS = 16
NO_KEY = 1.0e9
AGAIN = 16
GROUP = 8
FLIP = 3


def constants(lat_total, lon_total):
    d_theta = 0.5 * math.pi / lat_total
    d_phi = 1.5 * math.pi / lon_total
    spacing = R_LOW * min(d_theta, HALF_ROOT * d_phi)
    time_step = 0.25 * spacing
    kappa = 0.04 * spacing * spacing / time_step
    viscous = 0.06 * spacing * spacing / time_step
    return (
        d_theta,
        d_phi,
        time_step,
        kappa,
        viscous,
        0.05 / time_step,
        0.2 / time_step,
        4.0 * spacing,
    )


def lane_ids(rows):
    return lax.broadcasted_iota(jnp.int32, (rows, LANES), 1)


def sub_ids():
    return lax.broadcasted_iota(jnp.int32, (8, LANES), 0)


def rows_of(u):
    if isinstance(u, int):
        return slice(u * ROWS, (u + 1) * ROWS)
    return pl.ds(pl.multiple_of(u * ROWS, ROWS), ROWS)


def tile(ref, u):
    return ref[rows_of(u), :]


def pick(field, src, at, m, slot, accs):
    lane = lane_ids(8)
    cell = src[at]
    lon = lax.shift_right_logical(cell, 7)
    lat = lax.bitwise_and(cell, LANES - 1)
    both = field[pl.ds(pl.multiple_of(lon * ROWS, ROWS), 2 * ROWS), :]
    near = pltpu.roll(both, lax.bitwise_and(m - lat + LANES, LANES - 1), 1)
    accs = list(accs)
    if isinstance(slot, int):
        columns = [(2 * slot, near, lane == m), (2 * slot + 1, near, lane == lax.bitwise_and(m + 1, LANES - 1))]
    else:
        far = pltpu.roll(both, lax.bitwise_and(m - lat + LANES - 1, LANES - 1), 1)
        columns = []
        for number in range(2):
            mask = lane == jnp.where(slot == number, m, 2 * LANES)
            columns += [(2 * number, near, mask), (2 * number + 1, far, mask)]
    for number, column, mask in columns:
        old = accs[number]
        rows = [jnp.where(mask, column[8 * i : 8 * i + 8], old[8 * i : 8 * i + 8]) for i in range(4)]
        accs[number] = jnp.concatenate(rows, axis=0)
    return tuple(accs)


def gather_all(field, src, lon_cells=0, listed=None):
    def note(at, count):
        if listed is None:
            return count
        cell = src[at]
        lon = lax.shift_right_logical(cell, 7)
        lat = lax.bitwise_and(cell, LANES - 1)
        low = jnp.logical_or(lat < 2, lon < 2)
        high = jnp.logical_or(lat >= LANES - 3, lon >= lon_cells - 3)
        listed[count] = at
        return count + jnp.logical_or(low, high).astype(jnp.int32)

    def body(m, carry):
        count, accs = carry
        accs = pick(field, src, m, m, 0, accs)
        count = note(m, count)
        accs = pick(field, src, LANES + m, m, 1, accs)
        count = note(LANES + m, count)
        return count, accs

    zero = jnp.zeros((2 * ROWS, LANES), jnp.float32)
    count, accs = lax.fori_loop(0, LANES, body, (jnp.int32(0), (zero, zero, zero, zero)), unroll=32)
    if listed is not None:
        for k in range(AGAIN):
            listed[count + k] = 0
        listed[listed.shape[0] - 1] = count
    near0, far0, near1, far1 = accs
    return near0, pltpu.roll(far0, LANES - 1, 1), near1, pltpu.roll(far1, LANES - 1, 1)


def finish_rows(accs, table, sent):
    sub = sub_ids()
    for slot in range(2):
        near, far = accs[2 * slot], accs[2 * slot + 1]
        base = slot * 8
        w0 = table[base : base + 1, :]
        w1 = table[base + 1 : base + 2, :]
        w2 = table[base + 2 : base + 3, :]
        w3 = table[base + 3 : base + 4, :]
        value = w0 * near[:ROWS] + w1 * far[:ROWS] + w2 * near[ROWS:] + w3 * far[ROWS:]
        low, high = value[:8], value[8:]
        cosine = table[base + 4 : base + 5, :]
        sine = table[base + 5 : base + 6, :]
        turned = cosine * high + jnp.where(sub < 4, sine, -sine) * pltpu.roll(high, 4, 0)
        sent[slot * ROWS : slot * ROWS + 8, :] = low
        sent[slot * ROWS + 8 : slot * ROWS + 16, :] = turned
    sent[32:40, :] = table[16:24, :]


def put_edges(field, flag, lon_cells, edge_a, edge_b):
    first = field[0 : 2 * ROWS, :]
    last = field[(lon_cells - 2) * ROWS : lon_cells * ROWS, :]
    odd = flag[0] > 0
    edge_a[...] = jnp.where(odd, first, last)
    edge_b[...] = jnp.where(odd, last, first)


def strip_of(value, col):
    return pltpu.roll(value, 4 * col + 2, 1)


def start_kernel(
    lon_cells, state, src, counts, names, weights, turn, flag,
    field, edge_a, edge_b, strips, buffer, sent, table, listed, zeros, sems
):
    blocks = lon_cells // 32
    zeros[...] = jnp.zeros(zeros.shape, jnp.float32)
    count = zeros.shape[0]
    clears = []
    for number in range(buffer.shape[0] // count):
        copy = pltpu.make_async_copy(zeros, buffer.at[pl.ds(number * count, count), :], sems.at[number])
        copy.start()
        clears.append(copy)
    lane = lane_ids(ROWS)
    quad = lax.shift_right_logical(lane, 2)
    for block in range(blocks):
        acc = jnp.zeros((ROWS, LANES), jnp.float32)
        for col in range(32):
            u = block * 32 + col
            low = state[pl.ds(u, 8, stride=lon_cells), :]
            high = state[pl.ds(u + 8 * lon_cells, 8, stride=lon_cells), :]
            value = jnp.concatenate([low, high], axis=0)
            field[rows_of(u), :] = value
            acc = jnp.where(quad == col, strip_of(value, col), acc)
        strips[block * ROWS : (block + 1) * ROWS, :] = acc
    put_edges(field, flag, lon_cells, edge_a, edge_b)
    row = lane_ids(1)
    table[...] = jnp.zeros(table.shape, jnp.float32)
    angle = turn[...]
    cosine, sine = jnp.cos(angle), jnp.sin(angle)
    for slot in range(2):
        for corner in range(4):
            value = weights[2 * corner + slot : 2 * corner + slot + 1, :]
            table[8 * slot + corner : 8 * slot + corner + 1, :] = jnp.where(row < counts[slot], value, 0.0)
        table[8 * slot + 4 : 8 * slot + 5, :] = cosine[slot : slot + 1]
        table[8 * slot + 5 : 8 * slot + 6, :] = sine[slot : slot + 1]
        table[16 + slot : 17 + slot, :] = jnp.full((1, LANES), names[slot], jnp.int32).astype(jnp.float32)
    finish_rows(gather_all(field, src, lon_cells, listed), table, sent)
    for copy in clears:
        copy.wait()


def key_kernel(slots, keys, listed):
    lane = lane_ids(8)
    slot = slots[...]
    peer = lax.bitwise_xor(lax.shift_right_arithmetic(slot, 7), FLIP)
    shift = lax.bitwise_and(slot - lane, LANES - 1)
    key = jnp.where(slot >= 0, (peer * LANES + shift).astype(jnp.float32), NO_KEY)
    keys[...] = key

    def cond(carry):
        count, more = carry[0], carry[1]
        return jnp.logical_and(count < LANES, more > 0)

    def body(carry):
        count, _, last, found, total = carry
        now = jnp.min(jnp.where(key > last, key, NO_KEY), axis=1, keepdims=True)
        now = jnp.broadcast_to(now, (8, LANES))
        hit = now < NO_KEY
        more = (jnp.min(now) < NO_KEY).astype(jnp.int32)
        found = jnp.where(lane == count, jnp.where(hit, now, -1.0), found)
        total = total + more.astype(jnp.float32)
        return count + 1, more, now, found, total

    zero = jnp.zeros((8, LANES), jnp.float32)
    out = lax.while_loop(cond, body, (jnp.int32(0), jnp.int32(1), zero - 1.0, zero - 1.0, zero))
    listed[0:8, :] = out[3].astype(jnp.int32)
    listed[8:16, :] = out[4].astype(jnp.int32)


def fill_ghosts(received, keys, listed, ghosts):
    def body(step, accs):
        accs = list(accs)
        for row in range(4):
            for i in (2 * step, 2 * step + 1):
                key = listed[row, i]
                known = jnp.maximum(key, 0)
                peer = lax.shift_right_logical(known, 7)
                shift = lax.bitwise_and(known, LANES - 1)
                value = pltpu.roll(tile(received, peer), lax.bitwise_and(LANES - shift, LANES - 1), 1)
                accs[row] = jnp.where(keys[row : row + 1, :] == key.astype(jnp.float32), value, accs[row])
        return tuple(accs)

    zero = jnp.zeros((ROWS, LANES), jnp.float32)
    accs = lax.fori_loop(0, lax.shift_right_logical(listed[8, 0] + 1, 1), body, (zero, zero, zero, zero))
    for row in range(4):
        ghosts[row * ROWS : (row + 1) * ROWS, :] = accs[row]


def merge_strips(strip_a, strip_b, flag, ghosts, merged, blocks):
    lane = lane_ids(8)
    part = lax.bitwise_and(lane, 3)
    odd = flag[1] > 0
    north = flag[2] > 0
    first = part == jnp.where(north, 1, 2)
    second = part == jnp.where(north, 0, 3)
    for block in range(blocks):
        spread = lax.shift_right_logical(lane, 2) + 32 * block
        for half in range(2):
            at = block * ROWS + half * 8
            a = strip_a[at : at + 8, :]
            b = strip_b[at : at + 8, :]
            value = jnp.where(part < 2, jnp.where(odd, a, b), jnp.where(odd, b, a))
            wide0 = jnp.take_along_axis(ghosts[half * 8 : half * 8 + 8, :], spread, axis=1)
            wide1 = jnp.take_along_axis(ghosts[ROWS + half * 8 : ROWS + half * 8 + 8, :], spread, axis=1)
            merged[at : at + 8, :] = value + jnp.where(first, wide0, jnp.where(second, wide1, 0.0))


def coefficients(sin_t, cos_t, yang, consts):
    d_theta, d_phi, step, kappa, viscous, omega, buoyancy, radial = consts
    sub = sub_ids()
    low = sub < 4
    level = lax.bitwise_and(sub, 3).astype(jnp.float32)
    inverse = 1.0 / (level * radial + R_LOW)
    keep = 1.0 - yang
    over_sin = 1.0 / sin_t
    square = inverse * inverse
    advect_t = -step / (12.0 * d_theta) * inverse
    advect_p = -step / (12.0 * d_phi) * inverse * over_sin
    values = [advect_t, advect_p]
    for half in range(2):
        spread = jnp.where(low, step * kappa, step * viscous) if half == 0 else jnp.full((8, LANES), step * viscous)
        second_t = spread * square / (12.0 * d_theta * d_theta)
        first_t = spread * square * (cos_t * over_sin) / (12.0 * d_theta)
        second_p = spread * square * (over_sin * over_sin) / (12.0 * d_phi * d_phi)
        second_r = spread / (radial * radial)
        first_r = spread * inverse / radial
        middle = -30.0 * second_t - 30.0 * second_p - 2.0 * second_r
        values += [second_t, first_t, second_p, second_r, first_r, middle]
    twice = 2.0 * step * omega
    zero = jnp.zeros((8, LANES), jnp.float32)
    sign = jnp.where(low, 1.0, -1.0)
    values += [
        jnp.where(low, 0.0, step * buoyancy),
        jnp.where(low, zero, twice * keep * sin_t),
        jnp.where(low, zero, -twice * cos_t),
        jnp.where(low, 0.0, twice) + zero,
        sign * twice * keep * cos_t,
        sign * twice * sin_t,
        jnp.where(low, zero, -twice * keep * sin_t),
        jnp.where(low, zero, twice * cos_t),
        jnp.where(low, -twice, 0.0) + zero,
    ]
    return values


def inner_kernel(second, lon_cells, consts, *refs):
    refs = list(refs)
    field = refs.pop(0)
    origin = refs.pop(0) if second else None
    geo, result, strips, coef = refs
    base = 2 * lon_cells
    sin_t, cos_t, yang = (geo[base + 8 * i : base + 8 * i + 8, :] for i in range(3))
    for i, value in enumerate(coefficients(sin_t, cos_t, yang, consts)):
        coef[8 * i : 8 * i + 8, :] = value
    radial = consts[7]
    lane16 = lane_ids(ROWS)
    quad = lax.shift_right_logical(lane16, 2)
    sub = sub_ids()
    low = sub < 4
    level = lax.bitwise_and(sub, 3)
    top = level == 3
    bottom = level == 0
    advect_r = -consts[2] / (2.0 * radial)

    def c(i):
        return coef[8 * i : 8 * i + 8, :]

    def update(u, down2, down1, here, up1, up2):
        south1 = jnp.where(lane16 >= 1, pltpu.roll(here, 1, 1), 0.0)
        south2 = jnp.where(lane16 >= 2, pltpu.roll(here, 2, 1), 0.0)
        north1 = jnp.where(lane16 < LANES - 1, pltpu.roll(here, LANES - 1, 1), 0.0)
        north2 = jnp.where(lane16 < LANES - 2, pltpu.roll(here, LANES - 2, 1), 0.0)
        lat_odd = 8.0 * (north1 - south1) - (north2 - south2)
        lat_even = 16.0 * (north1 + south1) - (north2 + south2)
        lon_odd = 8.0 * (up1 - down1) - (up2 - down2)
        lon_even = 16.0 * (up1 + down1) - (up2 + down2)
        v0, v1 = here[:8], here[8:]
        r0, r1 = pltpu.roll(v0, 4, 0), pltpu.roll(v1, 4, 0)
        vel_r = jnp.where(low, r0, v0)
        vel_t = jnp.where(low, v1, r1)
        vel_p = jnp.where(low, r1, v1)
        along_t = vel_t * c(0)
        along_p = vel_p * c(1)
        along_r = vel_r * advect_r
        sin_p = geo[pl.ds(u, 1), :]
        cos_p = geo[pl.ds(lon_cells + u, 1), :]
        turn0 = c(14) * r0 + (c(15) + c(16) * sin_p) * vel_p + (c(17) * cos_p) * vel_t
        turn1 = (c(18) + c(19) * sin_p) * r1 + (c(20) + c(21) * sin_p + c(22) * cos_p) * vel_r
        out = []
        for half, value, turn in ((0, v0, turn0), (1, v1, turn1)):
            at = 2 + 6 * half
            part = slice(8 * half, 8 * half + 8)
            above = jnp.where(top, value, pltpu.roll(value, 7, 0))
            below = jnp.where(bottom, value, pltpu.roll(value, 1, 0))
            change = (
                (c(at + 1) + along_t) * lat_odd[part]
                + c(at) * lat_even[part]
                + along_p * lon_odd[part]
                + c(at + 2) * lon_even[part]
                + (c(at + 4) + along_r) * (above - below)
                + c(at + 3) * (above + below)
                + c(at + 5) * value
                + turn
            )
            out.append(value + change)
        new = jnp.concatenate(out, axis=0)
        if second:
            new = 0.5 * (tile(origin, u) + new)
        return new

    def at(u):
        if u < 0 or u >= lon_cells:
            return jnp.zeros((ROWS, LANES), jnp.float32)
        return tile(field, u)

    def group(index, block, col, tiles):
        acc = jnp.zeros((ROWS, LANES), jnp.float32)
        for k in range(GROUP):
            new = update(index + k, *tiles[k : k + 5])
            result[rows_of(index + k), :] = new
            acc = jnp.where(quad == col + k, strip_of(new, col + k), acc)
        rows = rows_of(block)
        mine = jnp.logical_and(quad >= col, quad < col + GROUP)
        strips[rows, :] = jnp.where(mine, acc, strips[rows, :])

    strips[...] = jnp.zeros(strips.shape, jnp.float32)
    for index in (0, lon_cells - GROUP):
        group(index, index // 32, index % 32, [at(u) for u in range(index - 2, index + GROUP + 2)])

    def body(number, carry):
        index = number * GROUP
        tiles = [tile(field, index + k) for k in range(-2, GROUP + 2)]
        group(index, lax.shift_right_logical(index, 5), lax.bitwise_and(index, 31), tiles)
        return carry

    lax.fori_loop(1, lon_cells // GROUP - 1, body, 0)


def rows_kernel(field, src, corners):
    for i, value in enumerate(gather_all(field, src)):
        corners[2 * i * ROWS : 2 * (i + 1) * ROWS, :] = value


def outer_kernel(second, final, lon_cells, consts, *refs):
    refs = list(refs)
    part, part_strips, own_a, own_b, own_strips, lon_a, lon_b, strip_a, strip_b, received, keys, listed, flag, geo = refs[:14]
    refs = refs[14:]
    if final:
        result = refs.pop(0)
    else:
        corners, again, src, table, result, sent, edge_a, edge_b, strips = refs[:9]
        refs = refs[9:]
    ghosts, merged, fixes, sides = refs
    blocks = lon_cells // 32
    fill_ghosts(received, keys, listed, ghosts)
    merge_strips(strip_a, strip_b, flag, ghosts, merged, blocks)

    base = 2 * lon_cells
    sin_t, cos_t, yang, strip_sin, strip_cos = (geo[base + 8 * i : base + 8 * i + 8, :] for i in range(5))
    low = sub_ids() < 4
    lane = lane_ids(8)
    scale = 0.5 if second else 1.0

    values = coefficients(strip_sin, strip_cos, yang, consts)
    quarter = lax.bitwise_and(lane, 3)
    for block in range(blocks):
        at = block * ROWS
        v1 = own_strips[at + 8 : at + 16, :]
        along = jnp.where(low, v1, pltpu.roll(v1, 4, 0)) * values[0]
        for half in range(2):
            rows = slice(at + 8 * half, at + 8 * half + 8)
            outside = merged[rows, :]
            left1, left2 = pltpu.roll(outside, LANES - 1, 1), pltpu.roll(outside, LANES - 2, 1)
            right1, right2 = pltpu.roll(outside, 1, 1), pltpu.roll(outside, 2, 1)
            near = jnp.where(quarter == 1, left1, jnp.where(quarter == 2, right1, 0.0))
            far = jnp.where(quarter < 2, left2, right2)
            first = jnp.where(quarter < 2, 8.0 * near - far, far - 8.0 * near)
            twice = 16.0 * near - far
            fixes[rows, :] = scale * ((values[3 + 6 * half] + along) * first + values[2 + 6 * half] * twice)

    values = coefficients(sin_t, cos_t, yang, consts)
    odd = flag[0] > 0
    west = flag[3] > 0
    for i, row in enumerate((3, 2, 2, 3)):
        came = jnp.where(odd, lon_a[...], lon_b[...]) if i < 2 else jnp.where(odd, lon_b[...], lon_a[...])
        ghost = jnp.where(west if i < 2 else jnp.logical_not(west), ghosts[rows_of(row), :], 0.0)
        sides[rows_of(i), :] = came[rows_of(i % 2)] + ghost
    before2, before1, after1, after2 = (sides[rows_of(i), :] for i in range(4))
    for i, (near, far, sign) in enumerate(
        ((before1, before2, -1.0), (None, before1, -1.0), (None, after1, 1.0), (after1, after2, 1.0))
    ):
        own = jnp.where(odd, own_a[...], own_b[...]) if i < 2 else jnp.where(odd, own_b[...], own_a[...])
        v1 = own[rows_of(i % 2)][8:]
        along = jnp.where(low, pltpu.roll(v1, 4, 0), v1) * values[1]
        first = -far if near is None else 8.0 * near - far
        twice = -far if near is None else 16.0 * near - far
        for half in range(2):
            rows = slice(8 * half, 8 * half + 8)
            change = sign * along * first[rows] + values[4 + 6 * half] * twice[rows]
            sides[i * ROWS + 8 * half : i * ROWS + 8 * half + 8, :] = scale * change

    lane16 = lane_ids(ROWS)
    rim = jnp.logical_or(lane16 < 2, lane16 >= LANES - 2)

    def corrected(u, block, col):
        moved = pltpu.roll(tile(fixes, block), lax.bitwise_and(LANES - 2 - 4 * col, LANES - 1), 1)
        return tile(part, u) + jnp.where(rim, moved, 0.0)

    def store(u, new):
        if final:
            result[pl.ds(u, 8, stride=lon_cells), :] = new[:8]
            result[pl.ds(u + 8 * lon_cells, 8, stride=lon_cells), :] = new[8:]
        else:
            result[rows_of(u), :] = new

    def body(block, carry):
        for col in range(32):
            u = block * 32 + col
            store(u, corrected(u, block, col))
        return carry

    lax.fori_loop(0, blocks, body, 0)
    if not final:
        strips[...] = part_strips[...] + fixes[...]
    quad = lax.shift_right_logical(lane16, 2)
    for i, u in enumerate((0, 1, lon_cells - 2, lon_cells - 1)):
        block, col = divmod(u, 32)
        change = sides[rows_of(i), :]
        store(u, corrected(u, block, col) + change)
        if not final:
            strips[rows_of(block), :] += jnp.where(quad == col, strip_of(change, col), 0.0)
    if final:
        return
    put_edges(result, flag, lon_cells, edge_a, edge_b)

    def repeat(step, accs):
        for k in range(AGAIN):
            at = again[AGAIN * step + k]
            accs = pick(result, src, at, lax.bitwise_and(at, LANES - 1), lax.shift_right_logical(at, 7), accs)
        return accs

    accs = tuple(corners[2 * i * ROWS : 2 * (i + 1) * ROWS, :] for i in range(4))
    steps = (again[again.shape[0] - 1] + AGAIN - 1) // AGAIN
    finish_rows(lax.fori_loop(0, steps, repeat, accs), table, sent)


def pack_kernel(message, _, buffer, staged, sems):
    target0 = jnp.max(message[32:33, :]).astype(jnp.int32)
    target1 = jnp.max(message[33:34, :]).astype(jnp.int32)
    same = target0 == target1
    slot0, slot1 = message[0:ROWS, :], message[ROWS : 2 * ROWS, :]
    staged[0:ROWS, :] = jnp.where(same, slot0 + slot1, slot0)
    staged[ROWS : 2 * ROWS, :] = slot1
    copies = [
        pltpu.make_async_copy(
            staged.at[pl.ds(at * ROWS, ROWS), :],
            buffer.at[pl.ds(pl.multiple_of(target * ROWS, ROWS), ROWS), :],
            sems.at[at],
        )
        for at, target in enumerate((target0, target1))
    ]
    copies[0].start()
    pl.when(jnp.logical_not(same))(copies[1].start)
    copies[0].wait()
    pl.when(jnp.logical_not(same))(copies[1].wait)


def crossing(count):
    return [(here, (here ^ FLIP) + count) for here in range(count)] + [(here + count, here ^ FLIP) for here in range(count)]


def pairs(count, first):
    route = []
    for low in range(first, count - 1, 2):
        route += [(low, low + 1), (low + 1, low)]
    return route


def on_device(state, partners, send_counts, source_cells, weights, turn_angles, ghost_slots):
    lat_blocks = lax.axis_size("colat")
    lon_axes = ("lon_hi", "core")
    lon_blocks = lax.axis_size(lon_axes)
    peers = lat_blocks * lon_blocks
    lon_cells, lat_cells = state.shape[3], state.shape[4]
    consts = constants(lat_cells * lat_blocks, lon_cells * lon_blocks)
    core = lax.axis_index("core")
    colat = lax.axis_index("colat")
    lon = lax.axis_index(lon_axes)
    yang = lax.axis_index("panel").astype(jnp.float32)
    flag = jnp.stack([lon % 2, colat % 2, colat == 0, lon == 0]).astype(jnp.int32)

    src = source_cells[0, 0, 0]
    theta = ((colat * lat_cells + jnp.arange(lat_cells, dtype=jnp.int32)).astype(jnp.float32) + 0.5) * consts[0] + 0.25 * math.pi
    rim_lat = (jnp.arange(LANES, dtype=jnp.int32) + 2) % 4 + jnp.where(jnp.arange(LANES, dtype=jnp.int32) % 4 < 2, lat_cells - 4, 0)
    rim_theta = ((colat * lat_cells + rim_lat).astype(jnp.float32) + 0.5) * consts[0] + 0.25 * math.pi
    phi = ((lon * lon_cells + jnp.arange(lon_cells, dtype=jnp.int32)).astype(jnp.float32) + 0.5) * consts[1] - 0.75 * math.pi
    geo = jnp.concatenate(
        [
            jnp.broadcast_to((yang * jnp.sin(phi))[:, None], (lon_cells, LANES)),
            jnp.broadcast_to((yang * jnp.cos(phi))[:, None], (lon_cells, LANES)),
            jnp.broadcast_to(jnp.sin(theta)[None], (8, LANES)),
            jnp.broadcast_to(jnp.cos(theta)[None], (8, LANES)),
            jnp.broadcast_to(yang, (8, LANES)),
            jnp.broadcast_to(jnp.sin(rim_theta)[None], (8, LANES)),
            jnp.broadcast_to(jnp.cos(rim_theta)[None], (8, LANES)),
        ]
    )
    slot = ghost_slots[0, 0, 0]
    pole = slot[: 4 * lon_cells].reshape(2, 2, lon_cells)
    pole = jnp.pad(jnp.maximum(pole[0], pole[1]), ((0, 0), (0, LANES - lon_cells)), constant_values=-1)
    side = slot[4 * lon_cells :].reshape(2, 2, LANES)
    slots = jnp.concatenate([pole, jnp.maximum(side[0], side[1]), jnp.full((4, LANES), -1, jnp.int32)])

    vmem = pl.BlockSpec(memory_space=pltpu.VMEM)
    smem = pl.BlockSpec(memory_space=pltpu.SMEM)

    def f32(*shape):
        return jax.ShapeDtypeStruct(shape, jnp.float32)

    cells = lon_cells * ROWS
    strip_rows = lon_cells // 32 * ROWS
    moving = [f32(cells, LANES), f32(40, LANES), f32(32, LANES), f32(32, LANES), f32(strip_rows, LANES)]
    params = pltpu.CompilerParams(vmem_limit_bytes=16 * 1024 * 1024)

    keys, listed = pl.pallas_call(
        key_kernel,
        out_shape=[f32(8, LANES), jax.ShapeDtypeStruct((16, LANES), jnp.int32)],
        in_specs=[vmem],
        out_specs=[vmem, vmem],
        compiler_params=params,
    )(slots)

    hbm = pl.BlockSpec(memory_space=pltpu.HBM)
    field, edge_a, edge_b, strips, buffer, sent, table, again = pl.pallas_call(
        functools.partial(start_kernel, lon_cells),
        out_shape=[moving[0], moving[2], moving[3], moving[4], f32(peers * ROWS, LANES), moving[1], f32(24, LANES)]
        + [jax.ShapeDtypeStruct((2 * LANES + 16,), jnp.int32)],
        in_specs=[vmem, smem, smem, smem, vmem, vmem, smem],
        out_specs=[vmem] * 4 + [hbm] + [vmem] * 2 + [smem],
        scratch_shapes=[
            pltpu.VMEM((LANES, LANES), jnp.float32),
            pltpu.SemaphoreType.DMA((peers * ROWS // LANES,)),
        ],
        compiler_params=params,
    )(
        state.reshape(cells, LANES),
        src,
        send_counts[0, 0, 0],
        partners[0, 0, 0],
        weights.reshape(8, LANES),
        turn_angles.reshape(2, LANES),
        flag,
    )

    origin = field
    for number in range(2 * STEPS):
        second = number % 2 == 1
        final = number == 2 * STEPS - 1
        over = lax.ppermute(sent, ("panel",) + lon_axes, crossing(lon_blocks))
        operands = [field] + ([origin] if second else []) + [geo]
        part, part_strips = pl.pallas_call(
            functools.partial(inner_kernel, second, lon_cells, consts),
            out_shape=[moving[0], moving[4]],
            in_specs=[vmem] * len(operands),
            out_specs=[vmem, vmem],
            scratch_shapes=[pltpu.VMEM((8 * 23, LANES), jnp.float32)],
            compiler_params=params,
            cost_estimate=pl.CostEstimate(flops=20_000_000, bytes_accessed=1 << 23, transcendentals=0),
        )(*operands)
        lon_a = lax.ppermute(edge_a, lon_axes, pairs(lon_blocks, 0))
        over, part, part_strips, lon_a = lax.optimization_barrier((over, part, part_strips, lon_a))
        buffer = pl.pallas_call(
            pack_kernel,
            out_shape=f32(peers * ROWS, LANES),
            in_specs=[vmem, hbm],
            out_specs=hbm,
            scratch_shapes=[pltpu.VMEM((2 * ROWS, LANES), jnp.float32), pltpu.SemaphoreType.DMA((2,))],
            input_output_aliases={1: 0},
            compiler_params=params,
        )(over, buffer)
        buffer, own_a, own_b, own_strips, part = lax.optimization_barrier((buffer, edge_a, edge_b, strips, part))
        received = lax.all_to_all(
            buffer.reshape(peers, ROWS, LANES), ("colat", "lon_hi", "core"), split_axis=0, concat_axis=0, tiled=True
        ).reshape(peers * ROWS, LANES)
        if not final:
            corners = pl.pallas_call(
                rows_kernel,
                out_shape=f32(8 * ROWS, LANES),
                in_specs=[vmem, smem],
                out_specs=vmem,
                compiler_params=params,
                cost_estimate=pl.CostEstimate(flops=8_000_000, bytes_accessed=1 << 22, transcendentals=0),
            )(part, src)
        lon_b = lax.ppermute(own_b, lon_axes, pairs(lon_blocks, 1))
        strip_a = lax.ppermute(own_strips, "colat", pairs(lat_blocks, 0))
        strip_b = lax.ppermute(own_strips, "colat", pairs(lat_blocks, 1))
        operands = [part, part_strips, own_a, own_b, own_strips, lon_a, lon_b, strip_a, strip_b, received, keys, listed, flag, geo]
        specs = [vmem] * 11 + [smem, smem, vmem]
        if not final:
            operands += [corners, again, src, table]
            specs += [vmem, smem, smem, vmem]
        out = pl.pallas_call(
            functools.partial(outer_kernel, second, final, lon_cells, consts),
            out_shape=moving[:1] if final else moving,
            in_specs=specs,
            out_specs=[vmem] * (1 if final else 5),
            scratch_shapes=[
                pltpu.VMEM((4 * ROWS, LANES), jnp.float32),
                pltpu.VMEM((strip_rows, LANES), jnp.float32),
                pltpu.VMEM((strip_rows, LANES), jnp.float32),
                pltpu.VMEM((4 * ROWS, LANES), jnp.float32),
            ],
            compiler_params=params,
        )(*operands)
        if final:
            return out[0].reshape(state.shape)
        field, sent, edge_a, edge_b, strips = out
        if second:
            origin = field


def solution(mesh):
    lon = mesh.shape["lon"]
    fine = Mesh(
        mesh.devices.reshape(mesh.shape["panel"], mesh.shape["colat"], lon // 2, 2), ("panel", "colat", "lon_hi", "core")
    )
    lon_axes = ("lon_hi", "core")
    table = P("panel", "colat", lon_axes, None)
    in_specs = (
        P(None, "panel", None, lon_axes, "colat"),
        table,
        table,
        table,
        P(None, "panel", "colat", lon_axes, None),
        table,
        table,
    )
    out_specs = P(None, "panel", None, lon_axes, "colat")
    return jax.shard_map(on_device, mesh=fine, in_specs=in_specs, out_specs=out_specs, check_vma=False)
```

```python
import functools
import math

import jax
import jax.numpy as jnp
import numpy as np
from jax import lax
from jax.experimental import pallas as pl
from jax.experimental.pallas import tpu as pltpu
from jax.sharding import Mesh, PartitionSpec as P

STEPS = 2
R_LOW = 0.7
HALF_ROOT = 0.7071067811865476
LANES = 128
ROWS = 16
NO_KEY = 1.0e9
AGAIN = 16
GROUP = 8
FLIP = 3


def constants(lat_total, lon_total):
    d_theta = 0.5 * math.pi / lat_total
    d_phi = 1.5 * math.pi / lon_total
    spacing = R_LOW * min(d_theta, HALF_ROOT * d_phi)
    time_step = 0.25 * spacing
    kappa = 0.04 * spacing * spacing / time_step
    viscous = 0.06 * spacing * spacing / time_step
    return (
        d_theta,
        d_phi,
        time_step,
        kappa,
        viscous,
        0.05 / time_step,
        0.2 / time_step,
        4.0 * spacing,
    )


def lane_ids(rows):
    return lax.broadcasted_iota(jnp.int32, (rows, LANES), 1)


def sub_ids():
    return lax.broadcasted_iota(jnp.int32, (8, LANES), 0)


def rows_of(u):
    if isinstance(u, int):
        return slice(u * ROWS, (u + 1) * ROWS)
    return pl.ds(pl.multiple_of(u * ROWS, ROWS), ROWS)


def tile(ref, u):
    return ref[rows_of(u), :]


def pick(field, src, at, m, slot, accs):
    lane = lane_ids(8)
    cell = src[at]
    lon = lax.shift_right_logical(cell, 7)
    lat = lax.bitwise_and(cell, LANES - 1)
    both = field[pl.ds(pl.multiple_of(lon * ROWS, ROWS), 2 * ROWS), :]
    near = pltpu.roll(both, lax.bitwise_and(m - lat + LANES, LANES - 1), 1)
    accs = list(accs)
    if isinstance(slot, int):
        columns = [(2 * slot, near, lane == m), (2 * slot + 1, near, lane == lax.bitwise_and(m + 1, LANES - 1))]
    else:
        far = pltpu.roll(both, lax.bitwise_and(m - lat + LANES - 1, LANES - 1), 1)
        columns = []
        for number in range(2):
            mask = lane == jnp.where(slot == number, m, 2 * LANES)
            columns += [(2 * number, near, mask), (2 * number + 1, far, mask)]
    for number, column, mask in columns:
        old = accs[number]
        rows = [jnp.where(mask, column[8 * i : 8 * i + 8], old[8 * i : 8 * i + 8]) for i in range(4)]
        accs[number] = jnp.concatenate(rows, axis=0)
    return tuple(accs)


def gather_all(field, src, lon_cells=0, listed=None):
    def note(at, count):
        if listed is None:
            return count
        cell = src[at]
        lon = lax.shift_right_logical(cell, 7)
        lat = lax.bitwise_and(cell, LANES - 1)
        low = jnp.logical_or(lat < 2, lon < 2)
        high = jnp.logical_or(lat >= LANES - 3, lon >= lon_cells - 3)
        listed[count] = at
        return count + jnp.logical_or(low, high).astype(jnp.int32)

    def body(m, carry):
        count, accs = carry
        accs = pick(field, src, m, m, 0, accs)
        count = note(m, count)
        accs = pick(field, src, LANES + m, m, 1, accs)
        count = note(LANES + m, count)
        return count, accs

    zero = jnp.zeros((2 * ROWS, LANES), jnp.float32)
    count, accs = lax.fori_loop(0, LANES, body, (jnp.int32(0), (zero, zero, zero, zero)), unroll=32)
    if listed is not None:
        for k in range(AGAIN):
            listed[count + k] = 0
        listed[listed.shape[0] - 1] = count
    near0, far0, near1, far1 = accs
    return near0, pltpu.roll(far0, LANES - 1, 1), near1, pltpu.roll(far1, LANES - 1, 1)


def finish_rows(accs, table, sent):
    sub = sub_ids()
    for slot in range(2):
        near, far = accs[2 * slot], accs[2 * slot + 1]
        base = slot * 8
        w0 = table[base : base + 1, :]
        w1 = table[base + 1 : base + 2, :]
        w2 = table[base + 2 : base + 3, :]
        w3 = table[base + 3 : base + 4, :]
        value = w0 * near[:ROWS] + w1 * far[:ROWS] + w2 * near[ROWS:] + w3 * far[ROWS:]
        low, high = value[:8], value[8:]
        cosine = table[base + 4 : base + 5, :]
        sine = table[base + 5 : base + 6, :]
        turned = cosine * high + jnp.where(sub < 4, sine, -sine) * pltpu.roll(high, 4, 0)
        sent[slot * ROWS : slot * ROWS + 8, :] = low
        sent[slot * ROWS + 8 : slot * ROWS + 16, :] = turned
    sent[32:40, :] = table[16:24, :]


def put_edges(field, flag, lon_cells, edge_a, edge_b):
    first = field[0 : 2 * ROWS, :]
    last = field[(lon_cells - 2) * ROWS : lon_cells * ROWS, :]
    odd = flag[0] > 0
    edge_a[...] = jnp.where(odd, first, last)
    edge_b[...] = jnp.where(odd, last, first)


def strip_of(value, col):
    return pltpu.roll(value, 4 * col + 2, 1)


def start_kernel(
    lon_cells, state, src, counts, names, weights, turn, flag,
    field, edge_a, edge_b, strips, buffer, sent, table, listed, zeros, sems
):
    blocks = lon_cells // 32
    zeros[...] = jnp.zeros(zeros.shape, jnp.float32)
    count = zeros.shape[0]
    clears = []
    for number in range(buffer.shape[0] // count):
        copy = pltpu.make_async_copy(zeros, buffer.at[pl.ds(number * count, count), :], sems.at[number])
        copy.start()
        clears.append(copy)
    lane = lane_ids(ROWS)
    quad = lax.shift_right_logical(lane, 2)
    for block in range(blocks):
        acc = jnp.zeros((ROWS, LANES), jnp.float32)
        for col in range(32):
            u = block * 32 + col
            low = state[pl.ds(u, 8, stride=lon_cells), :]
            high = state[pl.ds(u + 8 * lon_cells, 8, stride=lon_cells), :]
            value = jnp.concatenate([low, high], axis=0)
            field[rows_of(u), :] = value
            acc = jnp.where(quad == col, strip_of(value, col), acc)
        strips[block * ROWS : (block + 1) * ROWS, :] = acc
    put_edges(field, flag, lon_cells, edge_a, edge_b)
    row = lane_ids(1)
    table[...] = jnp.zeros(table.shape, jnp.float32)
    angle = turn[...]
    cosine, sine = jnp.cos(angle), jnp.sin(angle)
    for slot in range(2):
        for corner in range(4):
            value = weights[2 * corner + slot : 2 * corner + slot + 1, :]
            table[8 * slot + corner : 8 * slot + corner + 1, :] = jnp.where(row < counts[slot], value, 0.0)
        table[8 * slot + 4 : 8 * slot + 5, :] = cosine[slot : slot + 1]
        table[8 * slot + 5 : 8 * slot + 6, :] = sine[slot : slot + 1]
        table[16 + slot : 17 + slot, :] = jnp.full((1, LANES), names[slot], jnp.int32).astype(jnp.float32)
    finish_rows(gather_all(field, src, lon_cells, listed), table, sent)
    for copy in clears:
        copy.wait()


def key_kernel(slots, keys, listed):
    lane = lane_ids(8)
    slot = slots[...]
    peer = seat(lax.bitwise_xor(lax.shift_right_logical(jnp.maximum(slot, 0), 7), FLIP))
    shift = lax.bitwise_and(slot - lane, LANES - 1)
    key = jnp.where(slot >= 0, (peer * LANES + shift).astype(jnp.float32), NO_KEY)
    keys[...] = key

    def cond(carry):
        count, more = carry[0], carry[1]
        return jnp.logical_and(count < LANES, more > 0)

    def body(carry):
        count, _, last, found, total = carry
        now = jnp.min(jnp.where(key > last, key, NO_KEY), axis=1, keepdims=True)
        now = jnp.broadcast_to(now, (8, LANES))
        hit = now < NO_KEY
        more = (jnp.min(now) < NO_KEY).astype(jnp.int32)
        found = jnp.where(lane == count, jnp.where(hit, now, -1.0), found)
        total = total + more.astype(jnp.float32)
        return count + 1, more, now, found, total

    zero = jnp.zeros((8, LANES), jnp.float32)
    out = lax.while_loop(cond, body, (jnp.int32(0), jnp.int32(1), zero - 1.0, zero - 1.0, zero))
    listed[0:8, :] = out[3].astype(jnp.int32)
    listed[8:16, :] = out[4].astype(jnp.int32)


def fill_ghosts(received, keys, listed, ghosts):
    def body(step, accs):
        accs = list(accs)
        for row in range(4):
            for i in (2 * step, 2 * step + 1):
                key = listed[row, i]
                known = jnp.maximum(key, 0)
                peer = lax.shift_right_logical(known, 7)
                shift = lax.bitwise_and(known, LANES - 1)
                value = pltpu.roll(tile(received, peer), lax.bitwise_and(LANES - shift, LANES - 1), 1)
                accs[row] = jnp.where(keys[row : row + 1, :] == key.astype(jnp.float32), value, accs[row])
        return tuple(accs)

    zero = jnp.zeros((ROWS, LANES), jnp.float32)
    accs = lax.fori_loop(0, lax.shift_right_logical(listed[8, 0] + 1, 1), body, (zero, zero, zero, zero))
    for row in range(4):
        ghosts[row * ROWS : (row + 1) * ROWS, :] = accs[row]


def merge_strips(strip_a, strip_b, flag, ghosts, merged, blocks):
    lane = lane_ids(8)
    part = lax.bitwise_and(lane, 3)
    odd = flag[1] > 0
    north = flag[2] > 0
    first = part == jnp.where(north, 1, 2)
    second = part == jnp.where(north, 0, 3)
    for block in range(blocks):
        spread = lax.shift_right_logical(lane, 2) + 32 * block
        for half in range(2):
            at = block * ROWS + half * 8
            a = strip_a[at : at + 8, :]
            b = strip_b[at : at + 8, :]
            value = jnp.where(part < 2, jnp.where(odd, a, b), jnp.where(odd, b, a))
            wide0 = jnp.take_along_axis(ghosts[half * 8 : half * 8 + 8, :], spread, axis=1)
            wide1 = jnp.take_along_axis(ghosts[ROWS + half * 8 : ROWS + half * 8 + 8, :], spread, axis=1)
            merged[at : at + 8, :] = value + jnp.where(first, wide0, jnp.where(second, wide1, 0.0))


def coefficients(sin_t, cos_t, yang, consts):
    d_theta, d_phi, step, kappa, viscous, omega, buoyancy, radial = consts
    sub = sub_ids()
    low = sub < 4
    level = lax.bitwise_and(sub, 3).astype(jnp.float32)
    inverse = 1.0 / (level * radial + R_LOW)
    keep = 1.0 - yang
    over_sin = 1.0 / sin_t
    square = inverse * inverse
    advect_t = -step / (12.0 * d_theta) * inverse
    advect_p = -step / (12.0 * d_phi) * inverse * over_sin
    values = [advect_t, advect_p]
    for half in range(2):
        spread = jnp.where(low, step * kappa, step * viscous) if half == 0 else jnp.full((8, LANES), step * viscous)
        second_t = spread * square / (12.0 * d_theta * d_theta)
        first_t = spread * square * (cos_t * over_sin) / (12.0 * d_theta)
        second_p = spread * square * (over_sin * over_sin) / (12.0 * d_phi * d_phi)
        second_r = spread / (radial * radial)
        first_r = spread * inverse / radial
        middle = -30.0 * second_t - 30.0 * second_p - 2.0 * second_r
        values += [second_t, first_t, second_p, second_r, first_r, middle]
    twice = 2.0 * step * omega
    zero = jnp.zeros((8, LANES), jnp.float32)
    sign = jnp.where(low, 1.0, -1.0)
    values += [
        jnp.where(low, 0.0, step * buoyancy),
        jnp.where(low, zero, twice * keep * sin_t),
        jnp.where(low, zero, -twice * cos_t),
        jnp.where(low, 0.0, twice) + zero,
        sign * twice * keep * cos_t,
        sign * twice * sin_t,
        jnp.where(low, zero, -twice * keep * sin_t),
        jnp.where(low, zero, twice * cos_t),
        jnp.where(low, -twice, 0.0) + zero,
    ]
    return values


def inner_kernel(second, lon_cells, consts, *refs):
    refs = list(refs)
    field = refs.pop(0)
    origin = refs.pop(0) if second else None
    geo, result, strips, coef = refs
    base = 2 * lon_cells
    sin_t, cos_t, yang = (geo[base + 8 * i : base + 8 * i + 8, :] for i in range(3))
    for i, value in enumerate(coefficients(sin_t, cos_t, yang, consts)):
        coef[8 * i : 8 * i + 8, :] = value
    radial = consts[7]
    lane16 = lane_ids(ROWS)
    quad = lax.shift_right_logical(lane16, 2)
    sub = sub_ids()
    low = sub < 4
    level = lax.bitwise_and(sub, 3)
    top = level == 3
    bottom = level == 0
    advect_r = -consts[2] / (2.0 * radial)

    def c(i):
        return coef[8 * i : 8 * i + 8, :]

    def update(u, down2, down1, here, up1, up2):
        south1 = jnp.where(lane16 >= 1, pltpu.roll(here, 1, 1), 0.0)
        south2 = jnp.where(lane16 >= 2, pltpu.roll(here, 2, 1), 0.0)
        north1 = jnp.where(lane16 < LANES - 1, pltpu.roll(here, LANES - 1, 1), 0.0)
        north2 = jnp.where(lane16 < LANES - 2, pltpu.roll(here, LANES - 2, 1), 0.0)
        lat_odd = 8.0 * (north1 - south1) - (north2 - south2)
        lat_even = 16.0 * (north1 + south1) - (north2 + south2)
        lon_odd = 8.0 * (up1 - down1) - (up2 - down2)
        lon_even = 16.0 * (up1 + down1) - (up2 + down2)
        v0, v1 = here[:8], here[8:]
        r0, r1 = pltpu.roll(v0, 4, 0), pltpu.roll(v1, 4, 0)
        vel_r = jnp.where(low, r0, v0)
        vel_t = jnp.where(low, v1, r1)
        vel_p = jnp.where(low, r1, v1)
        along_t = vel_t * c(0)
        along_p = vel_p * c(1)
        along_r = vel_r * advect_r
        sin_p = geo[pl.ds(u, 1), :]
        cos_p = geo[pl.ds(lon_cells + u, 1), :]
        turn0 = c(14) * r0 + (c(15) + c(16) * sin_p) * vel_p + (c(17) * cos_p) * vel_t
        turn1 = (c(18) + c(19) * sin_p) * r1 + (c(20) + c(21) * sin_p + c(22) * cos_p) * vel_r
        out = []
        for half, value, turn in ((0, v0, turn0), (1, v1, turn1)):
            at = 2 + 6 * half
            part = slice(8 * half, 8 * half + 8)
            above = jnp.where(top, value, pltpu.roll(value, 7, 0))
            below = jnp.where(bottom, value, pltpu.roll(value, 1, 0))
            change = (
                (c(at + 1) + along_t) * lat_odd[part]
                + c(at) * lat_even[part]
                + along_p * lon_odd[part]
                + c(at + 2) * lon_even[part]
                + (c(at + 4) + along_r) * (above - below)
                + c(at + 3) * (above + below)
                + c(at + 5) * value
                + turn
            )
            out.append(value + change)
        new = jnp.concatenate(out, axis=0)
        if second:
            new = 0.5 * (tile(origin, u) + new)
        return new

    def at(u):
        if u < 0 or u >= lon_cells:
            return jnp.zeros((ROWS, LANES), jnp.float32)
        return tile(field, u)

    def group(index, block, col, tiles):
        acc = jnp.zeros((ROWS, LANES), jnp.float32)
        for k in range(GROUP):
            new = update(index + k, *tiles[k : k + 5])
            result[rows_of(index + k), :] = new
            acc = jnp.where(quad == col + k, strip_of(new, col + k), acc)
        rows = rows_of(block)
        mine = jnp.logical_and(quad >= col, quad < col + GROUP)
        strips[rows, :] = jnp.where(mine, acc, strips[rows, :])

    strips[...] = jnp.zeros(strips.shape, jnp.float32)
    for index in (0, lon_cells - GROUP):
        group(index, index // 32, index % 32, [at(u) for u in range(index - 2, index + GROUP + 2)])

    def body(number, carry):
        index = number * GROUP
        tiles = [tile(field, index + k) for k in range(-2, GROUP + 2)]
        group(index, lax.shift_right_logical(index, 5), lax.bitwise_and(index, 31), tiles)
        return carry

    lax.fori_loop(1, lon_cells // GROUP - 1, body, 0)


def rows_kernel(field, src, corners):
    for i, value in enumerate(gather_all(field, src)):
        corners[2 * i * ROWS : 2 * (i + 1) * ROWS, :] = value


def outer_kernel(second, final, lon_cells, consts, *refs):
    refs = list(refs)
    part, part_strips, own_a, own_b, own_strips, lon_a, lon_b, strip_a, strip_b, received, keys, listed, flag, geo = refs[:14]
    refs = refs[14:]
    if final:
        result = refs.pop(0)
    else:
        corners, again, src, table, result, sent, edge_a, edge_b, strips = refs[:9]
        refs = refs[9:]
    ghosts, merged, fixes, sides = refs
    blocks = lon_cells // 32
    fill_ghosts(received, keys, listed, ghosts)
    merge_strips(strip_a, strip_b, flag, ghosts, merged, blocks)

    base = 2 * lon_cells
    sin_t, cos_t, yang, strip_sin, strip_cos = (geo[base + 8 * i : base + 8 * i + 8, :] for i in range(5))
    low = sub_ids() < 4
    lane = lane_ids(8)
    scale = 0.5 if second else 1.0

    values = coefficients(strip_sin, strip_cos, yang, consts)
    quarter = lax.bitwise_and(lane, 3)
    for block in range(blocks):
        at = block * ROWS
        v1 = own_strips[at + 8 : at + 16, :]
        along = jnp.where(low, v1, pltpu.roll(v1, 4, 0)) * values[0]
        for half in range(2):
            rows = slice(at + 8 * half, at + 8 * half + 8)
            outside = merged[rows, :]
            left1, left2 = pltpu.roll(outside, LANES - 1, 1), pltpu.roll(outside, LANES - 2, 1)
            right1, right2 = pltpu.roll(outside, 1, 1), pltpu.roll(outside, 2, 1)
            near = jnp.where(quarter == 1, left1, jnp.where(quarter == 2, right1, 0.0))
            far = jnp.where(quarter < 2, left2, right2)
            first = jnp.where(quarter < 2, 8.0 * near - far, far - 8.0 * near)
            twice = 16.0 * near - far
            fixes[rows, :] = scale * ((values[3 + 6 * half] + along) * first + values[2 + 6 * half] * twice)

    values = coefficients(sin_t, cos_t, yang, consts)
    odd = flag[0] > 0
    west = flag[3] > 0
    for i, row in enumerate((3, 2, 2, 3)):
        came = jnp.where(odd, lon_a[...], lon_b[...]) if i < 2 else jnp.where(odd, lon_b[...], lon_a[...])
        ghost = jnp.where(west if i < 2 else jnp.logical_not(west), ghosts[rows_of(row), :], 0.0)
        sides[rows_of(i), :] = came[rows_of(i % 2)] + ghost
    before2, before1, after1, after2 = (sides[rows_of(i), :] for i in range(4))
    for i, (near, far, sign) in enumerate(
        ((before1, before2, -1.0), (None, before1, -1.0), (None, after1, 1.0), (after1, after2, 1.0))
    ):
        own = jnp.where(odd, own_a[...], own_b[...]) if i < 2 else jnp.where(odd, own_b[...], own_a[...])
        v1 = own[rows_of(i % 2)][8:]
        along = jnp.where(low, pltpu.roll(v1, 4, 0), v1) * values[1]
        first = -far if near is None else 8.0 * near - far
        twice = -far if near is None else 16.0 * near - far
        for half in range(2):
            rows = slice(8 * half, 8 * half + 8)
            change = sign * along * first[rows] + values[4 + 6 * half] * twice[rows]
            sides[i * ROWS + 8 * half : i * ROWS + 8 * half + 8, :] = scale * change

    lane16 = lane_ids(ROWS)
    rim = jnp.logical_or(lane16 < 2, lane16 >= LANES - 2)

    def corrected(u, block, col):
        moved = pltpu.roll(tile(fixes, block), lax.bitwise_and(LANES - 2 - 4 * col, LANES - 1), 1)
        return tile(part, u) + jnp.where(rim, moved, 0.0)

    def store(u, new):
        if final:
            result[pl.ds(u, 8, stride=lon_cells), :] = new[:8]
            result[pl.ds(u + 8 * lon_cells, 8, stride=lon_cells), :] = new[8:]
        else:
            result[rows_of(u), :] = new

    def body(block, carry):
        for col in range(32):
            u = block * 32 + col
            store(u, corrected(u, block, col))
        return carry

    lax.fori_loop(0, blocks, body, 0)
    if not final:
        strips[...] = part_strips[...] + fixes[...]
    quad = lax.shift_right_logical(lane16, 2)
    for i, u in enumerate((0, 1, lon_cells - 2, lon_cells - 1)):
        block, col = divmod(u, 32)
        change = sides[rows_of(i), :]
        store(u, corrected(u, block, col) + change)
        if not final:
            strips[rows_of(block), :] += jnp.where(quad == col, strip_of(change, col), 0.0)
    if final:
        return
    put_edges(result, flag, lon_cells, edge_a, edge_b)

    def repeat(step, accs):
        for k in range(AGAIN):
            at = again[AGAIN * step + k]
            accs = pick(result, src, at, lax.bitwise_and(at, LANES - 1), lax.shift_right_logical(at, 7), accs)
        return accs

    accs = tuple(corners[2 * i * ROWS : 2 * (i + 1) * ROWS, :] for i in range(4))
    steps = (again[again.shape[0] - 1] + AGAIN - 1) // AGAIN
    finish_rows(lax.fori_loop(0, steps, repeat, accs), table, sent)


def seat(block):
    return lax.bitwise_and(block, 15) * 4 + lax.shift_right_logical(block, 4)


def pack_kernel(message, _, buffer, staged, sems):
    target0 = jnp.max(message[32:33, :]).astype(jnp.int32)
    target1 = jnp.max(message[33:34, :]).astype(jnp.int32)
    same = target0 == target1
    slot0, slot1 = message[0:ROWS, :], message[ROWS : 2 * ROWS, :]
    staged[0:ROWS, :] = jnp.where(same, slot0 + slot1, slot0)
    staged[ROWS : 2 * ROWS, :] = slot1
    copies = [
        pltpu.make_async_copy(
            staged.at[pl.ds(at * ROWS, ROWS), :],
            buffer.at[pl.ds(pl.multiple_of(seat(target) * ROWS, ROWS), ROWS), :],
            sems.at[at],
        )
        for at, target in enumerate((target0, target1))
    ]
    copies[0].start()
    pl.when(jnp.logical_not(same))(copies[1].start)
    copies[0].wait()
    pl.when(jnp.logical_not(same))(copies[1].wait)


def crossing(count):
    return [(here, (here ^ FLIP) + count) for here in range(count)] + [(here + count, here ^ FLIP) for here in range(count)]


def pairs(count, first):
    route = []
    for low in range(first, count - 1, 2):
        route += [(low, low + 1), (low + 1, low)]
    return route


def on_device(state, partners, send_counts, source_cells, weights, turn_angles, ghost_slots):
    lat_blocks = lax.axis_size("colat")
    lon_axes = ("lon_hi", "core")
    lon_blocks = lax.axis_size(lon_axes)
    peers = lat_blocks * lon_blocks
    lon_cells, lat_cells = state.shape[3], state.shape[4]
    consts = constants(lat_cells * lat_blocks, lon_cells * lon_blocks)
    core = lax.axis_index("core")
    colat = lax.axis_index("colat")
    lon = lax.axis_index(lon_axes)
    yang = lax.axis_index("panel").astype(jnp.float32)
    flag = jnp.stack([lon % 2, colat % 2, colat == 0, lon == 0]).astype(jnp.int32)

    src = source_cells[0, 0, 0]
    theta = ((colat * lat_cells + jnp.arange(lat_cells, dtype=jnp.int32)).astype(jnp.float32) + 0.5) * consts[0] + 0.25 * math.pi
    rim_lat = (jnp.arange(LANES, dtype=jnp.int32) + 2) % 4 + jnp.where(jnp.arange(LANES, dtype=jnp.int32) % 4 < 2, lat_cells - 4, 0)
    rim_theta = ((colat * lat_cells + rim_lat).astype(jnp.float32) + 0.5) * consts[0] + 0.25 * math.pi
    phi = ((lon * lon_cells + jnp.arange(lon_cells, dtype=jnp.int32)).astype(jnp.float32) + 0.5) * consts[1] - 0.75 * math.pi
    geo = jnp.concatenate(
        [
            jnp.broadcast_to((yang * jnp.sin(phi))[:, None], (lon_cells, LANES)),
            jnp.broadcast_to((yang * jnp.cos(phi))[:, None], (lon_cells, LANES)),
            jnp.broadcast_to(jnp.sin(theta)[None], (8, LANES)),
            jnp.broadcast_to(jnp.cos(theta)[None], (8, LANES)),
            jnp.broadcast_to(yang, (8, LANES)),
            jnp.broadcast_to(jnp.sin(rim_theta)[None], (8, LANES)),
            jnp.broadcast_to(jnp.cos(rim_theta)[None], (8, LANES)),
        ]
    )
    slot = ghost_slots[0, 0, 0]
    pole = slot[: 4 * lon_cells].reshape(2, 2, lon_cells)
    pole = jnp.pad(jnp.maximum(pole[0], pole[1]), ((0, 0), (0, LANES - lon_cells)), constant_values=-1)
    side = slot[4 * lon_cells :].reshape(2, 2, LANES)
    slots = jnp.concatenate([pole, jnp.maximum(side[0], side[1]), jnp.full((4, LANES), -1, jnp.int32)])

    vmem = pl.BlockSpec(memory_space=pltpu.VMEM)
    smem = pl.BlockSpec(memory_space=pltpu.SMEM)

    def f32(*shape):
        return jax.ShapeDtypeStruct(shape, jnp.float32)

    cells = lon_cells * ROWS
    strip_rows = lon_cells // 32 * ROWS
    moving = [f32(cells, LANES), f32(40, LANES), f32(32, LANES), f32(32, LANES), f32(strip_rows, LANES)]
    params = pltpu.CompilerParams(vmem_limit_bytes=16 * 1024 * 1024)

    keys, listed = pl.pallas_call(
        key_kernel,
        out_shape=[f32(8, LANES), jax.ShapeDtypeStruct((16, LANES), jnp.int32)],
        in_specs=[vmem],
        out_specs=[vmem, vmem],
        compiler_params=params,
    )(slots)

    hbm = pl.BlockSpec(memory_space=pltpu.HBM)
    field, edge_a, edge_b, strips, buffer, sent, table, again = pl.pallas_call(
        functools.partial(start_kernel, lon_cells),
        out_shape=[moving[0], moving[2], moving[3], moving[4], f32(peers * ROWS, LANES), moving[1], f32(24, LANES)]
        + [jax.ShapeDtypeStruct((2 * LANES + 16,), jnp.int32)],
        in_specs=[vmem, smem, smem, smem, vmem, vmem, smem],
        out_specs=[vmem] * 4 + [hbm] + [vmem] * 2 + [smem],
        scratch_shapes=[
            pltpu.VMEM((LANES, LANES), jnp.float32),
            pltpu.SemaphoreType.DMA((peers * ROWS // LANES,)),
        ],
        compiler_params=params,
    )(
        state.reshape(cells, LANES),
        src,
        send_counts[0, 0, 0],
        partners[0, 0, 0],
        weights.reshape(8, LANES),
        turn_angles.reshape(2, LANES),
        flag,
    )

    origin = field
    for number in range(2 * STEPS):
        second = number % 2 == 1
        final = number == 2 * STEPS - 1
        over = lax.ppermute(sent, ("panel",) + lon_axes, crossing(lon_blocks))
        operands = [field] + ([origin] if second else []) + [geo]
        part, part_strips = pl.pallas_call(
            functools.partial(inner_kernel, second, lon_cells, consts),
            out_shape=[moving[0], moving[4]],
            in_specs=[vmem] * len(operands),
            out_specs=[vmem, vmem],
            scratch_shapes=[pltpu.VMEM((8 * 23, LANES), jnp.float32)],
            compiler_params=params,
            cost_estimate=pl.CostEstimate(flops=20_000_000, bytes_accessed=1 << 23, transcendentals=0),
        )(*operands)
        lon_a = lax.ppermute(edge_a, lon_axes, pairs(lon_blocks, 0))
        over, part, part_strips, lon_a = lax.optimization_barrier((over, part, part_strips, lon_a))
        buffer = pl.pallas_call(
            pack_kernel,
            out_shape=f32(peers * ROWS, LANES),
            in_specs=[vmem, hbm],
            out_specs=hbm,
            scratch_shapes=[pltpu.VMEM((2 * ROWS, LANES), jnp.float32), pltpu.SemaphoreType.DMA((2,))],
            input_output_aliases={1: 0},
            compiler_params=params,
        )(over, buffer)
        buffer, own_a, own_b, own_strips, part = lax.optimization_barrier((buffer, edge_a, edge_b, strips, part))
        received = lax.all_to_all(
            buffer.reshape(peers, ROWS, LANES), ("lon_hi", "core", "colat"), split_axis=0, concat_axis=0, tiled=True
        ).reshape(peers * ROWS, LANES)
        if not final:
            corners = pl.pallas_call(
                rows_kernel,
                out_shape=f32(8 * ROWS, LANES),
                in_specs=[vmem, smem],
                out_specs=vmem,
                compiler_params=params,
                cost_estimate=pl.CostEstimate(flops=8_000_000, bytes_accessed=1 << 22, transcendentals=0),
            )(part, src)
        lon_b = lax.ppermute(own_b, lon_axes, pairs(lon_blocks, 1))
        strip_a = lax.ppermute(own_strips, "colat", pairs(lat_blocks, 0))
        strip_b = lax.ppermute(own_strips, "colat", pairs(lat_blocks, 1))
        operands = [part, part_strips, own_a, own_b, own_strips, lon_a, lon_b, strip_a, strip_b, received, keys, listed, flag, geo]
        specs = [vmem] * 11 + [smem, smem, vmem]
        if not final:
            operands += [corners, again, src, table]
            specs += [vmem, smem, smem, vmem]
        out = pl.pallas_call(
            functools.partial(outer_kernel, second, final, lon_cells, consts),
            out_shape=moving[:1] if final else moving,
            in_specs=specs,
            out_specs=[vmem] * (1 if final else 5),
            scratch_shapes=[
                pltpu.VMEM((4 * ROWS, LANES), jnp.float32),
                pltpu.VMEM((strip_rows, LANES), jnp.float32),
                pltpu.VMEM((strip_rows, LANES), jnp.float32),
                pltpu.VMEM((4 * ROWS, LANES), jnp.float32),
            ],
            compiler_params=params,
        )(*operands)
        if final:
            return out[0].reshape(state.shape)
        field, sent, edge_a, edge_b, strips = out
        if second:
            origin = field


def solution(mesh):
    lon = mesh.shape["lon"]
    fine = Mesh(
        mesh.devices.reshape(mesh.shape["panel"], mesh.shape["colat"], lon // 2, 2), ("panel", "colat", "lon_hi", "core")
    )
    lon_axes = ("lon_hi", "core")
    table = P("panel", "colat", lon_axes, None)
    in_specs = (
        P(None, "panel", None, lon_axes, "colat"),
        table,
        table,
        table,
        P(None, "panel", "colat", lon_axes, None),
        table,
        table,
    )
    out_specs = P(None, "panel", None, lon_axes, "colat")
    return jax.shard_map(on_device, mesh=fine, in_specs=in_specs, out_specs=out_specs, check_vma=False)
```

```python
import functools
import math

import jax
import jax.numpy as jnp
import numpy as np
from jax import lax
from jax.experimental import pallas as pl
from jax.experimental.pallas import tpu as pltpu
from jax.sharding import Mesh, PartitionSpec as P

STEPS = 2
R_LOW = 0.7
HALF_ROOT = 0.7071067811865476
LANES = 128
ROWS = 16
NO_KEY = 1.0e9
AGAIN = 16
GROUP = 8
FLIP = 3


def constants(lat_total, lon_total):
    d_theta = 0.5 * math.pi / lat_total
    d_phi = 1.5 * math.pi / lon_total
    spacing = R_LOW * min(d_theta, HALF_ROOT * d_phi)
    time_step = 0.25 * spacing
    kappa = 0.04 * spacing * spacing / time_step
    viscous = 0.06 * spacing * spacing / time_step
    return (
        d_theta,
        d_phi,
        time_step,
        kappa,
        viscous,
        0.05 / time_step,
        0.2 / time_step,
        4.0 * spacing,
    )


def lane_ids(rows):
    return lax.broadcasted_iota(jnp.int32, (rows, LANES), 1)


def sub_ids():
    return lax.broadcasted_iota(jnp.int32, (8, LANES), 0)


def rows_of(u):
    if isinstance(u, int):
        return slice(u * ROWS, (u + 1) * ROWS)
    return pl.ds(pl.multiple_of(u * ROWS, ROWS), ROWS)


def tile(ref, u):
    return ref[rows_of(u), :]


def pick(field, src, at, m, slot, accs):
    lane = lane_ids(8)
    cell = src[at]
    lon = lax.shift_right_logical(cell, 7)
    lat = lax.bitwise_and(cell, LANES - 1)
    both = field[pl.ds(pl.multiple_of(lon * ROWS, ROWS), 2 * ROWS), :]
    near = pltpu.roll(both, lax.bitwise_and(m - lat + LANES, LANES - 1), 1)
    accs = list(accs)
    if isinstance(slot, int):
        columns = [(2 * slot, near, lane == m), (2 * slot + 1, near, lane == lax.bitwise_and(m + 1, LANES - 1))]
    else:
        far = pltpu.roll(both, lax.bitwise_and(m - lat + LANES - 1, LANES - 1), 1)
        columns = []
        for number in range(2):
            mask = lane == jnp.where(slot == number, m, 2 * LANES)
            columns += [(2 * number, near, mask), (2 * number + 1, far, mask)]
    for number, column, mask in columns:
        old = accs[number]
        rows = [jnp.where(mask, column[8 * i : 8 * i + 8], old[8 * i : 8 * i + 8]) for i in range(4)]
        accs[number] = jnp.concatenate(rows, axis=0)
    return tuple(accs)


def gather_all(field, src, lon_cells=0, listed=None):
    def note(at, count):
        if listed is None:
            return count
        cell = src[at]
        lon = lax.shift_right_logical(cell, 7)
        lat = lax.bitwise_and(cell, LANES - 1)
        low = jnp.logical_or(lat < 2, lon < 2)
        high = jnp.logical_or(lat >= LANES - 3, lon >= lon_cells - 3)
        listed[count] = at
        return count + jnp.logical_or(low, high).astype(jnp.int32)

    def body(m, carry):
        count, accs = carry
        accs = pick(field, src, m, m, 0, accs)
        count = note(m, count)
        accs = pick(field, src, LANES + m, m, 1, accs)
        count = note(LANES + m, count)
        return count, accs

    zero = jnp.zeros((2 * ROWS, LANES), jnp.float32)
    count, accs = lax.fori_loop(0, LANES, body, (jnp.int32(0), (zero, zero, zero, zero)), unroll=32)
    if listed is not None:
        for k in range(AGAIN):
            listed[count + k] = 0
        listed[listed.shape[0] - 1] = count
    near0, far0, near1, far1 = accs
    return near0, pltpu.roll(far0, LANES - 1, 1), near1, pltpu.roll(far1, LANES - 1, 1)


def finish_rows(accs, table, sent):
    sub = sub_ids()
    for slot in range(2):
        near, far = accs[2 * slot], accs[2 * slot + 1]
        base = slot * 8
        w0 = table[base : base + 1, :]
        w1 = table[base + 1 : base + 2, :]
        w2 = table[base + 2 : base + 3, :]
        w3 = table[base + 3 : base + 4, :]
        value = w0 * near[:ROWS] + w1 * far[:ROWS] + w2 * near[ROWS:] + w3 * far[ROWS:]
        low, high = value[:8], value[8:]
        cosine = table[base + 4 : base + 5, :]
        sine = table[base + 5 : base + 6, :]
        turned = cosine * high + jnp.where(sub < 4, sine, -sine) * pltpu.roll(high, 4, 0)
        sent[slot * ROWS : slot * ROWS + 8, :] = low
        sent[slot * ROWS + 8 : slot * ROWS + 16, :] = turned
    sent[32:40, :] = table[16:24, :]


def put_edges(field, flag, lon_cells, edge_a, edge_b):
    first = field[0 : 2 * ROWS, :]
    last = field[(lon_cells - 2) * ROWS : lon_cells * ROWS, :]
    odd = flag[0] > 0
    edge_a[...] = jnp.where(odd, first, last)
    edge_b[...] = jnp.where(odd, last, first)


def strip_of(value, col):
    return pltpu.roll(value, 4 * col + 2, 1)


def start_kernel(
    lon_cells, state, src, counts, names, weights, turn, flag,
    field, edge_a, edge_b, strips, buffer, sent, table, listed, zeros, sems
):
    blocks = lon_cells // 32
    zeros[...] = jnp.zeros(zeros.shape, jnp.float32)
    count = zeros.shape[0]
    clears = []
    for number in range(buffer.shape[0] // count):
        copy = pltpu.make_async_copy(zeros, buffer.at[pl.ds(number * count, count), :], sems.at[number])
        copy.start()
        clears.append(copy)
    lane = lane_ids(ROWS)
    quad = lax.shift_right_logical(lane, 2)
    for block in range(blocks):
        acc = jnp.zeros((ROWS, LANES), jnp.float32)
        for col in range(32):
            u = block * 32 + col
            low = state[pl.ds(u, 8, stride=lon_cells), :]
            high = state[pl.ds(u + 8 * lon_cells, 8, stride=lon_cells), :]
            value = jnp.concatenate([low, high], axis=0)
            field[rows_of(u), :] = value
            acc = jnp.where(quad == col, strip_of(value, col), acc)
        strips[block * ROWS : (block + 1) * ROWS, :] = acc
    put_edges(field, flag, lon_cells, edge_a, edge_b)
    row = lane_ids(1)
    table[...] = jnp.zeros(table.shape, jnp.float32)
    angle = turn[...]
    cosine, sine = jnp.cos(angle), jnp.sin(angle)
    for slot in range(2):
        for corner in range(4):
            value = weights[2 * corner + slot : 2 * corner + slot + 1, :]
            table[8 * slot + corner : 8 * slot + corner + 1, :] = jnp.where(row < counts[slot], value, 0.0)
        table[8 * slot + 4 : 8 * slot + 5, :] = cosine[slot : slot + 1]
        table[8 * slot + 5 : 8 * slot + 6, :] = sine[slot : slot + 1]
        table[16 + slot : 17 + slot, :] = jnp.full((1, LANES), names[slot], jnp.int32).astype(jnp.float32)
    finish_rows(gather_all(field, src, lon_cells, listed), table, sent)
    for copy in clears:
        copy.wait()


def key_kernel(slots, keys, listed):
    lane = lane_ids(8)
    slot = slots[...]
    peer = seat(lax.bitwise_xor(lax.shift_right_logical(jnp.maximum(slot, 0), 7), FLIP))
    shift = lax.bitwise_and(slot - lane, LANES - 1)
    key = jnp.where(slot >= 0, (peer * LANES + shift).astype(jnp.float32), NO_KEY)
    keys[...] = key

    def cond(carry):
        count, more = carry[0], carry[1]
        return jnp.logical_and(count < LANES, more > 0)

    def body(carry):
        count, _, last, found, total = carry
        now = jnp.min(jnp.where(key > last, key, NO_KEY), axis=1, keepdims=True)
        now = jnp.broadcast_to(now, (8, LANES))
        hit = now < NO_KEY
        more = (jnp.min(now) < NO_KEY).astype(jnp.int32)
        found = jnp.where(lane == count, jnp.where(hit, now, -1.0), found)
        total = total + more.astype(jnp.float32)
        return count + 1, more, now, found, total

    zero = jnp.zeros((8, LANES), jnp.float32)
    out = lax.while_loop(cond, body, (jnp.int32(0), jnp.int32(1), zero - 1.0, zero - 1.0, zero))
    listed[0:8, :] = out[3].astype(jnp.int32)
    listed[8:16, :] = out[4].astype(jnp.int32)


def fill_ghosts(received, keys, listed, ghosts):
    def body(step, accs):
        accs = list(accs)
        for row in range(4):
            for i in (2 * step, 2 * step + 1):
                key = listed[row, i]
                known = jnp.maximum(key, 0)
                peer = lax.shift_right_logical(known, 7)
                shift = lax.bitwise_and(known, LANES - 1)
                value = pltpu.roll(tile(received, peer), lax.bitwise_and(LANES - shift, LANES - 1), 1)
                accs[row] = jnp.where(keys[row : row + 1, :] == key.astype(jnp.float32), value, accs[row])
        return tuple(accs)

    zero = jnp.zeros((ROWS, LANES), jnp.float32)
    accs = lax.fori_loop(0, lax.shift_right_logical(listed[8, 0] + 1, 1), body, (zero, zero, zero, zero))
    for row in range(4):
        ghosts[row * ROWS : (row + 1) * ROWS, :] = accs[row]


def merge_strips(strip_a, strip_b, flag, ghosts, merged, blocks):
    lane = lane_ids(8)
    part = lax.bitwise_and(lane, 3)
    odd = flag[1] > 0
    north = flag[2] > 0
    first = part == jnp.where(north, 1, 2)
    second = part == jnp.where(north, 0, 3)
    for block in range(blocks):
        spread = lax.shift_right_logical(lane, 2) + 32 * block
        for half in range(2):
            at = block * ROWS + half * 8
            a = strip_a[at : at + 8, :]
            b = strip_b[at : at + 8, :]
            value = jnp.where(part < 2, jnp.where(odd, a, b), jnp.where(odd, b, a))
            wide0 = jnp.take_along_axis(ghosts[half * 8 : half * 8 + 8, :], spread, axis=1)
            wide1 = jnp.take_along_axis(ghosts[ROWS + half * 8 : ROWS + half * 8 + 8, :], spread, axis=1)
            merged[at : at + 8, :] = value + jnp.where(first, wide0, jnp.where(second, wide1, 0.0))


def coefficients(sin_t, cos_t, yang, consts):
    d_theta, d_phi, step, kappa, viscous, omega, buoyancy, radial = consts
    sub = sub_ids()
    low = sub < 4
    level = lax.bitwise_and(sub, 3).astype(jnp.float32)
    inverse = 1.0 / (level * radial + R_LOW)
    keep = 1.0 - yang
    over_sin = 1.0 / sin_t
    square = inverse * inverse
    advect_t = -step / (12.0 * d_theta) * inverse
    advect_p = -step / (12.0 * d_phi) * inverse * over_sin
    values = [advect_t, advect_p]
    for half in range(2):
        spread = jnp.where(low, step * kappa, step * viscous) if half == 0 else jnp.full((8, LANES), step * viscous)
        second_t = spread * square / (12.0 * d_theta * d_theta)
        first_t = spread * square * (cos_t * over_sin) / (12.0 * d_theta)
        second_p = spread * square * (over_sin * over_sin) / (12.0 * d_phi * d_phi)
        second_r = spread / (radial * radial)
        first_r = spread * inverse / radial
        middle = -30.0 * second_t - 30.0 * second_p - 2.0 * second_r
        values += [second_t, first_t, second_p, second_r, first_r, middle]
    twice = 2.0 * step * omega
    zero = jnp.zeros((8, LANES), jnp.float32)
    sign = jnp.where(low, 1.0, -1.0)
    values += [
        jnp.where(low, 0.0, step * buoyancy),
        jnp.where(low, zero, twice * keep * sin_t),
        jnp.where(low, zero, -twice * cos_t),
        jnp.where(low, 0.0, twice) + zero,
        sign * twice * keep * cos_t,
        sign * twice * sin_t,
        jnp.where(low, zero, -twice * keep * sin_t),
        jnp.where(low, zero, twice * cos_t),
        jnp.where(low, -twice, 0.0) + zero,
    ]
    return values


def inner_kernel(second, lon_cells, consts, *refs):
    refs = list(refs)
    field = refs.pop(0)
    origin = refs.pop(0) if second else None
    geo, result, strips, coef = refs
    base = 2 * lon_cells
    sin_t, cos_t, yang = (geo[base + 8 * i : base + 8 * i + 8, :] for i in range(3))
    for i, value in enumerate(coefficients(sin_t, cos_t, yang, consts)):
        coef[8 * i : 8 * i + 8, :] = value
    radial = consts[7]
    lane16 = lane_ids(ROWS)
    quad = lax.shift_right_logical(lane16, 2)
    sub = sub_ids()
    low = sub < 4
    level = lax.bitwise_and(sub, 3)
    top = level == 3
    bottom = level == 0
    advect_r = -consts[2] / (2.0 * radial)

    def c(i):
        return coef[8 * i : 8 * i + 8, :]

    def update(u, down2, down1, here, up1, up2):
        south1 = jnp.where(lane16 >= 1, pltpu.roll(here, 1, 1), 0.0)
        south2 = jnp.where(lane16 >= 2, pltpu.roll(here, 2, 1), 0.0)
        north1 = jnp.where(lane16 < LANES - 1, pltpu.roll(here, LANES - 1, 1), 0.0)
        north2 = jnp.where(lane16 < LANES - 2, pltpu.roll(here, LANES - 2, 1), 0.0)
        lat_odd = 8.0 * (north1 - south1) - (north2 - south2)
        lat_even = 16.0 * (north1 + south1) - (north2 + south2)
        lon_odd = 8.0 * (up1 - down1) - (up2 - down2)
        lon_even = 16.0 * (up1 + down1) - (up2 + down2)
        v0, v1 = here[:8], here[8:]
        r0, r1 = pltpu.roll(v0, 4, 0), pltpu.roll(v1, 4, 0)
        vel_r = jnp.where(low, r0, v0)
        vel_t = jnp.where(low, v1, r1)
        vel_p = jnp.where(low, r1, v1)
        along_t = vel_t * c(0)
        along_p = vel_p * c(1)
        along_r = vel_r * advect_r
        sin_p = geo[pl.ds(u, 1), :]
        cos_p = geo[pl.ds(lon_cells + u, 1), :]
        turn0 = c(14) * r0 + (c(15) + c(16) * sin_p) * vel_p + (c(17) * cos_p) * vel_t
        turn1 = (c(18) + c(19) * sin_p) * r1 + (c(20) + c(21) * sin_p + c(22) * cos_p) * vel_r
        out = []
        for half, value, turn in ((0, v0, turn0), (1, v1, turn1)):
            at = 2 + 6 * half
            part = slice(8 * half, 8 * half + 8)
            above = jnp.where(top, value, pltpu.roll(value, 7, 0))
            below = jnp.where(bottom, value, pltpu.roll(value, 1, 0))
            change = (
                (c(at + 1) + along_t) * lat_odd[part]
                + c(at) * lat_even[part]
                + along_p * lon_odd[part]
                + c(at + 2) * lon_even[part]
                + (c(at + 4) + along_r) * (above - below)
                + c(at + 3) * (above + below)
                + c(at + 5) * value
                + turn
            )
            out.append(value + change)
        new = jnp.concatenate(out, axis=0)
        if second:
            new = 0.5 * (tile(origin, u) + new)
        return new

    def at(u):
        if u < 0 or u >= lon_cells:
            return jnp.zeros((ROWS, LANES), jnp.float32)
        return tile(field, u)

    def group(index, block, col, tiles):
        acc = jnp.zeros((ROWS, LANES), jnp.float32)
        for k in range(GROUP):
            new = update(index + k, *tiles[k : k + 5])
            result[rows_of(index + k), :] = new
            acc = jnp.where(quad == col + k, strip_of(new, col + k), acc)
        rows = rows_of(block)
        mine = jnp.logical_and(quad >= col, quad < col + GROUP)
        strips[rows, :] = jnp.where(mine, acc, strips[rows, :])

    strips[...] = jnp.zeros(strips.shape, jnp.float32)
    for index in (0, lon_cells - GROUP):
        group(index, index // 32, index % 32, [at(u) for u in range(index - 2, index + GROUP + 2)])

    def body(number, carry):
        index = number * GROUP
        tiles = [tile(field, index + k) for k in range(-2, GROUP + 2)]
        group(index, lax.shift_right_logical(index, 5), lax.bitwise_and(index, 31), tiles)
        return carry

    lax.fori_loop(1, lon_cells // GROUP - 1, body, 0)


def rows_kernel(field, src, corners):
    for i, value in enumerate(gather_all(field, src)):
        corners[2 * i * ROWS : 2 * (i + 1) * ROWS, :] = value


def outer_kernel(second, final, lon_cells, consts, *refs):
    refs = list(refs)
    part, part_strips, own_a, own_b, own_strips, lon_a, lon_b, strip_a, strip_b, received, keys, listed, flag, geo = refs[:14]
    refs = refs[14:]
    if final:
        result = refs.pop(0)
    else:
        corners, again, src, table, result, sent, edge_a, edge_b, strips = refs[:9]
        refs = refs[9:]
    ghosts, merged, fixes, sides = refs
    blocks = lon_cells // 32
    fill_ghosts(received, keys, listed, ghosts)
    merge_strips(strip_a, strip_b, flag, ghosts, merged, blocks)

    base = 2 * lon_cells
    sin_t, cos_t, yang, strip_sin, strip_cos = (geo[base + 8 * i : base + 8 * i + 8, :] for i in range(5))
    low = sub_ids() < 4
    lane = lane_ids(8)
    scale = 0.5 if second else 1.0

    values = coefficients(strip_sin, strip_cos, yang, consts)
    quarter = lax.bitwise_and(lane, 3)
    for block in range(blocks):
        at = block * ROWS
        v1 = own_strips[at + 8 : at + 16, :]
        along = jnp.where(low, v1, pltpu.roll(v1, 4, 0)) * values[0]
        for half in range(2):
            rows = slice(at + 8 * half, at + 8 * half + 8)
            outside = merged[rows, :]
            left1, left2 = pltpu.roll(outside, LANES - 1, 1), pltpu.roll(outside, LANES - 2, 1)
            right1, right2 = pltpu.roll(outside, 1, 1), pltpu.roll(outside, 2, 1)
            near = jnp.where(quarter == 1, left1, jnp.where(quarter == 2, right1, 0.0))
            far = jnp.where(quarter < 2, left2, right2)
            first = jnp.where(quarter < 2, 8.0 * near - far, far - 8.0 * near)
            twice = 16.0 * near - far
            fixes[rows, :] = scale * ((values[3 + 6 * half] + along) * first + values[2 + 6 * half] * twice)

    values = coefficients(sin_t, cos_t, yang, consts)
    odd = flag[0] > 0
    west = flag[3] > 0
    for i, row in enumerate((3, 2, 2, 3)):
        came = jnp.where(odd, lon_a[...], lon_b[...]) if i < 2 else jnp.where(odd, lon_b[...], lon_a[...])
        ghost = jnp.where(west if i < 2 else jnp.logical_not(west), ghosts[rows_of(row), :], 0.0)
        sides[rows_of(i), :] = came[rows_of(i % 2)] + ghost
    before2, before1, after1, after2 = (sides[rows_of(i), :] for i in range(4))
    for i, (near, far, sign) in enumerate(
        ((before1, before2, -1.0), (None, before1, -1.0), (None, after1, 1.0), (after1, after2, 1.0))
    ):
        own = jnp.where(odd, own_a[...], own_b[...]) if i < 2 else jnp.where(odd, own_b[...], own_a[...])
        v1 = own[rows_of(i % 2)][8:]
        along = jnp.where(low, pltpu.roll(v1, 4, 0), v1) * values[1]
        first = -far if near is None else 8.0 * near - far
        twice = -far if near is None else 16.0 * near - far
        for half in range(2):
            rows = slice(8 * half, 8 * half + 8)
            change = sign * along * first[rows] + values[4 + 6 * half] * twice[rows]
            sides[i * ROWS + 8 * half : i * ROWS + 8 * half + 8, :] = scale * change

    lane16 = lane_ids(ROWS)
    rim = jnp.logical_or(lane16 < 2, lane16 >= LANES - 2)

    def corrected(u, block, col):
        moved = pltpu.roll(tile(fixes, block), lax.bitwise_and(LANES - 2 - 4 * col, LANES - 1), 1)
        return tile(part, u) + jnp.where(rim, moved, 0.0)

    def store(u, new):
        if final:
            result[pl.ds(u, 8, stride=lon_cells), :] = new[:8]
            result[pl.ds(u + 8 * lon_cells, 8, stride=lon_cells), :] = new[8:]
        else:
            result[rows_of(u), :] = new

    def body(block, carry):
        for col in range(32):
            u = block * 32 + col
            store(u, corrected(u, block, col))
        return carry

    lax.fori_loop(0, blocks, body, 0)
    if not final:
        strips[...] = part_strips[...] + fixes[...]
    quad = lax.shift_right_logical(lane16, 2)
    for i, u in enumerate((0, 1, lon_cells - 2, lon_cells - 1)):
        block, col = divmod(u, 32)
        change = sides[rows_of(i), :]
        store(u, corrected(u, block, col) + change)
        if not final:
            strips[rows_of(block), :] += jnp.where(quad == col, strip_of(change, col), 0.0)
    if final:
        return
    put_edges(result, flag, lon_cells, edge_a, edge_b)

    def repeat(step, accs):
        for k in range(AGAIN):
            at = again[AGAIN * step + k]
            accs = pick(result, src, at, lax.bitwise_and(at, LANES - 1), lax.shift_right_logical(at, 7), accs)
        return accs

    accs = tuple(corners[2 * i * ROWS : 2 * (i + 1) * ROWS, :] for i in range(4))
    steps = (again[again.shape[0] - 1] + AGAIN - 1) // AGAIN
    finish_rows(lax.fori_loop(0, steps, repeat, accs), table, sent)


def seat(block):
    return lax.bitwise_and(block, 1) * 32 + lax.bitwise_and(lax.shift_right_logical(block, 1), 7) * 4 + lax.shift_right_logical(block, 4)


def pack_kernel(message, _, buffer, staged, sems):
    target0 = jnp.max(message[32:33, :]).astype(jnp.int32)
    target1 = jnp.max(message[33:34, :]).astype(jnp.int32)
    same = target0 == target1
    slot0, slot1 = message[0:ROWS, :], message[ROWS : 2 * ROWS, :]
    staged[0:ROWS, :] = jnp.where(same, slot0 + slot1, slot0)
    staged[ROWS : 2 * ROWS, :] = slot1
    copies = [
        pltpu.make_async_copy(
            staged.at[pl.ds(at * ROWS, ROWS), :],
            buffer.at[pl.ds(pl.multiple_of(seat(target) * ROWS, ROWS), ROWS), :],
            sems.at[at],
        )
        for at, target in enumerate((target0, target1))
    ]
    copies[0].start()
    pl.when(jnp.logical_not(same))(copies[1].start)
    copies[0].wait()
    pl.when(jnp.logical_not(same))(copies[1].wait)


def crossing(count):
    return [(here, (here ^ FLIP) + count) for here in range(count)] + [(here + count, here ^ FLIP) for here in range(count)]


def pairs(count, first):
    route = []
    for low in range(first, count - 1, 2):
        route += [(low, low + 1), (low + 1, low)]
    return route


def on_device(state, partners, send_counts, source_cells, weights, turn_angles, ghost_slots):
    lat_blocks = lax.axis_size("colat")
    lon_axes = ("lon_hi", "core")
    lon_blocks = lax.axis_size(lon_axes)
    peers = lat_blocks * lon_blocks
    lon_cells, lat_cells = state.shape[3], state.shape[4]
    consts = constants(lat_cells * lat_blocks, lon_cells * lon_blocks)
    core = lax.axis_index("core")
    colat = lax.axis_index("colat")
    lon = lax.axis_index(lon_axes)
    yang = lax.axis_index("panel").astype(jnp.float32)
    flag = jnp.stack([lon % 2, colat % 2, colat == 0, lon == 0]).astype(jnp.int32)

    src = source_cells[0, 0, 0]
    theta = ((colat * lat_cells + jnp.arange(lat_cells, dtype=jnp.int32)).astype(jnp.float32) + 0.5) * consts[0] + 0.25 * math.pi
    rim_lat = (jnp.arange(LANES, dtype=jnp.int32) + 2) % 4 + jnp.where(jnp.arange(LANES, dtype=jnp.int32) % 4 < 2, lat_cells - 4, 0)
    rim_theta = ((colat * lat_cells + rim_lat).astype(jnp.float32) + 0.5) * consts[0] + 0.25 * math.pi
    phi = ((lon * lon_cells + jnp.arange(lon_cells, dtype=jnp.int32)).astype(jnp.float32) + 0.5) * consts[1] - 0.75 * math.pi
    geo = jnp.concatenate(
        [
            jnp.broadcast_to((yang * jnp.sin(phi))[:, None], (lon_cells, LANES)),
            jnp.broadcast_to((yang * jnp.cos(phi))[:, None], (lon_cells, LANES)),
            jnp.broadcast_to(jnp.sin(theta)[None], (8, LANES)),
            jnp.broadcast_to(jnp.cos(theta)[None], (8, LANES)),
            jnp.broadcast_to(yang, (8, LANES)),
            jnp.broadcast_to(jnp.sin(rim_theta)[None], (8, LANES)),
            jnp.broadcast_to(jnp.cos(rim_theta)[None], (8, LANES)),
        ]
    )
    slot = ghost_slots[0, 0, 0]
    pole = slot[: 4 * lon_cells].reshape(2, 2, lon_cells)
    pole = jnp.pad(jnp.maximum(pole[0], pole[1]), ((0, 0), (0, LANES - lon_cells)), constant_values=-1)
    side = slot[4 * lon_cells :].reshape(2, 2, LANES)
    slots = jnp.concatenate([pole, jnp.maximum(side[0], side[1]), jnp.full((4, LANES), -1, jnp.int32)])

    vmem = pl.BlockSpec(memory_space=pltpu.VMEM)
    smem = pl.BlockSpec(memory_space=pltpu.SMEM)

    def f32(*shape):
        return jax.ShapeDtypeStruct(shape, jnp.float32)

    cells = lon_cells * ROWS
    strip_rows = lon_cells // 32 * ROWS
    moving = [f32(cells, LANES), f32(40, LANES), f32(32, LANES), f32(32, LANES), f32(strip_rows, LANES)]
    params = pltpu.CompilerParams(vmem_limit_bytes=16 * 1024 * 1024)

    keys, listed = pl.pallas_call(
        key_kernel,
        out_shape=[f32(8, LANES), jax.ShapeDtypeStruct((16, LANES), jnp.int32)],
        in_specs=[vmem],
        out_specs=[vmem, vmem],
        compiler_params=params,
    )(slots)

    hbm = pl.BlockSpec(memory_space=pltpu.HBM)
    field, edge_a, edge_b, strips, buffer, sent, table, again = pl.pallas_call(
        functools.partial(start_kernel, lon_cells),
        out_shape=[moving[0], moving[2], moving[3], moving[4], f32(peers * ROWS, LANES), moving[1], f32(24, LANES)]
        + [jax.ShapeDtypeStruct((2 * LANES + 16,), jnp.int32)],
        in_specs=[vmem, smem, smem, smem, vmem, vmem, smem],
        out_specs=[vmem] * 4 + [hbm] + [vmem] * 2 + [smem],
        scratch_shapes=[
            pltpu.VMEM((LANES, LANES), jnp.float32),
            pltpu.SemaphoreType.DMA((peers * ROWS // LANES,)),
        ],
        compiler_params=params,
    )(
        state.reshape(cells, LANES),
        src,
        send_counts[0, 0, 0],
        partners[0, 0, 0],
        weights.reshape(8, LANES),
        turn_angles.reshape(2, LANES),
        flag,
    )

    origin = field
    for number in range(2 * STEPS):
        second = number % 2 == 1
        final = number == 2 * STEPS - 1
        over = lax.ppermute(sent, ("panel",) + lon_axes, crossing(lon_blocks))
        operands = [field] + ([origin] if second else []) + [geo]
        part, part_strips = pl.pallas_call(
            functools.partial(inner_kernel, second, lon_cells, consts),
            out_shape=[moving[0], moving[4]],
            in_specs=[vmem] * len(operands),
            out_specs=[vmem, vmem],
            scratch_shapes=[pltpu.VMEM((8 * 23, LANES), jnp.float32)],
            compiler_params=params,
            cost_estimate=pl.CostEstimate(flops=20_000_000, bytes_accessed=1 << 23, transcendentals=0),
        )(*operands)
        lon_a = lax.ppermute(edge_a, lon_axes, pairs(lon_blocks, 0))
        over, part, part_strips, lon_a = lax.optimization_barrier((over, part, part_strips, lon_a))
        buffer = pl.pallas_call(
            pack_kernel,
            out_shape=f32(peers * ROWS, LANES),
            in_specs=[vmem, hbm],
            out_specs=hbm,
            scratch_shapes=[pltpu.VMEM((2 * ROWS, LANES), jnp.float32), pltpu.SemaphoreType.DMA((2,))],
            input_output_aliases={1: 0},
            compiler_params=params,
        )(over, buffer)
        buffer, own_a, own_b, own_strips, part = lax.optimization_barrier((buffer, edge_a, edge_b, strips, part))
        received = lax.all_to_all(
            buffer.reshape(peers, ROWS, LANES), ("core", "lon_hi", "colat"), split_axis=0, concat_axis=0, tiled=True
        ).reshape(peers * ROWS, LANES)
        if not final:
            corners = pl.pallas_call(
                rows_kernel,
                out_shape=f32(8 * ROWS, LANES),
                in_specs=[vmem, smem],
                out_specs=vmem,
                compiler_params=params,
                cost_estimate=pl.CostEstimate(flops=8_000_000, bytes_accessed=1 << 22, transcendentals=0),
            )(part, src)
        lon_b = lax.ppermute(own_b, lon_axes, pairs(lon_blocks, 1))
        strip_a = lax.ppermute(own_strips, "colat", pairs(lat_blocks, 0))
        strip_b = lax.ppermute(own_strips, "colat", pairs(lat_blocks, 1))
        operands = [part, part_strips, own_a, own_b, own_strips, lon_a, lon_b, strip_a, strip_b, received, keys, listed, flag, geo]
        specs = [vmem] * 11 + [smem, smem, vmem]
        if not final:
            operands += [corners, again, src, table]
            specs += [vmem, smem, smem, vmem]
        out = pl.pallas_call(
            functools.partial(outer_kernel, second, final, lon_cells, consts),
            out_shape=moving[:1] if final else moving,
            in_specs=specs,
            out_specs=[vmem] * (1 if final else 5),
            scratch_shapes=[
                pltpu.VMEM((4 * ROWS, LANES), jnp.float32),
                pltpu.VMEM((strip_rows, LANES), jnp.float32),
                pltpu.VMEM((strip_rows, LANES), jnp.float32),
                pltpu.VMEM((4 * ROWS, LANES), jnp.float32),
            ],
            compiler_params=params,
        )(*operands)
        if final:
            return out[0].reshape(state.shape)
        field, sent, edge_a, edge_b, strips = out
        if second:
            origin = field


def solution(mesh):
    lon = mesh.shape["lon"]
    fine = Mesh(
        mesh.devices.reshape(mesh.shape["panel"], mesh.shape["colat"], lon // 2, 2), ("panel", "colat", "lon_hi", "core")
    )
    lon_axes = ("lon_hi", "core")
    table = P("panel", "colat", lon_axes, None)
    in_specs = (
        P(None, "panel", None, lon_axes, "colat"),
        table,
        table,
        table,
        P(None, "panel", "colat", lon_axes, None),
        table,
        table,
    )
    out_specs = P(None, "panel", None, lon_axes, "colat")
    return jax.shard_map(on_device, mesh=fine, in_specs=in_specs, out_specs=out_specs, check_vma=False)
```

```python
import functools
import math

import jax
import jax.numpy as jnp
import numpy as np
from jax import lax
from jax.experimental import pallas as pl
from jax.experimental.pallas import tpu as pltpu
from jax.sharding import Mesh, PartitionSpec as P

STEPS = 2
R_LOW = 0.7
HALF_ROOT = 0.7071067811865476
LANES = 128
ROWS = 16
NO_KEY = 1.0e9
AGAIN = 16
GROUP = 8
FLIP = 3


def constants(lat_total, lon_total):
    d_theta = 0.5 * math.pi / lat_total
    d_phi = 1.5 * math.pi / lon_total
    spacing = R_LOW * min(d_theta, HALF_ROOT * d_phi)
    time_step = 0.25 * spacing
    kappa = 0.04 * spacing * spacing / time_step
    viscous = 0.06 * spacing * spacing / time_step
    return (
        d_theta,
        d_phi,
        time_step,
        kappa,
        viscous,
        0.05 / time_step,
        0.2 / time_step,
        4.0 * spacing,
    )


def lane_ids(rows):
    return lax.broadcasted_iota(jnp.int32, (rows, LANES), 1)


def sub_ids():
    return lax.broadcasted_iota(jnp.int32, (8, LANES), 0)


def rows_of(u):
    if isinstance(u, int):
        return slice(u * ROWS, (u + 1) * ROWS)
    return pl.ds(pl.multiple_of(u * ROWS, ROWS), ROWS)


def tile(ref, u):
    return ref[rows_of(u), :]


def pick(field, src, at, m, slot, accs):
    lane = lane_ids(8)
    cell = src[at]
    lon = lax.shift_right_logical(cell, 7)
    lat = lax.bitwise_and(cell, LANES - 1)
    both = field[pl.ds(pl.multiple_of(lon * ROWS, ROWS), 2 * ROWS), :]
    near = pltpu.roll(both, lax.bitwise_and(m - lat + LANES, LANES - 1), 1)
    accs = list(accs)
    if isinstance(slot, int):
        columns = [(2 * slot, near, lane == m), (2 * slot + 1, near, lane == lax.bitwise_and(m + 1, LANES - 1))]
    else:
        far = pltpu.roll(both, lax.bitwise_and(m - lat + LANES - 1, LANES - 1), 1)
        columns = []
        for number in range(2):
            mask = lane == jnp.where(slot == number, m, 2 * LANES)
            columns += [(2 * number, near, mask), (2 * number + 1, far, mask)]
    for number, column, mask in columns:
        old = accs[number]
        rows = [jnp.where(mask, column[8 * i : 8 * i + 8], old[8 * i : 8 * i + 8]) for i in range(4)]
        accs[number] = jnp.concatenate(rows, axis=0)
    return tuple(accs)


def gather_all(field, src, lon_cells=0, listed=None):
    def note(at, count):
        if listed is None:
            return count
        cell = src[at]
        lon = lax.shift_right_logical(cell, 7)
        lat = lax.bitwise_and(cell, LANES - 1)
        low = jnp.logical_or(lat < 2, lon < 2)
        high = jnp.logical_or(lat >= LANES - 3, lon >= lon_cells - 3)
        listed[count] = at
        return count + jnp.logical_or(low, high).astype(jnp.int32)

    def body(m, carry):
        count, accs = carry
        accs = pick(field, src, m, m, 0, accs)
        count = note(m, count)
        accs = pick(field, src, LANES + m, m, 1, accs)
        count = note(LANES + m, count)
        return count, accs

    zero = jnp.zeros((2 * ROWS, LANES), jnp.float32)
    count, accs = lax.fori_loop(0, LANES, body, (jnp.int32(0), (zero, zero, zero, zero)), unroll=32)
    if listed is not None:
        for k in range(AGAIN):
            listed[count + k] = 0
        listed[listed.shape[0] - 1] = count
    near0, far0, near1, far1 = accs
    return near0, pltpu.roll(far0, LANES - 1, 1), near1, pltpu.roll(far1, LANES - 1, 1)


def finish_rows(accs, table, sent):
    sub = sub_ids()
    for slot in range(2):
        near, far = accs[2 * slot], accs[2 * slot + 1]
        base = slot * 8
        w0 = table[base : base + 1, :]
        w1 = table[base + 1 : base + 2, :]
        w2 = table[base + 2 : base + 3, :]
        w3 = table[base + 3 : base + 4, :]
        value = w0 * near[:ROWS] + w1 * far[:ROWS] + w2 * near[ROWS:] + w3 * far[ROWS:]
        low, high = value[:8], value[8:]
        cosine = table[base + 4 : base + 5, :]
        sine = table[base + 5 : base + 6, :]
        turned = cosine * high + jnp.where(sub < 4, sine, -sine) * pltpu.roll(high, 4, 0)
        sent[slot * ROWS : slot * ROWS + 8, :] = low
        sent[slot * ROWS + 8 : slot * ROWS + 16, :] = turned
    sent[32:40, :] = table[16:24, :]


def put_edges(field, flag, lon_cells, edge_a, edge_b):
    first = field[0 : 2 * ROWS, :]
    last = field[(lon_cells - 2) * ROWS : lon_cells * ROWS, :]
    odd = flag[0] > 0
    edge_a[...] = jnp.where(odd, first, last)
    edge_b[...] = jnp.where(odd, last, first)


def strip_of(value, col):
    return pltpu.roll(value, 4 * col + 2, 1)


def start_kernel(
    lon_cells, state, src, counts, names, weights, turn, flag,
    field, edge_a, edge_b, strips, buffer, sent, table, listed, zeros, sems
):
    blocks = lon_cells // 32
    zeros[...] = jnp.zeros(zeros.shape, jnp.float32)
    count = zeros.shape[0]
    clears = []
    for number in range(buffer.shape[0] // count):
        copy = pltpu.make_async_copy(zeros, buffer.at[pl.ds(number * count, count), :], sems.at[number])
        copy.start()
        clears.append(copy)
    lane = lane_ids(ROWS)
    quad = lax.shift_right_logical(lane, 2)
    for block in range(blocks):
        acc = jnp.zeros((ROWS, LANES), jnp.float32)
        for col in range(32):
            u = block * 32 + col
            low = state[pl.ds(u, 8, stride=lon_cells), :]
            high = state[pl.ds(u + 8 * lon_cells, 8, stride=lon_cells), :]
            value = jnp.concatenate([low, high], axis=0)
            field[rows_of(u), :] = value
            acc = jnp.where(quad == col, strip_of(value, col), acc)
        strips[block * ROWS : (block + 1) * ROWS, :] = acc
    put_edges(field, flag, lon_cells, edge_a, edge_b)
    row = lane_ids(1)
    table[...] = jnp.zeros(table.shape, jnp.float32)
    angle = turn[...]
    cosine, sine = jnp.cos(angle), jnp.sin(angle)
    for slot in range(2):
        for corner in range(4):
            value = weights[2 * corner + slot : 2 * corner + slot + 1, :]
            table[8 * slot + corner : 8 * slot + corner + 1, :] = jnp.where(row < counts[slot], value, 0.0)
        table[8 * slot + 4 : 8 * slot + 5, :] = cosine[slot : slot + 1]
        table[8 * slot + 5 : 8 * slot + 6, :] = sine[slot : slot + 1]
        table[16 + slot : 17 + slot, :] = jnp.full((1, LANES), names[slot], jnp.int32).astype(jnp.float32)
    finish_rows(gather_all(field, src, lon_cells, listed), table, sent)
    for copy in clears:
        copy.wait()


def key_kernel(slots, keys, listed):
    lane = lane_ids(8)
    slot = slots[...]
    peer = seat(lax.bitwise_xor(lax.shift_right_logical(jnp.maximum(slot, 0), 7), FLIP))
    shift = lax.bitwise_and(slot - lane, LANES - 1)
    key = jnp.where(slot >= 0, (peer * LANES + shift).astype(jnp.float32), NO_KEY)
    keys[...] = key

    def cond(carry):
        count, more = carry[0], carry[1]
        return jnp.logical_and(count < LANES, more > 0)

    def body(carry):
        count, _, last, found, total = carry
        now = jnp.min(jnp.where(key > last, key, NO_KEY), axis=1, keepdims=True)
        now = jnp.broadcast_to(now, (8, LANES))
        hit = now < NO_KEY
        more = (jnp.min(now) < NO_KEY).astype(jnp.int32)
        found = jnp.where(lane == count, jnp.where(hit, now, -1.0), found)
        total = total + more.astype(jnp.float32)
        return count + 1, more, now, found, total

    zero = jnp.zeros((8, LANES), jnp.float32)
    out = lax.while_loop(cond, body, (jnp.int32(0), jnp.int32(1), zero - 1.0, zero - 1.0, zero))
    listed[0:8, :] = out[3].astype(jnp.int32)
    listed[8:16, :] = out[4].astype(jnp.int32)


def fill_ghosts(received, keys, listed, ghosts):
    def body(step, accs):
        accs = list(accs)
        for row in range(4):
            for i in (2 * step, 2 * step + 1):
                key = listed[row, i]
                known = jnp.maximum(key, 0)
                peer = lax.shift_right_logical(known, 7)
                shift = lax.bitwise_and(known, LANES - 1)
                value = pltpu.roll(tile(received, peer), lax.bitwise_and(LANES - shift, LANES - 1), 1)
                accs[row] = jnp.where(keys[row : row + 1, :] == key.astype(jnp.float32), value, accs[row])
        return tuple(accs)

    zero = jnp.zeros((ROWS, LANES), jnp.float32)
    accs = lax.fori_loop(0, lax.shift_right_logical(listed[8, 0] + 1, 1), body, (zero, zero, zero, zero))
    for row in range(4):
        ghosts[row * ROWS : (row + 1) * ROWS, :] = accs[row]


def merge_strips(strip_a, strip_b, flag, ghosts, merged, blocks):
    lane = lane_ids(8)
    part = lax.bitwise_and(lane, 3)
    odd = flag[1] > 0
    north = flag[2] > 0
    first = part == jnp.where(north, 1, 2)
    second = part == jnp.where(north, 0, 3)
    for block in range(blocks):
        spread = lax.shift_right_logical(lane, 2) + 32 * block
        for half in range(2):
            at = block * ROWS + half * 8
            a = strip_a[at : at + 8, :]
            b = strip_b[at : at + 8, :]
            value = jnp.where(part < 2, jnp.where(odd, a, b), jnp.where(odd, b, a))
            wide0 = jnp.take_along_axis(ghosts[half * 8 : half * 8 + 8, :], spread, axis=1)
            wide1 = jnp.take_along_axis(ghosts[ROWS + half * 8 : ROWS + half * 8 + 8, :], spread, axis=1)
            merged[at : at + 8, :] = value + jnp.where(first, wide0, jnp.where(second, wide1, 0.0))


def coefficients(sin_t, cos_t, yang, consts):
    d_theta, d_phi, step, kappa, viscous, omega, buoyancy, radial = consts
    sub = sub_ids()
    low = sub < 4
    level = lax.bitwise_and(sub, 3).astype(jnp.float32)
    inverse = 1.0 / (level * radial + R_LOW)
    keep = 1.0 - yang
    over_sin = 1.0 / sin_t
    square = inverse * inverse
    advect_t = -step / (12.0 * d_theta) * inverse
    advect_p = -step / (12.0 * d_phi) * inverse * over_sin
    values = [advect_t, advect_p]
    for half in range(2):
        spread = jnp.where(low, step * kappa, step * viscous) if half == 0 else jnp.full((8, LANES), step * viscous)
        second_t = spread * square / (12.0 * d_theta * d_theta)
        first_t = spread * square * (cos_t * over_sin) / (12.0 * d_theta)
        second_p = spread * square * (over_sin * over_sin) / (12.0 * d_phi * d_phi)
        second_r = spread / (radial * radial)
        first_r = spread * inverse / radial
        middle = -30.0 * second_t - 30.0 * second_p - 2.0 * second_r
        values += [second_t, first_t, second_p, second_r, first_r, middle]
    twice = 2.0 * step * omega
    zero = jnp.zeros((8, LANES), jnp.float32)
    sign = jnp.where(low, 1.0, -1.0)
    values += [
        jnp.where(low, 0.0, step * buoyancy),
        jnp.where(low, zero, twice * keep * sin_t),
        jnp.where(low, zero, -twice * cos_t),
        jnp.where(low, 0.0, twice) + zero,
        sign * twice * keep * cos_t,
        sign * twice * sin_t,
        jnp.where(low, zero, -twice * keep * sin_t),
        jnp.where(low, zero, twice * cos_t),
        jnp.where(low, -twice, 0.0) + zero,
    ]
    return values


def inner_kernel(second, lon_cells, consts, *refs):
    refs = list(refs)
    field = refs.pop(0)
    origin = refs.pop(0) if second else None
    geo, result, strips, coef = refs
    base = 2 * lon_cells
    sin_t, cos_t, yang = (geo[base + 8 * i : base + 8 * i + 8, :] for i in range(3))
    for i, value in enumerate(coefficients(sin_t, cos_t, yang, consts)):
        coef[8 * i : 8 * i + 8, :] = value
    radial = consts[7]
    lane16 = lane_ids(ROWS)
    quad = lax.shift_right_logical(lane16, 2)
    sub = sub_ids()
    low = sub < 4
    level = lax.bitwise_and(sub, 3)
    top = level == 3
    bottom = level == 0
    advect_r = -consts[2] / (2.0 * radial)

    def c(i):
        return coef[8 * i : 8 * i + 8, :]

    def update(u, down2, down1, here, up1, up2):
        south1 = jnp.where(lane16 >= 1, pltpu.roll(here, 1, 1), 0.0)
        south2 = jnp.where(lane16 >= 2, pltpu.roll(here, 2, 1), 0.0)
        north1 = jnp.where(lane16 < LANES - 1, pltpu.roll(here, LANES - 1, 1), 0.0)
        north2 = jnp.where(lane16 < LANES - 2, pltpu.roll(here, LANES - 2, 1), 0.0)
        lat_odd = 8.0 * (north1 - south1) - (north2 - south2)
        lat_even = 16.0 * (north1 + south1) - (north2 + south2)
        lon_odd = 8.0 * (up1 - down1) - (up2 - down2)
        lon_even = 16.0 * (up1 + down1) - (up2 + down2)
        v0, v1 = here[:8], here[8:]
        r0, r1 = pltpu.roll(v0, 4, 0), pltpu.roll(v1, 4, 0)
        vel_r = jnp.where(low, r0, v0)
        vel_t = jnp.where(low, v1, r1)
        vel_p = jnp.where(low, r1, v1)
        along_t = vel_t * c(0)
        along_p = vel_p * c(1)
        along_r = vel_r * advect_r
        sin_p = geo[pl.ds(u, 1), :]
        cos_p = geo[pl.ds(lon_cells + u, 1), :]
        turn0 = c(14) * r0 + (c(15) + c(16) * sin_p) * vel_p + (c(17) * cos_p) * vel_t
        turn1 = (c(18) + c(19) * sin_p) * r1 + (c(20) + c(21) * sin_p + c(22) * cos_p) * vel_r
        out = []
        for half, value, turn in ((0, v0, turn0), (1, v1, turn1)):
            at = 2 + 6 * half
            part = slice(8 * half, 8 * half + 8)
            above = jnp.where(top, value, pltpu.roll(value, 7, 0))
            below = jnp.where(bottom, value, pltpu.roll(value, 1, 0))
            change = (
                (c(at + 1) + along_t) * lat_odd[part]
                + c(at) * lat_even[part]
                + along_p * lon_odd[part]
                + c(at + 2) * lon_even[part]
                + (c(at + 4) + along_r) * (above - below)
                + c(at + 3) * (above + below)
                + c(at + 5) * value
                + turn
            )
            out.append(value + change)
        new = jnp.concatenate(out, axis=0)
        if second:
            new = 0.5 * (tile(origin, u) + new)
        return new

    def at(u):
        if u < 0 or u >= lon_cells:
            return jnp.zeros((ROWS, LANES), jnp.float32)
        return tile(field, u)

    def group(index, block, col, tiles):
        acc = jnp.zeros((ROWS, LANES), jnp.float32)
        for k in range(GROUP):
            new = update(index + k, *tiles[k : k + 5])
            result[rows_of(index + k), :] = new
            acc = jnp.where(quad == col + k, strip_of(new, col + k), acc)
        rows = rows_of(block)
        mine = jnp.logical_and(quad >= col, quad < col + GROUP)
        strips[rows, :] = jnp.where(mine, acc, strips[rows, :])

    strips[...] = jnp.zeros(strips.shape, jnp.float32)
    for index in (0, lon_cells - GROUP):
        group(index, index // 32, index % 32, [at(u) for u in range(index - 2, index + GROUP + 2)])

    def body(number, carry):
        index = number * GROUP
        tiles = [tile(field, index + k) for k in range(-2, GROUP + 2)]
        group(index, lax.shift_right_logical(index, 5), lax.bitwise_and(index, 31), tiles)
        return carry

    lax.fori_loop(1, lon_cells // GROUP - 1, body, 0)


def rows_kernel(field, src, corners):
    for i, value in enumerate(gather_all(field, src)):
        corners[2 * i * ROWS : 2 * (i + 1) * ROWS, :] = value


def outer_kernel(second, final, lon_cells, consts, *refs):
    refs = list(refs)
    part, part_strips, own_a, own_b, own_strips, lon_a, lon_b, strip_a, strip_b, received, keys, listed, flag, geo = refs[:14]
    refs = refs[14:]
    if final:
        result = refs.pop(0)
    else:
        corners, again, src, table, result, sent, edge_a, edge_b, strips = refs[:9]
        refs = refs[9:]
    ghosts, merged, fixes, sides = refs
    blocks = lon_cells // 32
    fill_ghosts(received, keys, listed, ghosts)
    merge_strips(strip_a, strip_b, flag, ghosts, merged, blocks)

    base = 2 * lon_cells
    sin_t, cos_t, yang, strip_sin, strip_cos = (geo[base + 8 * i : base + 8 * i + 8, :] for i in range(5))
    low = sub_ids() < 4
    lane = lane_ids(8)
    scale = 0.5 if second else 1.0

    values = coefficients(strip_sin, strip_cos, yang, consts)
    quarter = lax.bitwise_and(lane, 3)
    for block in range(blocks):
        at = block * ROWS
        v1 = own_strips[at + 8 : at + 16, :]
        along = jnp.where(low, v1, pltpu.roll(v1, 4, 0)) * values[0]
        for half in range(2):
            rows = slice(at + 8 * half, at + 8 * half + 8)
            outside = merged[rows, :]
            left1, left2 = pltpu.roll(outside, LANES - 1, 1), pltpu.roll(outside, LANES - 2, 1)
            right1, right2 = pltpu.roll(outside, 1, 1), pltpu.roll(outside, 2, 1)
            near = jnp.where(quarter == 1, left1, jnp.where(quarter == 2, right1, 0.0))
            far = jnp.where(quarter < 2, left2, right2)
            first = jnp.where(quarter < 2, 8.0 * near - far, far - 8.0 * near)
            twice = 16.0 * near - far
            fixes[rows, :] = scale * ((values[3 + 6 * half] + along) * first + values[2 + 6 * half] * twice)

    values = coefficients(sin_t, cos_t, yang, consts)
    odd = flag[0] > 0
    west = flag[3] > 0
    for i, row in enumerate((3, 2, 2, 3)):
        came = jnp.where(odd, lon_a[...], lon_b[...]) if i < 2 else jnp.where(odd, lon_b[...], lon_a[...])
        ghost = jnp.where(west if i < 2 else jnp.logical_not(west), ghosts[rows_of(row), :], 0.0)
        sides[rows_of(i), :] = came[rows_of(i % 2)] + ghost
    before2, before1, after1, after2 = (sides[rows_of(i), :] for i in range(4))
    for i, (near, far, sign) in enumerate(
        ((before1, before2, -1.0), (None, before1, -1.0), (None, after1, 1.0), (after1, after2, 1.0))
    ):
        own = jnp.where(odd, own_a[...], own_b[...]) if i < 2 else jnp.where(odd, own_b[...], own_a[...])
        v1 = own[rows_of(i % 2)][8:]
        along = jnp.where(low, pltpu.roll(v1, 4, 0), v1) * values[1]
        first = -far if near is None else 8.0 * near - far
        twice = -far if near is None else 16.0 * near - far
        for half in range(2):
            rows = slice(8 * half, 8 * half + 8)
            change = sign * along * first[rows] + values[4 + 6 * half] * twice[rows]
            sides[i * ROWS + 8 * half : i * ROWS + 8 * half + 8, :] = scale * change

    lane16 = lane_ids(ROWS)
    rim = jnp.logical_or(lane16 < 2, lane16 >= LANES - 2)

    def corrected(u, block, col):
        moved = pltpu.roll(tile(fixes, block), lax.bitwise_and(LANES - 2 - 4 * col, LANES - 1), 1)
        return tile(part, u) + jnp.where(rim, moved, 0.0)

    def store(u, new):
        if final:
            result[pl.ds(u, 8, stride=lon_cells), :] = new[:8]
            result[pl.ds(u + 8 * lon_cells, 8, stride=lon_cells), :] = new[8:]
        else:
            result[rows_of(u), :] = new

    def body(block, carry):
        for col in range(32):
            u = block * 32 + col
            store(u, corrected(u, block, col))
        return carry

    lax.fori_loop(0, blocks, body, 0)
    if not final:
        strips[...] = part_strips[...] + fixes[...]
    quad = lax.shift_right_logical(lane16, 2)
    for i, u in enumerate((0, 1, lon_cells - 2, lon_cells - 1)):
        block, col = divmod(u, 32)
        change = sides[rows_of(i), :]
        store(u, corrected(u, block, col) + change)
        if not final:
            strips[rows_of(block), :] += jnp.where(quad == col, strip_of(change, col), 0.0)
    if final:
        return
    put_edges(result, flag, lon_cells, edge_a, edge_b)

    def repeat(step, accs):
        for k in range(AGAIN):
            at = again[AGAIN * step + k]
            accs = pick(result, src, at, lax.bitwise_and(at, LANES - 1), lax.shift_right_logical(at, 7), accs)
        return accs

    accs = tuple(corners[2 * i * ROWS : 2 * (i + 1) * ROWS, :] for i in range(4))
    steps = (again[again.shape[0] - 1] + AGAIN - 1) // AGAIN
    finish_rows(lax.fori_loop(0, steps, repeat, accs), table, sent)


def seat(block):
    return lax.bitwise_and(block, 1) * 32 + lax.bitwise_and(lax.shift_right_logical(block, 1), 7) * 4 + lax.shift_right_logical(block, 4)


def pack_kernel(message, _, buffer, staged, sems):
    target0 = jnp.max(message[32:33, :]).astype(jnp.int32)
    target1 = jnp.max(message[33:34, :]).astype(jnp.int32)
    same = target0 == target1
    slot0, slot1 = message[0:ROWS, :], message[ROWS : 2 * ROWS, :]
    staged[0:ROWS, :] = jnp.where(same, slot0 + slot1, slot0)
    staged[ROWS : 2 * ROWS, :] = slot1
    copies = [
        pltpu.make_async_copy(
            staged.at[pl.ds(at * ROWS, ROWS), :],
            buffer.at[pl.ds(pl.multiple_of(seat(target) * ROWS, ROWS), ROWS), :],
            sems.at[at],
        )
        for at, target in enumerate((target0, target1))
    ]
    copies[0].start()
    pl.when(jnp.logical_not(same))(copies[1].start)
    copies[0].wait()
    pl.when(jnp.logical_not(same))(copies[1].wait)


def crossing(count):
    return [(here, (here ^ FLIP) + count) for here in range(count)] + [(here + count, here ^ FLIP) for here in range(count)]


def pairs(count, first):
    route = []
    for low in range(first, count - 1, 2):
        route += [(low, low + 1), (low + 1, low)]
    return route


def on_device(state, partners, send_counts, source_cells, weights, turn_angles, ghost_slots):
    lat_blocks = lax.axis_size("colat")
    lon_axes = ("lon_hi", "core")
    lon_blocks = lax.axis_size(lon_axes)
    peers = lat_blocks * lon_blocks
    lon_cells, lat_cells = state.shape[3], state.shape[4]
    consts = constants(lat_cells * lat_blocks, lon_cells * lon_blocks)
    core = lax.axis_index("core")
    colat = lax.axis_index("colat")
    lon = lax.axis_index(lon_axes)
    yang = lax.axis_index("panel").astype(jnp.float32)
    flag = jnp.stack([lon % 2, colat % 2, colat == 0, lon == 0]).astype(jnp.int32)

    src = source_cells[0, 0, 0]
    theta = ((colat * lat_cells + jnp.arange(lat_cells, dtype=jnp.int32)).astype(jnp.float32) + 0.5) * consts[0] + 0.25 * math.pi
    rim_lat = (jnp.arange(LANES, dtype=jnp.int32) + 2) % 4 + jnp.where(jnp.arange(LANES, dtype=jnp.int32) % 4 < 2, lat_cells - 4, 0)
    rim_theta = ((colat * lat_cells + rim_lat).astype(jnp.float32) + 0.5) * consts[0] + 0.25 * math.pi
    phi = ((lon * lon_cells + jnp.arange(lon_cells, dtype=jnp.int32)).astype(jnp.float32) + 0.5) * consts[1] - 0.75 * math.pi
    geo = jnp.concatenate(
        [
            jnp.broadcast_to((yang * jnp.sin(phi))[:, None], (lon_cells, LANES)),
            jnp.broadcast_to((yang * jnp.cos(phi))[:, None], (lon_cells, LANES)),
            jnp.broadcast_to(jnp.sin(theta)[None], (8, LANES)),
            jnp.broadcast_to(jnp.cos(theta)[None], (8, LANES)),
            jnp.broadcast_to(yang, (8, LANES)),
            jnp.broadcast_to(jnp.sin(rim_theta)[None], (8, LANES)),
            jnp.broadcast_to(jnp.cos(rim_theta)[None], (8, LANES)),
        ]
    )
    slot = ghost_slots[0, 0, 0]
    pole = slot[: 4 * lon_cells].reshape(2, 2, lon_cells)
    pole = jnp.pad(jnp.maximum(pole[0], pole[1]), ((0, 0), (0, LANES - lon_cells)), constant_values=-1)
    side = slot[4 * lon_cells :].reshape(2, 2, LANES)
    slots = jnp.concatenate([pole, jnp.maximum(side[0], side[1]), jnp.full((4, LANES), -1, jnp.int32)])

    vmem = pl.BlockSpec(memory_space=pltpu.VMEM)
    smem = pl.BlockSpec(memory_space=pltpu.SMEM)

    def f32(*shape):
        return jax.ShapeDtypeStruct(shape, jnp.float32)

    cells = lon_cells * ROWS
    strip_rows = lon_cells // 32 * ROWS
    moving = [f32(cells, LANES), f32(40, LANES), f32(32, LANES), f32(32, LANES), f32(strip_rows, LANES)]
    params = pltpu.CompilerParams(vmem_limit_bytes=16 * 1024 * 1024)

    keys, listed = pl.pallas_call(
        key_kernel,
        out_shape=[f32(8, LANES), jax.ShapeDtypeStruct((16, LANES), jnp.int32)],
        in_specs=[vmem],
        out_specs=[vmem, vmem],
        compiler_params=params,
    )(slots)

    hbm = pl.BlockSpec(memory_space=pltpu.HBM)
    field, edge_a, edge_b, strips, buffer, sent, table, again = pl.pallas_call(
        functools.partial(start_kernel, lon_cells),
        out_shape=[moving[0], moving[2], moving[3], moving[4], f32(peers * ROWS, LANES), moving[1], f32(24, LANES)]
        + [jax.ShapeDtypeStruct((2 * LANES + 16,), jnp.int32)],
        in_specs=[vmem, smem, smem, smem, vmem, vmem, smem],
        out_specs=[vmem] * 4 + [hbm] + [vmem] * 2 + [smem],
        scratch_shapes=[
            pltpu.VMEM((LANES, LANES), jnp.float32),
            pltpu.SemaphoreType.DMA((peers * ROWS // LANES,)),
        ],
        compiler_params=params,
    )(
        state.reshape(cells, LANES),
        src,
        send_counts[0, 0, 0],
        partners[0, 0, 0],
        weights.reshape(8, LANES),
        turn_angles.reshape(2, LANES),
        flag,
    )

    origin = field
    for number in range(2 * STEPS):
        second = number % 2 == 1
        final = number == 2 * STEPS - 1
        over = lax.ppermute(sent, ("panel",) + lon_axes, crossing(lon_blocks))
        operands = [field] + ([origin] if second else []) + [geo]
        part, part_strips = pl.pallas_call(
            functools.partial(inner_kernel, second, lon_cells, consts),
            out_shape=[moving[0], moving[4]],
            in_specs=[vmem] * len(operands),
            out_specs=[vmem, vmem],
            scratch_shapes=[pltpu.VMEM((8 * 23, LANES), jnp.float32)],
            compiler_params=params,
            cost_estimate=pl.CostEstimate(flops=20_000_000, bytes_accessed=1 << 23, transcendentals=0),
        )(*operands)
        over, part, part_strips = lax.optimization_barrier((over, part, part_strips))
        buffer = pl.pallas_call(
            pack_kernel,
            out_shape=f32(peers * ROWS, LANES),
            in_specs=[vmem, hbm],
            out_specs=hbm,
            scratch_shapes=[pltpu.VMEM((2 * ROWS, LANES), jnp.float32), pltpu.SemaphoreType.DMA((2,))],
            input_output_aliases={1: 0},
            compiler_params=params,
        )(over, buffer)
        buffer, own_a, own_b, own_strips, part = lax.optimization_barrier((buffer, edge_a, edge_b, strips, part))
        received = lax.all_to_all(
            buffer.reshape(peers, ROWS, LANES), ("core", "lon_hi", "colat"), split_axis=0, concat_axis=0, tiled=True
        ).reshape(peers * ROWS, LANES)
        if not final:
            corners = pl.pallas_call(
                rows_kernel,
                out_shape=f32(8 * ROWS, LANES),
                in_specs=[vmem, smem],
                out_specs=vmem,
                compiler_params=params,
                cost_estimate=pl.CostEstimate(flops=8_000_000, bytes_accessed=1 << 22, transcendentals=0),
            )(part, src)
        lon_a = lax.ppermute(own_a, lon_axes, pairs(lon_blocks, 0))
        lon_b = lax.ppermute(own_b, lon_axes, pairs(lon_blocks, 1))
        strip_a = lax.ppermute(own_strips, "colat", pairs(lat_blocks, 0))
        strip_b = lax.ppermute(own_strips, "colat", pairs(lat_blocks, 1))
        operands = [part, part_strips, own_a, own_b, own_strips, lon_a, lon_b, strip_a, strip_b, received, keys, listed, flag, geo]
        specs = [vmem] * 11 + [smem, smem, vmem]
        if not final:
            operands += [corners, again, src, table]
            specs += [vmem, smem, smem, vmem]
        out = pl.pallas_call(
            functools.partial(outer_kernel, second, final, lon_cells, consts),
            out_shape=moving[:1] if final else moving,
            in_specs=specs,
            out_specs=[vmem] * (1 if final else 5),
            scratch_shapes=[
                pltpu.VMEM((4 * ROWS, LANES), jnp.float32),
                pltpu.VMEM((strip_rows, LANES), jnp.float32),
                pltpu.VMEM((strip_rows, LANES), jnp.float32),
                pltpu.VMEM((4 * ROWS, LANES), jnp.float32),
            ],
            compiler_params=params,
        )(*operands)
        if final:
            return out[0].reshape(state.shape)
        field, sent, edge_a, edge_b, strips = out
        if second:
            origin = field


def solution(mesh):
    lon = mesh.shape["lon"]
    fine = Mesh(
        mesh.devices.reshape(mesh.shape["panel"], mesh.shape["colat"], lon // 2, 2), ("panel", "colat", "lon_hi", "core")
    )
    lon_axes = ("lon_hi", "core")
    table = P("panel", "colat", lon_axes, None)
    in_specs = (
        P(None, "panel", None, lon_axes, "colat"),
        table,
        table,
        table,
        P(None, "panel", "colat", lon_axes, None),
        table,
        table,
    )
    out_specs = P(None, "panel", None, lon_axes, "colat")
    return jax.shard_map(on_device, mesh=fine, in_specs=in_specs, out_specs=out_specs, check_vma=False)
```
